256 devices in a mesh: lon: 16 (over y, x_hi, core), lat: 16 (over z, x_lo).
Axes of the slice: x: 4 (x_hi: 2, x_lo: 2; x = x_hi * 2 + x_lo), y: 4, z: 8, core: 2. Of those that a mesh axis runs over, the one named last changes fastest.
Arguments:
- fields: float32 [3, 1, 2048, 12288], P(None, None, 'lat', 'lon'), may hold values from -5 to 7
- zonal_fraction: float32 [1, 2048, 12288], P(None, 'lat', 'lon'), may hold values from 0 to 1
- merid_courant: float32 [1, 2048, 12288], P(None, 'lat', 'lon'), may hold values from -0.4 to 0.4
- hop_counts: int32 [2048], P('lat'), may hold values from 0 to 4, as said below
- filter_rows: int32 [512], replicated, may hold values from 0 to 2047, as said below
Outputs:
- new_fields: float32 [3, 1, 2048, 12288], P(None, None, 'lat', 'lon')
The draws below stay inside these ranges and needn't reach their ends.
Inputs may be any that keep to these rules, and one draw needn't show every extreme that they name: `hop_counts`: the largest, 4, is taken in every draw. `filter_rows`: ascending and distinct; every listed row lies among the first or the last 512 rows, and each aligned block of 128 rows there holds exactly 64 listed rows.
All inputs are finite; a program needn't handle non-finite values.
Results may differ from the reference program's by a relative error of at most 0.0003.
Values sent between devices are 32-bit elements; how exact they have to be, the bound alone decides.
No kernel may reach another device: no remote copies, remote signals or barrier semaphores. Data moves between devices by JAX's collectives and lax.ppermute only.
A program may use at most 128 MiB of HBM per device.

```python
import math
import jax
import jax.numpy as jnp
from jax import lax

NLON = 12288
ROWS_DEV = 128
LEVELS = 1
COMP = 3
MAX_HOP = 4
NLAT = 2048
SECTOR = 768
FR_BAND = 64
NFR = 512


def draw_fields(key, part):
    base = jax.random.truncated_normal(key, -5.0, 5.0, (COMP, LEVELS, NLAT, NLON), jnp.float32)
    return base


def draw_hop_counts(key, part):
    row_index = jnp.arange(NLAT, dtype=jnp.int32)
    distance = jnp.abs(2 * row_index - (NLAT - 1))
    highest = 1 + MAX_HOP * distance // NLAT
    drawn = jax.random.randint(key, (NLAT,), 0, highest + 1)
    drawn = jnp.where((row_index == 0) | (row_index == NLAT - 1), MAX_HOP, drawn)
    drawn = jnp.where(row_index == NLAT // 2, 0, drawn)
    return drawn.astype(jnp.int32)


def draw_filter_rows(key, part):
    bands = NFR // FR_BAND
    per_side = bands // 2
    all_bands = NLAT // ROWS_DEV
    scores = jax.random.randint(key, (bands, ROWS_DEV), 0, 1 << 20) * ROWS_DEV + jnp.arange(ROWS_DEV, dtype=jnp.int32)[None, :]
    unused, picked = lax.top_k(scores, FR_BAND)
    picked = jnp.sort(picked, axis=1)
    position = jnp.arange(bands, dtype=jnp.int32)
    band_number = jnp.where(position < per_side, position, position + (all_bands - bands))
    return (band_number[:, None] * ROWS_DEV + picked).reshape(NFR).astype(jnp.int32)


def block_scale(key, dims, split, low, largest):
    def one(axis_at, shards_of):
        draws = jax.random.uniform(jax.random.fold_in(jax.random.fold_in(key, 6), axis_at), (shards_of,), jnp.float32, low / len(split), largest / len(split))
        return jnp.repeat(jnp.exp(draws), dims[axis_at] // shards_of).reshape((-1,) + (1,) * (len(dims) - axis_at - 1))

    factor_of = one(*split[0])
    for cut in split[1:]:
        factor_of = factor_of * one(*cut)
    return factor_of


def setup_inputs(seed: int = 0) -> dict:
    streams_of = jax.random.split(jax.random.key(seed), 6)
    fields = draw_fields(jax.random.fold_in(streams_of[5], 71), 0)
    zonal_fraction = jnp.clip(1.0 * jax.random.uniform(streams_of[1], (LEVELS, NLAT, NLON), jnp.float32) ** block_scale(streams_of[1], (LEVELS, NLAT, NLON), ((1, 16), (2, 16)), -0.2, 0.2), 0.0, 1.0)
    merid_courant = jnp.clip(jax.random.uniform(streams_of[2], (LEVELS, NLAT, NLON), jnp.float32, -0.4, 0.4) * block_scale(streams_of[2], (LEVELS, NLAT, NLON), ((1, 16), (2, 16)), -0.4, 0.0), -0.4, 0.4)
    hop_counts = draw_hop_counts(jax.random.fold_in(streams_of[5], 71), 0)
    filter_rows = draw_filter_rows(jax.random.fold_in(streams_of[5], 71), 0)
    return {"fields": fields, "zonal_fraction": zonal_fraction, "merid_courant": merid_courant, "hop_counts": hop_counts, "filter_rows": filter_rows}


cos_cutoff = 0.7071067811865476


def cubic_weights(fraction):
    offset = 1.0 - fraction
    w_far = -offset * (offset - 1.0) * (offset - 2.0) / 6.0
    w_near = (offset + 1.0) * (offset - 1.0) * (offset - 2.0) / 2.0
    w_next = -(offset + 1.0) * offset * (offset - 2.0) / 2.0
    w_last = (offset + 1.0) * offset * (offset - 1.0) / 6.0
    return w_far, w_near, w_next, w_last


def zonal_row(inputs):
    row_fields, hop_count, fraction = inputs
    doubled = jnp.concatenate([row_fields, row_fields], axis=-1)
    start = ((NLON - hop_count * SECTOR) % NLON).astype(jnp.int32)
    moved = lax.dynamic_slice_in_dim(doubled, start, NLON, axis=2)
    w_far, w_near, w_next, w_last = cubic_weights(fraction[None])
    return (w_far * jnp.roll(moved, 2, axis=-1) + w_near * jnp.roll(moved, 1, axis=-1)
            + w_next * moved + w_last * jnp.roll(moved, -1, axis=-1))


def reference(fields, zonal_fraction, merid_courant, hop_counts, filter_rows):
    by_rows = jnp.moveaxis(fields, 2, 0)
    fraction_rows = jnp.moveaxis(zonal_fraction, 1, 0)
    zonal = lax.map(zonal_row, (by_rows, hop_counts, fraction_rows))
    zonal = jnp.moveaxis(zonal, 0, 2)
    row_float = jnp.arange(NLAT, dtype=jnp.float32)
    step_angle = math.pi / NLAT
    cos_center = jnp.sin((row_float + 0.5) * step_angle)
    cos_north = jnp.where(row_float < NLAT - 1, jnp.sin((row_float + 1.0) * step_angle), 0.0)
    above = jnp.concatenate([zonal[:, :, 1:], jnp.zeros_like(zonal[:, :, :1])], axis=2)
    flux = cos_north[:, None] * (jnp.maximum(merid_courant, 0.0) * zonal + jnp.minimum(merid_courant, 0.0) * above)
    south = jnp.concatenate([jnp.zeros_like(flux[:, :, :1]), flux[:, :, :-1]], axis=2)
    merid = zonal - (flux - south) / cos_center[:, None]
    picked = merid[:, :, filter_rows, :]
    spectrum = jnp.fft.rfft(picked, axis=-1)
    wave = jnp.arange(NLON // 2 + 1, dtype=jnp.float32)
    sine = jnp.sin(wave * (math.pi / NLON))
    ratio = cos_center[filter_rows] / cos_cutoff
    ratio_sq = (ratio * ratio)[:, None]
    damping = ratio_sq / jnp.maximum(ratio_sq, (sine * sine)[None, :])
    filtered = jnp.fft.irfft(spectrum * damping, n=NLON, axis=-1).astype(jnp.float32)
    return merid.at[:, :, filter_rows, :].set(filtered)
```

```python
import functools
import math

import jax
import jax.numpy as jnp
import ml_dtypes
import numpy as np
from jax import lax
from jax.experimental import pallas as pl
from jax.experimental.pallas import tpu as pltpu
from jax.sharding import PartitionSpec as P

NLON = 12288
NLAT = 2048
SECTORS = 16
BAND = 128
ROWS = 8
TILES = 6
LANES = 128
OUTER = SECTORS * TILES
COMP = 3
ARRAYS = COMP + 2
HALF = OUTER // 2 + 1
HALF_PAD = 56
VMEM_LIMIT = 48 * 1024 * 1024

cos_cutoff = 0.7071067811865476


def split_bf16(table):
    high = table.astype(np.float32).astype(ml_dtypes.bfloat16)
    low = (table - high.astype(np.float64)).astype(np.float32).astype(ml_dtypes.bfloat16)
    return high, low


def filter_tables():
    place = np.arange(OUTER)
    a = TILES * (place % SECTORS) + place // SECTORS
    c = np.arange(HALF_PAD)
    valid = (c < HALF)[:, None]
    angle = 2.0 * np.pi * ((c[:, None] * a[None, :]) % OUTER) / OUTER
    first = np.concatenate([np.where(valid, np.cos(angle), 0.0), np.where(valid, -np.sin(angle), 0.0)], axis=0)
    weight = np.where((c == 0) | (c == OUTER // 2), 1.0, 2.0) / NLON
    inner_only = (c > 0) & (c < OUTER // 2)
    last = np.concatenate(
        [
            np.where(valid, np.cos(angle) * weight[:, None], 0.0),
            np.where(valid & inner_only[:, None], -np.sin(angle) * weight[:, None], 0.0),
        ],
        axis=0,
    ).T
    b = np.arange(LANES)
    twist = 2.0 * np.pi * (c[:, None] * b[None, :]) / NLON
    inner = 2.0 * np.pi * ((b[:, None] * b[None, :]) % LANES) / LANES
    cos_in, sin_in = np.cos(inner), np.sin(inner)
    forward = np.block([[cos_in, -sin_in], [sin_in, cos_in]])
    backward = np.block([[cos_in, sin_in], [-sin_in, cos_in]])
    sine = np.sin(np.pi * (c[:, None] + OUTER * b[None, :]) / NLON)
    first_h, first_l = split_bf16(first)
    last_h, last_l = split_bf16(last)
    forward_h, forward_l = split_bf16(forward)
    backward_h, backward_l = split_bf16(backward)
    return (
        np.concatenate([first_h, first_h, first_l], axis=1),
        np.concatenate([forward_h, forward_h, forward_l], axis=0),
        np.concatenate([backward_h, backward_h, backward_l], axis=0),
        np.concatenate([last_h, last_h, last_l], axis=1),
        np.cos(twist).astype(np.float32),
        np.sin(twist).astype(np.float32),
        (sine * sine).astype(np.float32),
    )


def latitude_tables():
    row = np.arange(NLAT, dtype=np.float32)
    step = np.float32(math.pi / NLAT)
    center = np.sin(((row + np.float32(0.5)) * step).astype(np.float64)).astype(np.float32)
    north = np.sin(((row + np.float32(1.0)) * step).astype(np.float64)).astype(np.float32)
    north[-1] = 0.0
    return center, north


def halves(value):
    high = value.astype(jnp.bfloat16)
    low = (value - high.astype(jnp.float32)).astype(jnp.bfloat16)
    return high, low


def first_row():
    return lax.axis_index("lat") * BAND + lax.axis_index("lon") * ROWS


def zonal_kernel(hop_ref, in_ref, zonal_ref, courant_ref, up_ref, down_ref):
    hop_at = lax.axis_index("lon") * ROWS
    lane = lax.broadcasted_iota(jnp.int32, (SECTORS, LANES), 1)

    def fetch(array, t, r):
        return in_ref[pl.ds((array * TILES + t) * ROWS + r, SECTORS, stride=ARRAYS * TILES * ROWS), :]

    for r in range(ROWS):
        hop = hop_ref[hop_at + r]
        weights = []
        for t in range(TILES):
            offset = 1.0 - fetch(COMP, t, r)
            w_far = -offset * (offset - 1.0) * (offset - 2.0) * (1.0 / 6.0)
            w_near = (offset + 1.0) * (offset - 1.0) * (offset - 2.0) * 0.5
            w_next = -(offset + 1.0) * offset * (offset - 2.0) * 0.5
            w_last = (offset + 1.0) * offset * (offset - 1.0) * (1.0 / 6.0)
            weights.append((w_far, w_near, w_next, w_last))
            courant = fetch(COMP + 1, t, r)
            courant_ref[r, t * SECTORS : (t + 1) * SECTORS, :] = courant
            if r == ROWS - 1:
                up_ref[COMP, t * SECTORS : (t + 1) * SECTORS, :] = courant
        for c in range(COMP):
            here = [pltpu.roll(fetch(c, t, r), hop, 0) for t in range(TILES)]
            back_one = [pltpu.roll(v, 1, 1) for v in here]
            back_two = [pltpu.roll(v, 2, 1) for v in here]
            ahead = [pltpu.roll(v, LANES - 1, 1) for v in here]
            for t in range(TILES):
                if t > 0:
                    one_before, two_before = back_one[t - 1], back_two[t - 1]
                else:
                    one_before = pltpu.roll(back_one[TILES - 1], 1, 0)
                    two_before = pltpu.roll(back_two[TILES - 1], 1, 0)
                if t < TILES - 1:
                    after = ahead[t + 1]
                else:
                    after = pltpu.roll(ahead[0], SECTORS - 1, 0)
                w_far, w_near, w_next, w_last = weights[t]
                value = (
                    w_far * jnp.where(lane < 2, two_before, back_two[t])
                    + w_near * jnp.where(lane < 1, one_before, back_one[t])
                    + w_next * here[t]
                    + w_last * jnp.where(lane == LANES - 1, after, ahead[t])
                )
                at = slice(t * SECTORS, (t + 1) * SECTORS)
                zonal_ref[c, r, at, :] = value
                if r == 0:
                    down_ref[c, at, :] = value
                if r == ROWS - 1:
                    up_ref[c, at, :] = value


def filter_group(slabs, damping, tables):
    first, forward, backward, last, twist_cos, twist_sin = tables
    count = len(slabs)
    high, low = halves(jnp.concatenate(slabs, axis=1))
    spectrum = jnp.dot(first, jnp.concatenate([high, low, high], axis=0), preferred_element_type=jnp.float32)
    parts = []
    for k in range(count):
        real = spectrum[:HALF_PAD, k * LANES : (k + 1) * LANES]
        imag = spectrum[HALF_PAD:, k * LANES : (k + 1) * LANES]
        parts.append(
            jnp.concatenate([real * twist_cos + imag * twist_sin, imag * twist_cos - real * twist_sin], axis=1)
        )
    high, low = halves(jnp.concatenate(parts, axis=0))
    spectrum = jnp.dot(jnp.concatenate([high, low, high], axis=1), forward, preferred_element_type=jnp.float32)
    parts = []
    for k in range(count):
        rows = spectrum[k * HALF_PAD : (k + 1) * HALF_PAD]
        parts.append(rows * jnp.concatenate([damping[k], damping[k]], axis=1))
    high, low = halves(jnp.concatenate(parts, axis=0))
    spectrum = jnp.dot(jnp.concatenate([high, low, high], axis=1), backward, preferred_element_type=jnp.float32)
    parts = []
    for k in range(count):
        real = spectrum[k * HALF_PAD : (k + 1) * HALF_PAD, :LANES]
        imag = spectrum[k * HALF_PAD : (k + 1) * HALF_PAD, LANES:]
        parts.append(
            jnp.concatenate([real * twist_cos - imag * twist_sin, imag * twist_cos + real * twist_sin], axis=0)
        )
    high, low = halves(jnp.concatenate(parts, axis=1))
    rebuilt = jnp.dot(last, jnp.concatenate([high, low, high], axis=0), preferred_element_type=jnp.float32)
    return [rebuilt[:, k * LANES : (k + 1) * LANES] for k in range(count)]


def filter_rows_into(out_ref, rows, merid_of, listed_ref, center_ref, sine_sq, tables):
    start = first_row()
    for at in range(0, len(rows), 2):
        group = rows[at : at + 2]
        slabs, damping, flags = [], [], []
        for r in group:
            center = center_ref[start + r]
            ratio = center * (1.0 / cos_cutoff)
            ratio_sq = jnp.full((HALF_PAD, LANES), ratio * ratio, jnp.float32)
            damp = ratio_sq / jnp.maximum(ratio_sq, sine_sq)
            listed = jnp.max(jnp.where(listed_ref[...] == start + r, 1, 0)) > 0
            for c in range(COMP):
                slabs.append(merid_of(r, c))
                damping.append(damp)
                flags.append((r, c, listed))
        filtered = filter_group(slabs, damping, tables)
        for (r, c, listed), plain, value in zip(flags, slabs, filtered):
            chosen = jnp.where(listed, value, plain)
            for t in range(TILES):
                out_ref[pl.ds((c * TILES + t) * ROWS + r, SECTORS, stride=COMP * TILES * ROWS), :] = chosen[
                    t * SECTORS : (t + 1) * SECTORS
                ]


def flux_of(north, courant, own, above):
    return north * (jnp.maximum(courant, 0.0) * own + jnp.minimum(courant, 0.0) * above)


def interior_kernel(
    center_ref, north_ref, listed_ref, zonal_ref, courant_ref, first_ref, forward_ref, backward_ref, last_ref,
    twist_cos_ref, twist_sin_ref, sine_ref, out_ref,
):
    start = first_row()
    tables = (first_ref[...], forward_ref[...], backward_ref[...], last_ref[...], twist_cos_ref[...], twist_sin_ref[...])

    def merid_of(r, c):
        own = zonal_ref[c, r]
        flux = flux_of(north_ref[start + r], courant_ref[r], own, zonal_ref[c, r + 1])
        south = flux_of(north_ref[start + r - 1], courant_ref[r - 1], zonal_ref[c, r - 1], own)
        return own - (flux - south) / jnp.full((OUTER, LANES), center_ref[start + r], jnp.float32)

    filter_rows_into(out_ref, list(range(1, ROWS - 1)), merid_of, listed_ref, center_ref, sine_ref[...], tables)


def edge_kernel(
    center_ref, north_ref, listed_ref, zonal_ref, courant_ref, below_ref, above_ref, first_ref, forward_ref,
    backward_ref, last_ref, twist_cos_ref, twist_sin_ref, sine_ref, partial_ref, out_ref,
):
    start = first_row()
    tables = (first_ref[...], forward_ref[...], backward_ref[...], last_ref[...], twist_cos_ref[...], twist_sin_ref[...])
    north_before = jnp.where(start > 0, north_ref[jnp.maximum(start - 1, 0)], 0.0)

    def merid_of(r, c):
        own = zonal_ref[c, r]
        if r == 0:
            flux = flux_of(north_ref[start], courant_ref[0], own, zonal_ref[c, 1])
            south = flux_of(north_before, below_ref[COMP], below_ref[c], own)
        else:
            flux = flux_of(north_ref[start + r], courant_ref[r], own, above_ref[c])
            south = flux_of(north_ref[start + r - 1], courant_ref[r - 1], zonal_ref[c, r - 1], own)
        return own - (flux - south) / jnp.full((OUTER, LANES), center_ref[start + r], jnp.float32)

    def place(rows):
        filter_rows_into(out_ref, rows, merid_of, listed_ref, center_ref, sine_ref[...], tables)

    copied = [r for r in range(1, ROWS - 1)]
    for q in range(COMP * TILES):
        for r in copied:
            at = pl.ds(q * ROWS + r, SECTORS, stride=COMP * TILES * ROWS)
            out_ref[at, :] = partial_ref[at, :]
    place([0, ROWS - 1])


def on_device(fields, zonal_fraction, merid_courant, hop_counts, filter_rows):
    smem = pl.BlockSpec(memory_space=pltpu.SMEM)
    vmem = pl.BlockSpec(memory_space=pltpu.VMEM)
    params = pltpu.CompilerParams(vmem_limit_bytes=VMEM_LIMIT)
    stacked = jnp.concatenate([fields[:, 0], zonal_fraction, merid_courant], axis=0)
    outgoing = stacked.reshape(ARRAYS, SECTORS, ROWS, TILES, LANES).transpose(1, 0, 3, 2, 4)
    outgoing = outgoing.reshape(SECTORS, ARRAYS * TILES * ROWS, LANES)
    incoming = lax.all_to_all(outgoing, "lon", 0, 0, tiled=True)
    incoming = incoming.reshape(SECTORS * ARRAYS * TILES * ROWS, LANES)
    f32 = jnp.float32
    zonal, courant, up, down = pl.pallas_call(
        zonal_kernel,
        out_shape=(
            jax.ShapeDtypeStruct((COMP, ROWS, OUTER, LANES), f32),
            jax.ShapeDtypeStruct((ROWS, OUTER, LANES), f32),
            jax.ShapeDtypeStruct((COMP + 1, OUTER, LANES), f32),
            jax.ShapeDtypeStruct((COMP, OUTER, LANES), f32),
        ),
        in_specs=[smem, vmem],
        out_specs=(vmem, vmem, vmem, vmem),
        compiler_params=params,
    )(hop_counts, incoming)
    bands = NLAT // BAND
    total = bands * SECTORS

    def device_of(block):
        return (block % SECTORS) * bands + block // SECTORS

    upward = [(device_of(i), device_of(i + 1)) for i in range(total - 1)]
    below = lax.ppermute(up, ("lon", "lat"), upward)
    above = lax.ppermute(down, ("lon", "lat"), [(j, i) for i, j in upward])
    first, forward, backward, last, twist_cos, twist_sin, sine_sq = [jnp.asarray(v) for v in filter_tables()]
    center, north = [jnp.asarray(v) for v in latitude_tables()]
    listed = filter_rows.reshape(4, LANES)
    out_shape = jax.ShapeDtypeStruct((SECTORS * COMP * TILES * ROWS, LANES), f32)
    constants = (first, forward, backward, last, twist_cos, twist_sin, sine_sq)
    partial = pl.pallas_call(
        interior_kernel,
        out_shape=out_shape,
        in_specs=[smem, smem] + [vmem] * 10,
        out_specs=vmem,
        compiler_params=params,
        cost_estimate=pl.CostEstimate(flops=3_000_000_000, bytes_accessed=4_000_000, transcendentals=0),
    )(center, north, listed, zonal, courant, *constants)
    returning = pl.pallas_call(
        edge_kernel,
        out_shape=out_shape,
        in_specs=[smem, smem] + [vmem] * 13,
        out_specs=vmem,
        compiler_params=params,
        cost_estimate=pl.CostEstimate(flops=1_000_000_000, bytes_accessed=4_000_000, transcendentals=0),
    )(center, north, listed, zonal, courant, below, above, *constants, partial)
    arrived = lax.all_to_all(
        returning.reshape(SECTORS, COMP * TILES * ROWS, LANES), "lon", 0, 0, tiled=True
    )
    arrived = arrived.reshape(SECTORS, COMP, TILES, ROWS, LANES).transpose(1, 0, 3, 2, 4)
    return arrived.reshape(COMP, 1, BAND, TILES * LANES)


def solution(mesh):
    in_specs = (
        P(None, None, "lat", "lon"),
        P(None, "lat", "lon"),
        P(None, "lat", "lon"),
        P("lat"),
        P(),
    )
    out_specs = P(None, None, "lat", "lon")
    return jax.shard_map(
        on_device, mesh=mesh, in_specs=in_specs, out_specs=out_specs, check_vma=False
    )
```

```python
import functools
import math

import jax
import jax.numpy as jnp
import ml_dtypes
import numpy as np
from jax import lax
from jax.experimental import pallas as pl
from jax.experimental.pallas import tpu as pltpu
from jax.sharding import PartitionSpec as P

NLON = 12288
NLAT = 2048
SECTORS = 16
BAND = 128
ROWS = 8
TILES = 6
LANES = 128
OUTER = SECTORS * TILES
COMP = 3
ARRAYS = COMP + 2
HALF = OUTER // 2 + 1
HALF_PAD = 56
ORDER = tuple(4 * y + 2 * x + core for x in (0, 1) for y in ((0, 1, 2, 3), (3, 2, 1, 0))[x] for core in (0, 1))
KEPT = (0, 1, 6, 7)
INNER = (1, 2, 3, 4, 5, 6)
GROUP = 2
VMEM_LIMIT = 48 * 1024 * 1024

cos_cutoff = 0.7071067811865476


def split_bf16(table):
    high = table.astype(np.float32).astype(ml_dtypes.bfloat16)
    low = (table - high.astype(np.float64)).astype(np.float32).astype(ml_dtypes.bfloat16)
    return high, low


def filter_tables():
    at = np.arange(OUTER)
    a = TILES * np.asarray(ORDER)[at % SECTORS] + at // SECTORS
    c = np.arange(HALF_PAD)
    valid = (c < HALF)[:, None]
    angle = 2.0 * np.pi * ((c[:, None] * a[None, :]) % OUTER) / OUTER
    first = np.concatenate([np.where(valid, np.cos(angle), 0.0), np.where(valid, -np.sin(angle), 0.0)], axis=0)
    weight = np.where((c == 0) | (c == OUTER // 2), 1.0, 2.0) / NLON
    inner_only = (c > 0) & (c < OUTER // 2)
    last = np.concatenate(
        [
            np.where(valid, np.cos(angle) * weight[:, None], 0.0),
            np.where(valid & inner_only[:, None], -np.sin(angle) * weight[:, None], 0.0),
        ],
        axis=0,
    ).T
    b = np.arange(LANES)
    twist = 2.0 * np.pi * (c[:, None] * b[None, :]) / NLON
    inner = 2.0 * np.pi * ((b[:, None] * b[None, :]) % LANES) / LANES
    cos_in, sin_in = np.cos(inner), np.sin(inner)
    forward = np.block([[cos_in, -sin_in], [sin_in, cos_in]])
    backward = np.block([[cos_in, sin_in], [-sin_in, cos_in]])
    sine = np.sin(np.pi * (c[:, None] + OUTER * b[None, :]) / NLON)
    first_h, first_l = split_bf16(first)
    last_h, last_l = split_bf16(last)
    forward_h, forward_l = split_bf16(forward)
    backward_h, backward_l = split_bf16(backward)
    return (
        np.concatenate([first_h, first_h, first_l], axis=1),
        np.concatenate([forward_h, forward_h, forward_l], axis=0),
        np.concatenate([backward_h, backward_h, backward_l], axis=0),
        np.concatenate([last_h, last_h, last_l], axis=1),
        np.cos(twist).astype(np.float32),
        np.sin(twist).astype(np.float32),
        (sine * sine).astype(np.float32),
    )


def latitude_tables():
    row = np.arange(NLAT, dtype=np.float32)
    step = np.float32(math.pi / NLAT)
    center = np.sin(((row + np.float32(0.5)) * step).astype(np.float64)).astype(np.float32)
    north = np.sin(((row + np.float32(1.0)) * step).astype(np.float64)).astype(np.float32)
    north[-1] = 0.0
    return center, north


def halves(value):
    high = value.astype(jnp.bfloat16)
    low = (value - high.astype(jnp.float32)).astype(jnp.bfloat16)
    return high, low


def place_of(sector):
    along, core = lax.shift_right_logical(sector, 2) * 2, lax.bitwise_and(sector, 1)
    return jnp.where(lax.bitwise_and(sector, 2) == 0, along + core, 14 - along + core)


def sector_at(place):
    along, core = lax.shift_right_logical(lax.bitwise_and(place, 7), 1) * 4, lax.bitwise_and(place, 1)
    return jnp.where(place < 8, along + core, 14 - along + core)


def first_row():
    return lax.axis_index("lat") * BAND + place_of(lax.axis_index("lon")) * ROWS


def from_sector(tile, source):
    low, high = tile[:8], tile[8:]
    parts = []
    for at in (slice(0, 8), slice(8, 16)):
        index = lax.bitwise_and(source[at], 7)
        parts.append(
            jnp.where(
                source[at] < 8,
                jnp.take_along_axis(low, index, axis=0, mode="promise_in_bounds"),
                jnp.take_along_axis(high, index, axis=0, mode="promise_in_bounds"),
            )
        )
    return jnp.concatenate(parts, axis=0)


def fetch(in_ref, array, t, r):
    return in_ref[pl.ds((array * TILES + t) * ROWS + r, SECTORS, stride=ARRAYS * TILES * ROWS), :]


def zonal_row(in_ref, hop, r, store):
    lane = lax.broadcasted_iota(jnp.int32, (SECTORS, LANES), 1)
    own_sector = sector_at(lax.broadcasted_iota(jnp.int32, (SECTORS, LANES), 0))

    def source(hops):
        return place_of(lax.bitwise_and(own_sector - hops + SECTORS, SECTORS - 1))

    sources, sources_before, sources_after = source(hop), source(hop + 1), source(hop - 1)
    weights = []
    for t in range(TILES):
        offset = 1.0 - fetch(in_ref, COMP, t, r)
        w_far = -offset * (offset - 1.0) * (offset - 2.0) * (1.0 / 6.0)
        w_near = (offset + 1.0) * (offset - 1.0) * (offset - 2.0) * 0.5
        w_next = -(offset + 1.0) * offset * (offset - 2.0) * 0.5
        w_last = (offset + 1.0) * offset * (offset - 1.0) * (1.0 / 6.0)
        weights.append((w_far, w_near, w_next, w_last))
    for c in range(COMP):
        raw = [fetch(in_ref, c, t, r) for t in range(TILES)]
        here = [from_sector(v, sources) for v in raw]
        before = from_sector(raw[TILES - 1], sources_before)
        after = from_sector(raw[0], sources_after)
        back_one = [pltpu.roll(v, 1, 1) for v in [before] + here]
        back_two = [pltpu.roll(v, 2, 1) for v in [before] + here]
        ahead = [pltpu.roll(v, LANES - 1, 1) for v in here + [after]]
        for t in range(TILES):
            w_far, w_near, w_next, w_last = weights[t]
            store(
                c,
                slice(t * SECTORS, (t + 1) * SECTORS),
                w_far * jnp.where(lane < 2, back_two[t], back_two[t + 1])
                + w_near * jnp.where(lane < 1, back_one[t], back_one[t + 1])
                + w_next * here[t]
                + w_last * jnp.where(lane == LANES - 1, ahead[t + 1], ahead[t]),
            )


def rim_kernel(hop_ref, in_ref, rim_ref):
    hop_at = place_of(lax.axis_index("lon")) * ROWS
    odd = lax.rem(lax.axis_index("lon"), 2)
    for r, target in ((0, 1 - odd), (ROWS - 1, odd)):

        def store(c, at, value):
            rim_ref[target, c, at, :] = value

        zonal_row(in_ref, hop_ref[hop_at + r], r, store)
        for t in range(TILES):
            rim_ref[target, COMP, t * SECTORS : (t + 1) * SECTORS, :] = fetch(in_ref, COMP + 1, t, r)


def filter_group(slabs, damping, tables):
    first, forward, backward, last, twist_cos, twist_sin = tables
    count = len(slabs)
    high, low = halves(jnp.concatenate(slabs, axis=1))
    spectrum = jnp.dot(first, jnp.concatenate([high, low, high], axis=0), preferred_element_type=jnp.float32)
    parts = []
    for k in range(count):
        real = spectrum[:HALF_PAD, k * LANES : (k + 1) * LANES]
        imag = spectrum[HALF_PAD:, k * LANES : (k + 1) * LANES]
        parts.append(
            jnp.concatenate([real * twist_cos + imag * twist_sin, imag * twist_cos - real * twist_sin], axis=1)
        )
    high, low = halves(jnp.concatenate(parts, axis=0))
    spectrum = jnp.dot(jnp.concatenate([high, low, high], axis=1), forward, preferred_element_type=jnp.float32)
    parts = []
    for k in range(count):
        rows = spectrum[k * HALF_PAD : (k + 1) * HALF_PAD]
        parts.append(rows * jnp.concatenate([damping[k], damping[k]], axis=1))
    high, low = halves(jnp.concatenate(parts, axis=0))
    spectrum = jnp.dot(jnp.concatenate([high, low, high], axis=1), backward, preferred_element_type=jnp.float32)
    parts = []
    for k in range(count):
        real = spectrum[k * HALF_PAD : (k + 1) * HALF_PAD, :LANES]
        imag = spectrum[k * HALF_PAD : (k + 1) * HALF_PAD, LANES:]
        parts.append(
            jnp.concatenate([real * twist_cos - imag * twist_sin, imag * twist_cos + real * twist_sin], axis=0)
        )
    high, low = halves(jnp.concatenate(parts, axis=1))
    rebuilt = jnp.dot(last, jnp.concatenate([high, low, high], axis=0), preferred_element_type=jnp.float32)
    return [rebuilt[:, k * LANES : (k + 1) * LANES] for k in range(count)]


def filter_rows_into(out_ref, rows, merid_of, listed_ref, center_ref, sine_sq, tables):
    start = first_row()
    for at in range(0, len(rows), GROUP):
        group = rows[at : at + GROUP]
        slabs, damping, flags = [], [], []
        for r in group:
            center = center_ref[start + r]
            ratio = center * (1.0 / cos_cutoff)
            ratio_sq = jnp.full((HALF_PAD, LANES), ratio * ratio, jnp.float32)
            damp = ratio_sq / jnp.maximum(ratio_sq, sine_sq)
            listed = jnp.max(jnp.where(listed_ref[...] == start + r, 1, 0)) > 0
            for c in range(COMP):
                slabs.append(merid_of(r, c))
                damping.append(damp)
                flags.append((r, c, listed))
        filtered = filter_group(slabs, damping, tables)
        for (r, c, listed), plain, value in zip(flags, slabs, filtered):
            chosen = jnp.where(listed, value, plain)
            for t in range(TILES):
                out_ref[pl.ds((c * TILES + t) * ROWS + r, SECTORS, stride=COMP * TILES * ROWS), :] = chosen[
                    t * SECTORS : (t + 1) * SECTORS
                ]


def flux_of(north, courant, own, above):
    return north * (jnp.maximum(courant, 0.0) * own + jnp.minimum(courant, 0.0) * above)


def interior_kernel(
    hop_ref, center_ref, north_ref, listed_ref, in_ref, first_ref, forward_ref, backward_ref, last_ref,
    twist_cos_ref, twist_sin_ref, sine_ref, out_ref, kept_ref, kept_courant_ref, zonal_ref, courant_ref,
):
    start = first_row()
    hop_at = place_of(lax.axis_index("lon")) * ROWS
    tables = (first_ref[...], forward_ref[...], backward_ref[...], last_ref[...], twist_cos_ref[...], twist_sin_ref[...])
    for r in range(ROWS):

        def store(c, at, value):
            zonal_ref[c, r, at, :] = value
            if r in KEPT:
                kept_ref[c, KEPT.index(r), at, :] = value

        zonal_row(in_ref, hop_ref[hop_at + r], r, store)
        for t in range(TILES):
            at = slice(t * SECTORS, (t + 1) * SECTORS)
            value = fetch(in_ref, COMP + 1, t, r)
            courant_ref[r, at, :] = value
            if r in KEPT:
                kept_courant_ref[KEPT.index(r), at, :] = value

    def merid_of(r, c):
        own = zonal_ref[c, r]
        flux = flux_of(north_ref[start + r], courant_ref[r], own, zonal_ref[c, r + 1])
        south = flux_of(north_ref[start + r - 1], courant_ref[r - 1], zonal_ref[c, r - 1], own)
        return own - (flux - south) / jnp.full((OUTER, LANES), center_ref[start + r], jnp.float32)

    filter_rows_into(out_ref, INNER, merid_of, listed_ref, center_ref, sine_ref[...], tables)


def edge_kernel(
    center_ref, north_ref, listed_ref, kept_ref, courant_ref, swap_ref, swap_far_ref, first_ref, forward_ref,
    backward_ref, last_ref, twist_cos_ref, twist_sin_ref, sine_ref, partial_ref, out_ref,
):
    del partial_ref
    start = first_row()
    odd = lax.rem(lax.axis_index("lon"), 2) == 1
    tables = (first_ref[...], forward_ref[...], backward_ref[...], last_ref[...], twist_cos_ref[...], twist_sin_ref[...])
    north_before = jnp.where(start > 0, north_ref[jnp.maximum(start - 1, 0)], 0.0)

    def merid_of(r, c):
        at = KEPT.index(r)
        own = kept_ref[c, at]
        if r == 0:
            flux = flux_of(north_ref[start], courant_ref[at], own, kept_ref[c, at + 1])
            below = jnp.where(odd, swap_ref[c], swap_far_ref[c])
            below_courant = jnp.where(odd, swap_ref[COMP], swap_far_ref[COMP])
            south = flux_of(north_before, below_courant, below, own)
        else:
            above = jnp.where(odd, swap_far_ref[c], swap_ref[c])
            flux = flux_of(north_ref[start + r], courant_ref[at], own, above)
            south = flux_of(north_ref[start + r - 1], courant_ref[at - 1], kept_ref[c, at - 1], own)
        return own - (flux - south) / jnp.full((OUTER, LANES), center_ref[start + r], jnp.float32)

    filter_rows_into(out_ref, (0, ROWS - 1), merid_of, listed_ref, center_ref, sine_ref[...], tables)


def on_device(fields, zonal_fraction, merid_courant, hop_counts, filter_rows):
    smem = pl.BlockSpec(memory_space=pltpu.SMEM)
    vmem = pl.BlockSpec(memory_space=pltpu.VMEM)
    params = pltpu.CompilerParams(vmem_limit_bytes=VMEM_LIMIT)
    stacked = jnp.concatenate([fields[:, 0], zonal_fraction, merid_courant], axis=0)
    outgoing = stacked.reshape(ARRAYS, SECTORS, ROWS, TILES, LANES).transpose(1, 0, 3, 2, 4)
    outgoing = outgoing.reshape(SECTORS, ARRAYS * TILES * ROWS, LANES)
    incoming = lax.all_to_all(outgoing, "lon", 0, 0, tiled=True, axis_index_groups=[list(ORDER)])
    incoming = incoming.reshape(SECTORS * ARRAYS * TILES * ROWS, LANES)
    f32 = jnp.float32
    rim = pl.pallas_call(
        rim_kernel,
        out_shape=jax.ShapeDtypeStruct((2, COMP + 1, OUTER, LANES), f32),
        in_specs=[smem, vmem],
        out_specs=vmem,
        compiler_params=params,
    )(hop_counts, incoming)
    bands = NLAT // BAND
    total = bands * SECTORS

    def device_of(block):
        return ORDER[block % SECTORS] * bands + block // SECTORS

    def swap(value, first_block):
        pairs = [(device_of(i), device_of(i + 1)) for i in range(first_block, total - 1, 2)]
        return lax.ppermute(value, ("lon", "lat"), pairs + [(j, i) for i, j in pairs])

    swapped = swap(rim[0], 0)
    swapped_far = swap(rim[1], 1)
    first, forward, backward, last, twist_cos, twist_sin, sine_sq = [jnp.asarray(v) for v in filter_tables()]
    center, north = [jnp.asarray(v) for v in latitude_tables()]
    listed = filter_rows.reshape(4, LANES)
    out_shape = jax.ShapeDtypeStruct((SECTORS * COMP * TILES * ROWS, LANES), f32)
    constants = (first, forward, backward, last, twist_cos, twist_sin, sine_sq)
    partial, kept, kept_courant = pl.pallas_call(
        interior_kernel,
        out_shape=(
            out_shape,
            jax.ShapeDtypeStruct((COMP, len(KEPT), OUTER, LANES), f32),
            jax.ShapeDtypeStruct((len(KEPT), OUTER, LANES), f32),
        ),
        in_specs=[smem] * 3 + [vmem] * 9,
        out_specs=(vmem, vmem, vmem),
        scratch_shapes=[
            pltpu.VMEM((COMP, ROWS, OUTER, LANES), f32),
            pltpu.VMEM((ROWS, OUTER, LANES), f32),
        ],
        compiler_params=params,
        cost_estimate=pl.CostEstimate(flops=5_000_000_000, bytes_accessed=8_000_000, transcendentals=0),
    )(hop_counts, center, north, listed, incoming, *constants)
    returning = pl.pallas_call(
        edge_kernel,
        out_shape=out_shape,
        in_specs=[smem, smem] + [vmem] * 13,
        out_specs=vmem,
        input_output_aliases={14: 0},
        compiler_params=params,
        cost_estimate=pl.CostEstimate(flops=1_000_000_000, bytes_accessed=4_000_000, transcendentals=0),
    )(center, north, listed, kept, kept_courant, swapped, swapped_far, *constants, partial)
    arrived = lax.all_to_all(
        returning.reshape(SECTORS, COMP * TILES * ROWS, LANES), "lon", 0, 0, tiled=True, axis_index_groups=[list(ORDER)]
    )
    arrived = arrived.reshape(SECTORS, COMP, TILES, ROWS, LANES).transpose(1, 0, 3, 2, 4)
    return arrived.reshape(COMP, 1, BAND, TILES * LANES)


def solution(mesh):
    in_specs = (
        P(None, None, "lat", "lon"),
        P(None, "lat", "lon"),
        P(None, "lat", "lon"),
        P("lat"),
        P(),
    )
    out_specs = P(None, None, "lat", "lon")
    return jax.shard_map(
        on_device, mesh=mesh, in_specs=in_specs, out_specs=out_specs, check_vma=False
    )
```

```python
import functools
import math

import jax
import jax.numpy as jnp
import ml_dtypes
import numpy as np
from jax import lax
from jax.experimental import pallas as pl
from jax.experimental.pallas import tpu as pltpu
from jax.sharding import PartitionSpec as P

NLON = 12288
NLAT = 2048
SECTORS = 16
BAND = 128
ROWS = 8
TILES = 6
LANES = 128
OUTER = SECTORS * TILES
COMP = 3
ARRAYS = COMP + 2
HALF = OUTER // 2 + 1
HALF_PAD = 56
ORDER = tuple(4 * y + 2 * x + core for x in (0, 1) for y in ((0, 1, 2, 3), (3, 2, 1, 0))[x] for core in (0, 1))
INNER = (1, 2, 3, 4, 5, 6)
GROUP = 6
VMEM_LIMIT = 48 * 1024 * 1024

cos_cutoff = 0.7071067811865476


def split_bf16(table):
    high = table.astype(np.float32).astype(ml_dtypes.bfloat16)
    low = (table - high.astype(np.float64)).astype(np.float32).astype(ml_dtypes.bfloat16)
    return high, low


def filter_tables():
    at = np.arange(OUTER)
    a = TILES * np.asarray(ORDER)[at % SECTORS] + at // SECTORS
    c = np.arange(HALF_PAD)
    valid = (c < HALF)[:, None]
    angle = 2.0 * np.pi * ((c[:, None] * a[None, :]) % OUTER) / OUTER
    first = np.concatenate([np.where(valid, np.cos(angle), 0.0), np.where(valid, -np.sin(angle), 0.0)], axis=0)
    weight = np.where((c == 0) | (c == OUTER // 2), 1.0, 2.0) / NLON
    inner_only = (c > 0) & (c < OUTER // 2)
    last = np.concatenate(
        [
            np.where(valid, np.cos(angle) * weight[:, None], 0.0),
            np.where(valid & inner_only[:, None], -np.sin(angle) * weight[:, None], 0.0),
        ],
        axis=0,
    ).T
    b = np.arange(LANES)
    twist = 2.0 * np.pi * (c[:, None] * b[None, :]) / NLON
    inner = 2.0 * np.pi * ((b[:, None] * b[None, :]) % LANES) / LANES
    cos_in, sin_in = np.cos(inner), np.sin(inner)
    forward = np.block([[cos_in, -sin_in], [sin_in, cos_in]])
    backward = np.block([[cos_in, sin_in], [-sin_in, cos_in]])
    sine = np.sin(np.pi * (c[:, None] + OUTER * b[None, :]) / NLON)
    first_h, first_l = split_bf16(first)
    last_h, last_l = split_bf16(last)
    forward_h, forward_l = split_bf16(forward)
    backward_h, backward_l = split_bf16(backward)
    return (
        np.concatenate([first_h, first_h, first_l], axis=1),
        np.concatenate([forward_h, forward_h, forward_l], axis=0),
        np.concatenate([backward_h, backward_h, backward_l], axis=0),
        np.concatenate([last_h, last_h, last_l], axis=1),
        np.cos(twist).astype(np.float32),
        np.sin(twist).astype(np.float32),
        (sine * sine).astype(np.float32),
    )


NORTH, SOUTH, RATIO = range(3)


def latitude_table():
    row = np.arange(NLAT, dtype=np.float32)
    step = np.float32(math.pi / NLAT)
    center = np.sin(((row + np.float32(0.5)) * step).astype(np.float64))
    north = np.sin(((row + np.float32(1.0)) * step).astype(np.float64))
    north[-1] = 0.0
    south = np.concatenate([np.zeros(1), north[:-1]])
    ratio = center / cos_cutoff
    kinds = [v.reshape(NLAT // ROWS, ROWS) for v in (north / center, south / center, ratio * ratio)]
    return np.pad(np.concatenate(kinds, axis=1), ((0, 0), (0, LANES - 3 * ROWS))).astype(np.float32)


def latitude_line(table_ref):
    block = lax.axis_index("lat") * SECTORS + place_of(lax.axis_index("lon"))
    return table_ref[pl.ds(block, 1), :]


def spread(line, lane, rows=SECTORS):
    return jnp.broadcast_to(line[:, lane : lane + 1], (rows, LANES))


def own_hops(hop_ref):
    start = place_of(lax.axis_index("lon")) * ROWS
    line = pltpu.roll(jnp.broadcast_to(hop_ref[...], (8, LANES)), lax.rem(LANES - start, LANES), 1)[:1]
    return [spread(line, r) for r in range(ROWS)]


def halves(value):
    high = value.astype(jnp.bfloat16)
    low = (value - high.astype(jnp.float32)).astype(jnp.bfloat16)
    return high, low


def place_of(sector):
    along, core = lax.shift_right_logical(sector, 2) * 2, lax.bitwise_and(sector, 1)
    return jnp.where(lax.bitwise_and(sector, 2) == 0, along + core, 14 - along + core)


def sector_at(place):
    along, core = lax.shift_right_logical(lax.bitwise_and(place, 7), 1) * 4, lax.bitwise_and(place, 1)
    return jnp.where(place < 8, along + core, 14 - along + core)


def first_row():
    return lax.axis_index("lat") * BAND + place_of(lax.axis_index("lon")) * ROWS


def from_sector(tile, source):
    low, high = tile[:8], tile[8:]
    parts = []
    for at in (slice(0, 8), slice(8, 16)):
        index = lax.bitwise_and(source[at], 7)
        parts.append(
            jnp.where(
                source[at] < 8,
                jnp.take_along_axis(low, index, axis=0, mode="promise_in_bounds"),
                jnp.take_along_axis(high, index, axis=0, mode="promise_in_bounds"),
            )
        )
    return jnp.concatenate(parts, axis=0)


def fetch(in_ref, array, t, r):
    return in_ref[pl.ds((array * TILES + t) * ROWS + r, SECTORS, stride=ARRAYS * TILES * ROWS), :]


def zonal_row(in_ref, hop, r, store):
    lane = lax.broadcasted_iota(jnp.int32, (SECTORS, LANES), 1)
    own_sector = sector_at(lax.broadcasted_iota(jnp.int32, (SECTORS, LANES), 0))

    def source(hops):
        return place_of(lax.bitwise_and(own_sector - hops + SECTORS, SECTORS - 1))

    sources, sources_before, sources_after = source(hop), source(hop + 1), source(hop - 1)
    weights = []
    for t in range(TILES):
        offset = 1.0 - fetch(in_ref, COMP, t, r)
        w_far = -offset * (offset - 1.0) * (offset - 2.0) * (1.0 / 6.0)
        w_near = (offset + 1.0) * (offset - 1.0) * (offset - 2.0) * 0.5
        w_next = -(offset + 1.0) * offset * (offset - 2.0) * 0.5
        w_last = (offset + 1.0) * offset * (offset - 1.0) * (1.0 / 6.0)
        weights.append((w_far, w_near, w_next, w_last))
    for c in range(COMP):
        raw = [fetch(in_ref, c, t, r) for t in range(TILES)]
        here = [from_sector(v, sources) for v in raw]
        before = from_sector(raw[TILES - 1], sources_before)
        after = from_sector(raw[0], sources_after)
        back_one = [pltpu.roll(v, 1, 1) for v in [before] + here]
        back_two = [pltpu.roll(v, 2, 1) for v in [before] + here]
        ahead = [pltpu.roll(v, LANES - 1, 1) for v in here + [after]]
        for t in range(TILES):
            w_far, w_near, w_next, w_last = weights[t]
            store(
                c,
                slice(t * SECTORS, (t + 1) * SECTORS),
                w_far * jnp.where(lane < 2, back_two[t], back_two[t + 1])
                + w_near * jnp.where(lane < 1, back_one[t], back_one[t + 1])
                + w_next * here[t]
                + w_last * jnp.where(lane == LANES - 1, ahead[t + 1], ahead[t]),
            )


def rim_kernel(hop_ref, in_ref, rim_ref, near_ref, far_ref):
    hops = own_hops(hop_ref)
    odd = lax.rem(lax.axis_index("lon"), 2) == 1
    rows = []
    for at, r in enumerate((0, ROWS - 1)):
        values = {}

        def store(c, block, value):
            values[c, block.start] = value

        zonal_row(in_ref, hops[r], r, store)
        for t in range(TILES):
            values[COMP, t * SECTORS] = fetch(in_ref, COMP + 1, t, r)
        for (c, place), value in values.items():
            rim_ref[at, c, place : place + SECTORS, :] = value
        rows.append(values)
    for c, place in rows[0]:
        first, last = rows[0][c, place], rows[1][c, place]
        near_ref[c, place : place + SECTORS, :] = jnp.where(odd, first, last)
        far_ref[c, place : place + SECTORS, :] = jnp.where(odd, last, first)


def filter_group(slabs, damping, tables):
    first, forward, backward, last, twist_cos, twist_sin = tables
    count = len(slabs)
    high, low = halves(jnp.concatenate(slabs, axis=1))
    spectrum = jnp.dot(first, jnp.concatenate([high, low, high], axis=0), preferred_element_type=jnp.float32)
    parts = []
    for k in range(count):
        real = spectrum[:HALF_PAD, k * LANES : (k + 1) * LANES]
        imag = spectrum[HALF_PAD:, k * LANES : (k + 1) * LANES]
        parts.append(
            jnp.concatenate([real * twist_cos + imag * twist_sin, imag * twist_cos - real * twist_sin], axis=1)
        )
    high, low = halves(jnp.concatenate(parts, axis=0))
    spectrum = jnp.dot(jnp.concatenate([high, low, high], axis=1), forward, preferred_element_type=jnp.float32)
    parts = []
    for k in range(count):
        rows = spectrum[k * HALF_PAD : (k + 1) * HALF_PAD]
        parts.append(rows * jnp.concatenate([damping[k], damping[k]], axis=1))
    high, low = halves(jnp.concatenate(parts, axis=0))
    spectrum = jnp.dot(jnp.concatenate([high, low, high], axis=1), backward, preferred_element_type=jnp.float32)
    parts = []
    for k in range(count):
        real = spectrum[k * HALF_PAD : (k + 1) * HALF_PAD, :LANES]
        imag = spectrum[k * HALF_PAD : (k + 1) * HALF_PAD, LANES:]
        parts.append(
            jnp.concatenate([real * twist_cos - imag * twist_sin, imag * twist_cos + real * twist_sin], axis=0)
        )
    high, low = halves(jnp.concatenate(parts, axis=1))
    rebuilt = jnp.dot(last, jnp.concatenate([high, low, high], axis=0), preferred_element_type=jnp.float32)
    return [rebuilt[:, k * LANES : (k + 1) * LANES] for k in range(count)]


def listed_mask(listed_ref, row):
    hit = jnp.where(listed_ref[...] == row, 1.0, 0.0)
    hit = jnp.max(jnp.max(hit, axis=1, keepdims=True), axis=0, keepdims=True)
    return jnp.broadcast_to(hit, (SECTORS, LANES)) > 0.5


def filter_rows_into(out_ref, rows, merid_ref, listed_ref, line, sine_sq, tables, group_size):
    start = first_row()
    for at in range(0, len(rows), group_size):
        group = range(at, min(at + group_size, len(rows)))
        damping = []
        for i in group:
            ratio_sq = spread(line, RATIO * ROWS + rows[i], HALF_PAD)
            damping.extend([ratio_sq / jnp.maximum(ratio_sq, sine_sq)] * COMP)
        slabs = [merid_ref[c, i] for i in group for c in range(COMP)]
        filtered = filter_group(slabs, damping, tables)
        for i in group:
            listed = listed_mask(listed_ref, start + rows[i])
            for c in range(COMP):
                value = filtered[(i - at) * COMP + c]
                for t in range(TILES):
                    block = slice(t * SECTORS, (t + 1) * SECTORS)
                    out_ref[pl.ds((c * TILES + t) * ROWS + rows[i], SECTORS, stride=COMP * TILES * ROWS), :] = jnp.where(
                        listed, value[block], merid_ref[c, i, block, :]
                    )


def through_face(courant, own, above):
    return jnp.maximum(courant, 0.0) * own + jnp.minimum(courant, 0.0) * above


def interior_kernel(
    hop_ref, table_ref, listed_ref, in_ref, rim_ref, first_ref, forward_ref, backward_ref,
    last_ref, twist_cos_ref, twist_sin_ref, sine_ref, out_ref, kept_ref, zonal_ref, merid_ref,
):
    line = latitude_line(table_ref)
    hops = own_hops(hop_ref)
    tables = (first_ref[...], forward_ref[...], backward_ref[...], last_ref[...], twist_cos_ref[...], twist_sin_ref[...])
    for r in INNER:

        def store(c, at, value):
            zonal_ref[c, r, at, :] = value

        zonal_row(in_ref, hops[r], r, store)
    north = [spread(line, NORTH * ROWS + r) for r in range(ROWS)]
    south = [spread(line, SOUTH * ROWS + r) for r in range(ROWS)]
    for t in range(TILES):
        at = slice(t * SECTORS, (t + 1) * SECTORS)
        own = [rim_ref[0, c, at, :] for c in range(COMP)]
        last_row = [rim_ref[1, c, at, :] for c in range(COMP)]
        before = None
        for r in range(ROWS - 1):
            courant = fetch(in_ref, COMP + 1, t, r)
            above = last_row if r == ROWS - 2 else [zonal_ref[c, r + 1, at, :] for c in range(COMP)]
            face = [through_face(courant, own[c], above[c]) for c in range(COMP)]
            for c in range(COMP):
                merid = own[c] - north[r] * face[c]
                if r == 0:
                    kept_ref[0, c, at, :] = merid
                else:
                    merid_ref[c, r - 1, at, :] = merid + south[r] * before[c]
            own, before = above, face
        for c in range(COMP):
            kept_ref[1, c, at, :] = own[c] + south[ROWS - 1] * before[c]
    filter_rows_into(out_ref, INNER, merid_ref, listed_ref, line, sine_ref[...], tables, GROUP)


def edge_kernel(
    table_ref, listed_ref, kept_ref, rim_ref, swap_ref, swap_far_ref, first_ref, forward_ref,
    backward_ref, last_ref, twist_cos_ref, twist_sin_ref, sine_ref, partial_ref, out_ref, merid_ref,
):
    del partial_ref
    line = latitude_line(table_ref)
    south, north = spread(line, SOUTH * ROWS), spread(line, NORTH * ROWS + ROWS - 1)
    is_odd = lax.rem(lax.axis_index("lon"), 2) == 1
    tables = (first_ref[...], forward_ref[...], backward_ref[...], last_ref[...], twist_cos_ref[...], twist_sin_ref[...])
    for t in range(TILES):
        at = slice(t * SECTORS, (t + 1) * SECTORS)
        near = [swap_ref[c, at, :] for c in range(COMP + 1)]
        far = [swap_far_ref[c, at, :] for c in range(COMP + 1)]
        below = [jnp.where(is_odd, n, f) for n, f in zip(near, far)]
        above = [jnp.where(is_odd, f, n) for n, f in zip(near, far)]
        courant = rim_ref[1, COMP, at, :]
        for c in range(COMP):
            face = through_face(below[COMP], below[c], rim_ref[0, c, at, :])
            merid_ref[c, 0, at, :] = kept_ref[0, c, at, :] + south * face
            face = through_face(courant, rim_ref[1, c, at, :], above[c])
            merid_ref[c, 1, at, :] = kept_ref[1, c, at, :] - north * face
    filter_rows_into(out_ref, (0, ROWS - 1), merid_ref, listed_ref, line, sine_ref[...], tables, 2)


def on_device(fields, zonal_fraction, merid_courant, hop_counts, filter_rows):
    vmem = pl.BlockSpec(memory_space=pltpu.VMEM)
    params = pltpu.CompilerParams(vmem_limit_bytes=VMEM_LIMIT)
    hops = hop_counts.reshape(1, BAND)
    stacked = jnp.concatenate([fields[:, 0], zonal_fraction, merid_courant], axis=0)
    outgoing = stacked.reshape(ARRAYS, SECTORS, ROWS, TILES, LANES).transpose(1, 0, 3, 2, 4)
    outgoing = outgoing.reshape(SECTORS, ARRAYS * TILES * ROWS, LANES)
    incoming = lax.all_to_all(outgoing, "lon", 0, 0, tiled=True, axis_index_groups=[list(ORDER)])
    incoming = incoming.reshape(SECTORS * ARRAYS * TILES * ROWS, LANES)
    f32 = jnp.float32
    edge_shape = jax.ShapeDtypeStruct((COMP + 1, OUTER, LANES), f32)
    rim, near, far = pl.pallas_call(
        rim_kernel,
        out_shape=(jax.ShapeDtypeStruct((2, COMP + 1, OUTER, LANES), f32), edge_shape, edge_shape),
        in_specs=[vmem, vmem],
        out_specs=(vmem, vmem, vmem),
        compiler_params=params,
    )(hops, incoming)
    bands = NLAT // BAND
    total = bands * SECTORS

    def device_of(block):
        return ORDER[block % SECTORS] * bands + block // SECTORS

    def swap(value, first_block):
        pairs = [(device_of(i), device_of(i + 1)) for i in range(first_block, total - 1, 2)]
        return lax.ppermute(value, ("lon", "lat"), pairs + [(j, i) for i, j in pairs])

    swapped = swap(near, 0)
    swapped_far = swap(far, 1)
    first, forward, backward, last, twist_cos, twist_sin, sine_sq = [jnp.asarray(v) for v in filter_tables()]
    latitudes = jnp.asarray(latitude_table())
    listed = filter_rows.reshape(4, LANES)
    out_shape = jax.ShapeDtypeStruct((SECTORS * COMP * TILES * ROWS, LANES), f32)
    constants = (first, forward, backward, last, twist_cos, twist_sin, sine_sq)
    partial, kept = pl.pallas_call(
        interior_kernel,
        out_shape=(out_shape, jax.ShapeDtypeStruct((2, COMP, OUTER, LANES), f32)),
        in_specs=[vmem] * 12,
        out_specs=(vmem, vmem),
        scratch_shapes=[
            pltpu.VMEM((COMP, ROWS, OUTER, LANES), f32),
            pltpu.VMEM((COMP, len(INNER), OUTER, LANES), f32),
        ],
        compiler_params=params,
        cost_estimate=pl.CostEstimate(flops=5_000_000_000, bytes_accessed=8_000_000, transcendentals=0),
    )(hops, latitudes, listed, incoming, rim, *constants)
    returning = pl.pallas_call(
        edge_kernel,
        out_shape=out_shape,
        in_specs=[vmem] * 14,
        out_specs=vmem,
        input_output_aliases={13: 0},
        scratch_shapes=[pltpu.VMEM((COMP, 2, OUTER, LANES), f32)],
        compiler_params=params,
        cost_estimate=pl.CostEstimate(flops=1_000_000_000, bytes_accessed=4_000_000, transcendentals=0),
    )(latitudes, listed, kept, rim, swapped, swapped_far, *constants, partial)
    arrived = lax.all_to_all(
        returning.reshape(SECTORS, COMP * TILES * ROWS, LANES), "lon", 0, 0, tiled=True, axis_index_groups=[list(ORDER)]
    )
    arrived = arrived.reshape(SECTORS, COMP, TILES, ROWS, LANES).transpose(1, 0, 3, 2, 4)
    return arrived.reshape(COMP, 1, BAND, TILES * LANES)


def solution(mesh):
    in_specs = (
        P(None, None, "lat", "lon"),
        P(None, "lat", "lon"),
        P(None, "lat", "lon"),
        P("lat"),
        P(),
    )
    out_specs = P(None, None, "lat", "lon")
    return jax.shard_map(
        on_device, mesh=mesh, in_specs=in_specs, out_specs=out_specs, check_vma=False
    )
```

```python
import functools
import math

import jax
import jax.numpy as jnp
import ml_dtypes
import numpy as np
from jax import lax
from jax.experimental import pallas as pl
from jax.experimental.pallas import tpu as pltpu
from jax.sharding import PartitionSpec as P

NLON = 12288
NLAT = 2048
SECTORS = 16
BAND = 128
ROWS = 8
TILES = 6
LANES = 128
OUTER = SECTORS * TILES
COMP = 3
ARRAYS = COMP + 2
HALF = OUTER // 2 + 1
HALF_PAD = 56
ORDER = tuple(4 * y + 2 * x + core for x in (0, 1) for y in ((0, 1, 2, 3), (3, 2, 1, 0))[x] for core in (0, 1))
INNER = (1, 2, 3, 4, 5, 6)
VMEM_LIMIT = 48 * 1024 * 1024

cos_cutoff = 0.7071067811865476


def split_bf16(table):
    high = table.astype(np.float32).astype(ml_dtypes.bfloat16)
    low = (table - high.astype(np.float64)).astype(np.float32).astype(ml_dtypes.bfloat16)
    return high, low


def filter_tables():
    at = np.arange(OUTER)
    a = TILES * np.asarray(ORDER)[at % SECTORS] + at // SECTORS
    c = np.arange(HALF_PAD)
    valid = (c < HALF)[:, None]
    angle = 2.0 * np.pi * ((c[:, None] * a[None, :]) % OUTER) / OUTER
    first = np.concatenate([np.where(valid, np.cos(angle), 0.0), np.where(valid, -np.sin(angle), 0.0)], axis=0)
    weight = np.where((c == 0) | (c == OUTER // 2), 1.0, 2.0) / NLON
    inner_only = (c > 0) & (c < OUTER // 2)
    last = np.concatenate(
        [
            np.where(valid, np.cos(angle) * weight[:, None], 0.0),
            np.where(valid & inner_only[:, None], -np.sin(angle) * weight[:, None], 0.0),
        ],
        axis=0,
    ).T
    b = np.arange(LANES)
    twist = 2.0 * np.pi * (c[:, None] * b[None, :]) / NLON
    inner = 2.0 * np.pi * ((b[:, None] * b[None, :]) % LANES) / LANES
    cos_in, sin_in = np.cos(inner), np.sin(inner)
    forward = np.block([[cos_in, -sin_in], [sin_in, cos_in]])
    backward = np.block([[cos_in, sin_in], [-sin_in, cos_in]])
    sine = np.sin(np.pi * (c[:, None] + OUTER * b[None, :]) / NLON)
    first_h, first_l = split_bf16(first)
    last_h, last_l = split_bf16(last)
    forward_h, forward_l = split_bf16(forward)
    backward_h, backward_l = split_bf16(backward)
    return (
        np.concatenate([first_h, first_h, first_l], axis=1),
        np.concatenate([forward_h, forward_h, forward_l], axis=0),
        np.concatenate([backward_h, backward_h, backward_l], axis=0),
        np.concatenate([last_h, last_h, last_l], axis=1),
        np.cos(twist).astype(np.float32),
        np.sin(twist).astype(np.float32),
        (sine * sine).astype(np.float32),
    )


NORTH, SOUTH, RATIO = range(3)


def latitude_table():
    row = np.arange(NLAT, dtype=np.float32)
    step = np.float32(math.pi / NLAT)
    center = np.sin(((row + np.float32(0.5)) * step).astype(np.float64))
    north = np.sin(((row + np.float32(1.0)) * step).astype(np.float64))
    north[-1] = 0.0
    south = np.concatenate([np.zeros(1), north[:-1]])
    ratio = center / cos_cutoff
    kinds = [v.reshape(NLAT // ROWS, ROWS) for v in (north / center, south / center, ratio * ratio)]
    return np.pad(np.concatenate(kinds, axis=1), ((0, 0), (0, LANES - 3 * ROWS))).astype(np.float32)


def latitude_line(table_ref):
    block = lax.axis_index("lat") * SECTORS + place_of(lax.axis_index("lon"))
    return table_ref[pl.ds(block, 1), :]


def spread(line, lane, rows=SECTORS):
    return jnp.broadcast_to(line[:, lane : lane + 1], (rows, LANES))


def own_hops(hop_ref):
    start = place_of(lax.axis_index("lon")) * ROWS
    line = pltpu.roll(jnp.broadcast_to(hop_ref[...], (8, LANES)), lax.rem(LANES - start, LANES), 1)[:1]
    return [spread(line, r) for r in range(ROWS)]


def halves(value):
    high = value.astype(jnp.bfloat16)
    low = (value - high.astype(jnp.float32)).astype(jnp.bfloat16)
    return high, low


def place_of(sector):
    along, core = lax.shift_right_logical(sector, 2) * 2, lax.bitwise_and(sector, 1)
    return jnp.where(lax.bitwise_and(sector, 2) == 0, along + core, 14 - along + core)


def sector_at(place):
    along, core = lax.shift_right_logical(lax.bitwise_and(place, 7), 1) * 4, lax.bitwise_and(place, 1)
    return jnp.where(place < 8, along + core, 14 - along + core)


def first_row():
    return lax.axis_index("lat") * BAND + place_of(lax.axis_index("lon")) * ROWS


def from_sector(tile, source):
    low, high = tile[:8], tile[8:]
    parts = []
    for at in (slice(0, 8), slice(8, 16)):
        index = lax.bitwise_and(source[at], 7)
        parts.append(
            jnp.where(
                source[at] < 8,
                jnp.take_along_axis(low, index, axis=0, mode="promise_in_bounds"),
                jnp.take_along_axis(high, index, axis=0, mode="promise_in_bounds"),
            )
        )
    return jnp.concatenate(parts, axis=0)


def fetch(in_ref, array, t, r):
    return in_ref[pl.ds((array * TILES + t) * ROWS + r, SECTORS, stride=ARRAYS * TILES * ROWS), :]


def zonal_row(in_ref, hop, r, store):
    lane = lax.broadcasted_iota(jnp.int32, (SECTORS, LANES), 1)
    own_sector = sector_at(lax.broadcasted_iota(jnp.int32, (SECTORS, LANES), 0))

    def source(hops):
        return place_of(lax.bitwise_and(own_sector - hops + SECTORS, SECTORS - 1))

    sources, sources_before, sources_after = source(hop), source(hop + 1), source(hop - 1)
    weights = []
    for t in range(TILES):
        offset = 1.0 - fetch(in_ref, COMP, t, r)
        w_far = -offset * (offset - 1.0) * (offset - 2.0) * (1.0 / 6.0)
        w_near = (offset + 1.0) * (offset - 1.0) * (offset - 2.0) * 0.5
        w_next = -(offset + 1.0) * offset * (offset - 2.0) * 0.5
        w_last = (offset + 1.0) * offset * (offset - 1.0) * (1.0 / 6.0)
        weights.append((w_far, w_near, w_next, w_last))
    for c in range(COMP):
        raw = [fetch(in_ref, c, t, r) for t in range(TILES)]
        here = [from_sector(v, sources) for v in raw]
        before = from_sector(raw[TILES - 1], sources_before)
        after = from_sector(raw[0], sources_after)
        back_one = [pltpu.roll(v, 1, 1) for v in [before] + here]
        back_two = [pltpu.roll(v, 2, 1) for v in [before] + here]
        ahead = [pltpu.roll(v, LANES - 1, 1) for v in here + [after]]
        for t in range(TILES):
            w_far, w_near, w_next, w_last = weights[t]
            store(
                c,
                slice(t * SECTORS, (t + 1) * SECTORS),
                w_far * jnp.where(lane < 2, back_two[t], back_two[t + 1])
                + w_near * jnp.where(lane < 1, back_one[t], back_one[t + 1])
                + w_next * here[t]
                + w_last * jnp.where(lane == LANES - 1, ahead[t + 1], ahead[t]),
            )


def rim_kernel(hop_ref, in_ref, rim_ref, near_ref, far_ref):
    hops = own_hops(hop_ref)
    odd = lax.rem(lax.axis_index("lon"), 2) == 1
    rows = []
    for at, r in enumerate((0, ROWS - 1)):
        values = {}

        def store(c, block, value):
            values[c, block.start] = value

        zonal_row(in_ref, hops[r], r, store)
        for t in range(TILES):
            values[COMP, t * SECTORS] = fetch(in_ref, COMP + 1, t, r)
        for (c, place), value in values.items():
            rim_ref[at, c, place : place + SECTORS, :] = value
        rows.append(values)
    for c, place in rows[0]:
        first, last = rows[0][c, place], rows[1][c, place]
        near_ref[c, place : place + SECTORS, :] = jnp.where(odd, first, last)
        far_ref[c, place : place + SECTORS, :] = jnp.where(odd, last, first)


def filter_group(slabs, damping, tables):
    first, forward, backward, last, twist_cos, twist_sin = tables
    count = len(slabs)
    high, low = halves(jnp.concatenate(slabs, axis=1))
    spectrum = jnp.dot(first, jnp.concatenate([high, low, high], axis=0), preferred_element_type=jnp.float32)
    parts = []
    for k in range(count):
        real = spectrum[:HALF_PAD, k * LANES : (k + 1) * LANES]
        imag = spectrum[HALF_PAD:, k * LANES : (k + 1) * LANES]
        parts.append(
            jnp.concatenate([real * twist_cos + imag * twist_sin, imag * twist_cos - real * twist_sin], axis=1)
        )
    high, low = halves(jnp.concatenate(parts, axis=0))
    spectrum = jnp.dot(jnp.concatenate([high, low, high], axis=1), forward, preferred_element_type=jnp.float32)
    parts = []
    for k in range(count):
        rows = spectrum[k * HALF_PAD : (k + 1) * HALF_PAD]
        parts.append(rows * jnp.concatenate([damping[k], damping[k]], axis=1))
    high, low = halves(jnp.concatenate(parts, axis=0))
    spectrum = jnp.dot(jnp.concatenate([high, low, high], axis=1), backward, preferred_element_type=jnp.float32)
    parts = []
    for k in range(count):
        real = spectrum[k * HALF_PAD : (k + 1) * HALF_PAD, :LANES]
        imag = spectrum[k * HALF_PAD : (k + 1) * HALF_PAD, LANES:]
        parts.append(
            jnp.concatenate([real * twist_cos - imag * twist_sin, imag * twist_cos + real * twist_sin], axis=0)
        )
    high, low = halves(jnp.concatenate(parts, axis=1))
    rebuilt = jnp.dot(last, jnp.concatenate([high, low, high], axis=0), preferred_element_type=jnp.float32)
    return [rebuilt[:, k * LANES : (k + 1) * LANES] for k in range(count)]


def listed_mask(listed_ref, row):
    hit = jnp.where(listed_ref[...] == row, 1.0, 0.0)
    hit = jnp.max(jnp.max(hit, axis=1, keepdims=True), axis=0, keepdims=True)
    return jnp.broadcast_to(hit, (SECTORS, LANES)) > 0.5


def filter_rows_into(out_ref, rows, ratios, merid_ref, listed_ref, sine_sq, tables):
    start = first_row()
    damping = []
    for ratio_sq in ratios:
        damping.extend([ratio_sq / jnp.maximum(ratio_sq, sine_sq)] * COMP)
    slabs = [merid_ref[c, i] for i in range(len(rows)) for c in range(COMP)]
    filtered = filter_group(slabs, damping, tables)
    for i, row in enumerate(rows):
        listed = listed_mask(listed_ref, start + row)
        for c in range(COMP):
            value = filtered[i * COMP + c]
            for t in range(TILES):
                block = slice(t * SECTORS, (t + 1) * SECTORS)
                out_ref[pl.ds((c * TILES + t) * ROWS + row, SECTORS, stride=COMP * TILES * ROWS), :] = jnp.where(
                    listed, value[block], merid_ref[c, i, block, :]
                )


def through_face(courant, own, above):
    return jnp.maximum(courant, 0.0) * own + jnp.minimum(courant, 0.0) * above


def outer_rows(line):
    odd = lax.rem(lax.axis_index("lon"), 2) == 1
    first, last = spread(line, RATIO * ROWS, HALF_PAD), spread(line, RATIO * ROWS + ROWS - 1, HALF_PAD)
    near, far = jnp.where(odd, 0, ROWS - 1), jnp.where(odd, ROWS - 1, 0)
    return near, far, jnp.where(odd, first, last), jnp.where(odd, last, first)


def interior_kernel(
    hop_ref, table_ref, listed_ref, in_ref, rim_ref, swap_ref, first_ref, forward_ref, backward_ref, last_ref,
    twist_cos_ref, twist_sin_ref, sine_ref, out_ref, kept_ref, zonal_ref, merid_ref,
):
    line = latitude_line(table_ref)
    hops = own_hops(hop_ref)
    odd = lax.rem(lax.axis_index("lon"), 2) == 1
    tables = (first_ref[...], forward_ref[...], backward_ref[...], last_ref[...], twist_cos_ref[...], twist_sin_ref[...])
    for r in INNER:

        def store(c, at, value):
            zonal_ref[c, r, at, :] = value

        zonal_row(in_ref, hops[r], r, store)
    north = [spread(line, NORTH * ROWS + r) for r in range(ROWS)]
    south = [spread(line, SOUTH * ROWS + r) for r in range(ROWS)]
    outside = jnp.where(odd, south[0], -north[ROWS - 1])
    for t in range(TILES):
        at = slice(t * SECTORS, (t + 1) * SECTORS)
        first_row_of = own = [rim_ref[0, c, at, :] for c in range(COMP)]
        last_row_of = [rim_ref[1, c, at, :] for c in range(COMP)]
        before = None
        kept = []
        for r in range(ROWS - 1):
            courant = fetch(in_ref, COMP + 1, t, r)
            above = last_row_of if r == ROWS - 2 else [zonal_ref[c, r + 1, at, :] for c in range(COMP)]
            face = [through_face(courant, own[c], above[c]) for c in range(COMP)]
            for c in range(COMP):
                merid = own[c] - north[r] * face[c]
                if r == 0:
                    kept.append(merid)
                else:
                    merid_ref[c, r - 1, at, :] = merid + south[r] * before[c]
            own, before = above, face
        courant = jnp.where(odd, swap_ref[COMP, at, :], rim_ref[1, COMP, at, :])
        for c in range(COMP):
            last = last_row_of[c] + south[ROWS - 1] * before[c]
            other = swap_ref[c, at, :]
            face = through_face(
                courant, jnp.where(odd, other, last_row_of[c]), jnp.where(odd, first_row_of[c], other)
            )
            merid_ref[c, len(INNER), at, :] = jnp.where(odd, kept[c], last) + outside * face
            kept_ref[c, at, :] = jnp.where(odd, last, kept[c])
    near, _, ratio, _ = outer_rows(line)
    ratios = [spread(line, RATIO * ROWS + r, HALF_PAD) for r in INNER] + [ratio]
    filter_rows_into(out_ref, INNER + (near,), ratios, merid_ref, listed_ref, sine_ref[...], tables)


def edge_kernel(
    table_ref, listed_ref, kept_ref, rim_ref, swap_ref, first_ref, forward_ref, backward_ref, last_ref,
    twist_cos_ref, twist_sin_ref, sine_ref, partial_ref, out_ref, merid_ref,
):
    del partial_ref
    line = latitude_line(table_ref)
    odd = lax.rem(lax.axis_index("lon"), 2) == 1
    tables = (first_ref[...], forward_ref[...], backward_ref[...], last_ref[...], twist_cos_ref[...], twist_sin_ref[...])
    outside = jnp.where(odd, -spread(line, NORTH * ROWS + ROWS - 1), spread(line, SOUTH * ROWS))
    for t in range(TILES):
        at = slice(t * SECTORS, (t + 1) * SECTORS)
        courant = jnp.where(odd, rim_ref[1, COMP, at, :], swap_ref[COMP, at, :])
        for c in range(COMP):
            other = swap_ref[c, at, :]
            face = through_face(
                courant, jnp.where(odd, rim_ref[1, c, at, :], other), jnp.where(odd, other, rim_ref[0, c, at, :])
            )
            merid_ref[c, 0, at, :] = kept_ref[c, at, :] + outside * face
    _, far, _, ratio = outer_rows(line)
    filter_rows_into(out_ref, (far,), [ratio], merid_ref, listed_ref, sine_ref[...], tables)


def on_device(fields, zonal_fraction, merid_courant, hop_counts, filter_rows):
    vmem = pl.BlockSpec(memory_space=pltpu.VMEM)
    params = pltpu.CompilerParams(vmem_limit_bytes=VMEM_LIMIT)
    hops = hop_counts.reshape(1, BAND)
    stacked = jnp.concatenate([fields[:, 0], zonal_fraction, merid_courant], axis=0)
    outgoing = stacked.reshape(ARRAYS, SECTORS, ROWS, TILES, LANES).transpose(1, 0, 3, 2, 4)
    outgoing = outgoing.reshape(SECTORS, ARRAYS * TILES * ROWS, LANES)
    incoming = lax.all_to_all(outgoing, "lon", 0, 0, tiled=True, axis_index_groups=[list(ORDER)])
    incoming = incoming.reshape(SECTORS * ARRAYS * TILES * ROWS, LANES)
    f32 = jnp.float32
    edge_shape = jax.ShapeDtypeStruct((COMP + 1, OUTER, LANES), f32)
    rim, near, far = pl.pallas_call(
        rim_kernel,
        out_shape=(jax.ShapeDtypeStruct((2, COMP + 1, OUTER, LANES), f32), edge_shape, edge_shape),
        in_specs=[vmem, vmem],
        out_specs=(vmem, vmem, vmem),
        compiler_params=params,
    )(hops, incoming)
    bands = NLAT // BAND
    total = bands * SECTORS

    def device_of(block):
        return ORDER[block % SECTORS] * bands + block // SECTORS

    def swap(value, first_block):
        pairs = [(device_of(i), device_of(i + 1)) for i in range(first_block, total - 1, 2)]
        return lax.ppermute(value, ("lon", "lat"), pairs + [(j, i) for i, j in pairs])

    swapped = swap(near, 0)
    swapped_far = swap(far, 1)
    first, forward, backward, last, twist_cos, twist_sin, sine_sq = [jnp.asarray(v) for v in filter_tables()]
    latitudes = jnp.asarray(latitude_table())
    listed = filter_rows.reshape(4, LANES)
    out_shape = jax.ShapeDtypeStruct((SECTORS * COMP * TILES * ROWS, LANES), f32)
    constants = (first, forward, backward, last, twist_cos, twist_sin, sine_sq)
    partial, kept = pl.pallas_call(
        interior_kernel,
        out_shape=(out_shape, jax.ShapeDtypeStruct((COMP, OUTER, LANES), f32)),
        in_specs=[vmem] * 13,
        out_specs=(vmem, vmem),
        scratch_shapes=[
            pltpu.VMEM((COMP, ROWS, OUTER, LANES), f32),
            pltpu.VMEM((COMP, len(INNER) + 1, OUTER, LANES), f32),
        ],
        compiler_params=params,
        cost_estimate=pl.CostEstimate(flops=5_000_000_000, bytes_accessed=8_000_000, transcendentals=0),
    )(hops, latitudes, listed, incoming, rim, swapped, *constants)
    returning = pl.pallas_call(
        edge_kernel,
        out_shape=out_shape,
        in_specs=[vmem] * 13,
        out_specs=vmem,
        input_output_aliases={12: 0},
        scratch_shapes=[pltpu.VMEM((COMP, 1, OUTER, LANES), f32)],
        compiler_params=params,
        cost_estimate=pl.CostEstimate(flops=1_000_000_000, bytes_accessed=4_000_000, transcendentals=0),
    )(latitudes, listed, kept, rim, swapped_far, *constants, partial)
    arrived = lax.all_to_all(
        returning.reshape(SECTORS, COMP * TILES * ROWS, LANES), "lon", 0, 0, tiled=True, axis_index_groups=[list(ORDER)]
    )
    arrived = arrived.reshape(SECTORS, COMP, TILES, ROWS, LANES).transpose(1, 0, 3, 2, 4)
    return arrived.reshape(COMP, 1, BAND, TILES * LANES)


def solution(mesh):
    in_specs = (
        P(None, None, "lat", "lon"),
        P(None, "lat", "lon"),
        P(None, "lat", "lon"),
        P("lat"),
        P(),
    )
    out_specs = P(None, None, "lat", "lon")
    return jax.shard_map(
        on_device, mesh=mesh, in_specs=in_specs, out_specs=out_specs, check_vma=False
    )
```

```python
import functools
import math

import jax
import jax.numpy as jnp
import ml_dtypes
import numpy as np
from jax import lax
from jax.experimental import pallas as pl
from jax.experimental.pallas import tpu as pltpu
from jax.sharding import PartitionSpec as P

NLON = 12288
NLAT = 2048
SECTORS = 16
BAND = 128
ROWS = 8
TILES = 6
LANES = 128
OUTER = SECTORS * TILES
COMP = 3
ARRAYS = COMP + 2
HALF = OUTER // 2 + 1
HALF_PAD = 56
START_Y, STEP_Y, START_X = 2, 1, 1
ORDER = tuple(
    4 * ((START_Y + STEP_Y * (step if side == 0 else 3 - step)) % 4) + 2 * (START_X ^ side) + core
    for side in (0, 1)
    for step in range(4)
    for core in (0, 1)
)
INNER = (1, 2, 3, 4, 5, 6)
VMEM_LIMIT = 48 * 1024 * 1024

cos_cutoff = 0.7071067811865476


def split_bf16(table):
    high = table.astype(np.float32).astype(ml_dtypes.bfloat16)
    low = (table - high.astype(np.float64)).astype(np.float32).astype(ml_dtypes.bfloat16)
    return high, low


def filter_tables():
    at = np.arange(OUTER)
    a = TILES * np.asarray(ORDER)[at % SECTORS] + at // SECTORS
    c = np.arange(HALF_PAD)
    valid = (c < HALF)[:, None]
    angle = 2.0 * np.pi * ((c[:, None] * a[None, :]) % OUTER) / OUTER
    first = np.concatenate([np.where(valid, np.cos(angle), 0.0), np.where(valid, -np.sin(angle), 0.0)], axis=0)
    weight = np.where((c == 0) | (c == OUTER // 2), 1.0, 2.0) / NLON
    inner_only = (c > 0) & (c < OUTER // 2)
    last = np.concatenate(
        [
            np.where(valid, np.cos(angle) * weight[:, None], 0.0),
            np.where(valid & inner_only[:, None], -np.sin(angle) * weight[:, None], 0.0),
        ],
        axis=0,
    ).T
    b = np.arange(LANES)
    twist = 2.0 * np.pi * (c[:, None] * b[None, :]) / NLON
    inner = 2.0 * np.pi * ((b[:, None] * b[None, :]) % LANES) / LANES
    cos_in, sin_in = np.cos(inner), np.sin(inner)
    forward = np.block([[cos_in, -sin_in], [sin_in, cos_in]])
    backward = np.block([[cos_in, sin_in], [-sin_in, cos_in]])
    sine = np.sin(np.pi * (c[:, None] + OUTER * b[None, :]) / NLON)
    first_h, first_l = split_bf16(first)
    last_h, last_l = split_bf16(last)
    forward_h, forward_l = split_bf16(forward)
    backward_h, backward_l = split_bf16(backward)
    return (
        np.concatenate([first_h, first_h, first_l], axis=1),
        np.concatenate([forward_h, forward_h, forward_l], axis=0),
        np.concatenate([backward_h, backward_h, backward_l], axis=0),
        np.concatenate([last_h, last_h, last_l], axis=1),
        np.cos(twist).astype(np.float32),
        np.sin(twist).astype(np.float32),
        (sine * sine).astype(np.float32),
    )


NORTH, SOUTH, RATIO = range(3)


def latitude_table():
    row = np.arange(NLAT, dtype=np.float32)
    step = np.float32(math.pi / NLAT)
    center = np.sin(((row + np.float32(0.5)) * step).astype(np.float64))
    north = np.sin(((row + np.float32(1.0)) * step).astype(np.float64))
    north[-1] = 0.0
    south = np.concatenate([np.zeros(1), north[:-1]])
    ratio = center / cos_cutoff
    kinds = [v.reshape(NLAT // ROWS, ROWS) for v in (north / center, south / center, ratio * ratio)]
    return np.pad(np.concatenate(kinds, axis=1), ((0, 0), (0, LANES - 3 * ROWS))).astype(np.float32)


def latitude_line(table_ref):
    block = lax.axis_index("lat") * SECTORS + place_of(lax.axis_index("lon"))
    return table_ref[pl.ds(block, 1), :]


def spread(line, lane, rows=SECTORS):
    return jnp.broadcast_to(line[:, lane : lane + 1], (rows, LANES))


def own_hops(hop_ref):
    start = place_of(lax.axis_index("lon")) * ROWS
    line = pltpu.roll(jnp.broadcast_to(hop_ref[...], (8, LANES)), lax.rem(LANES - start, LANES), 1)[:1]
    return [spread(line, r) for r in range(ROWS)]


def halves(value):
    high = value.astype(jnp.bfloat16)
    low = (value - high.astype(jnp.float32)).astype(jnp.bfloat16)
    return high, low


def place_of(sector):
    step = lax.bitwise_and(STEP_Y * (lax.shift_right_logical(sector, 2) - START_Y), 3)
    core = lax.bitwise_and(sector, 1)
    return jnp.where(lax.bitwise_and(sector, 2) == 2 * START_X, 2 * step + core, 14 - 2 * step + core)


def sector_at(place):
    at, core = lax.shift_right_logical(lax.bitwise_and(place, 7), 1), lax.bitwise_and(place, 1)
    y = lax.bitwise_and(START_Y + STEP_Y * jnp.where(place < 8, at, 3 - at), 3)
    return 4 * y + jnp.where(place < 8, 2 * START_X, 2 - 2 * START_X) + core


def first_row():
    return lax.axis_index("lat") * BAND + place_of(lax.axis_index("lon")) * ROWS


def from_sector(tile, source):
    low, high = tile[:8], tile[8:]
    parts = []
    for at in (slice(0, 8), slice(8, 16)):
        index = lax.bitwise_and(source[at], 7)
        parts.append(
            jnp.where(
                source[at] < 8,
                jnp.take_along_axis(low, index, axis=0, mode="promise_in_bounds"),
                jnp.take_along_axis(high, index, axis=0, mode="promise_in_bounds"),
            )
        )
    return jnp.concatenate(parts, axis=0)


def fetch(in_ref, array, t, r):
    return in_ref[pl.ds((array * TILES + t) * ROWS + r, SECTORS, stride=ARRAYS * TILES * ROWS), :]


def zonal_row(in_ref, hop, r, store):
    lane = lax.broadcasted_iota(jnp.int32, (SECTORS, LANES), 1)
    own_sector = sector_at(lax.broadcasted_iota(jnp.int32, (SECTORS, LANES), 0))

    def source(hops):
        return place_of(lax.bitwise_and(own_sector - hops + SECTORS, SECTORS - 1))

    sources, sources_before, sources_after = source(hop), source(hop + 1), source(hop - 1)
    weights = []
    for t in range(TILES):
        offset = 1.0 - fetch(in_ref, COMP, t, r)
        w_far = -offset * (offset - 1.0) * (offset - 2.0) * (1.0 / 6.0)
        w_near = (offset + 1.0) * (offset - 1.0) * (offset - 2.0) * 0.5
        w_next = -(offset + 1.0) * offset * (offset - 2.0) * 0.5
        w_last = (offset + 1.0) * offset * (offset - 1.0) * (1.0 / 6.0)
        weights.append((w_far, w_near, w_next, w_last))
    for c in range(COMP):
        raw = [fetch(in_ref, c, t, r) for t in range(TILES)]
        here = [from_sector(v, sources) for v in raw]
        before = from_sector(raw[TILES - 1], sources_before)
        after = from_sector(raw[0], sources_after)
        back_one = [pltpu.roll(v, 1, 1) for v in [before] + here]
        back_two = [pltpu.roll(v, 2, 1) for v in [before] + here]
        ahead = [pltpu.roll(v, LANES - 1, 1) for v in here + [after]]
        for t in range(TILES):
            w_far, w_near, w_next, w_last = weights[t]
            store(
                c,
                slice(t * SECTORS, (t + 1) * SECTORS),
                w_far * jnp.where(lane < 2, back_two[t], back_two[t + 1])
                + w_near * jnp.where(lane < 1, back_one[t], back_one[t + 1])
                + w_next * here[t]
                + w_last * jnp.where(lane == LANES - 1, ahead[t + 1], ahead[t]),
            )


def rim_kernel(hop_ref, in_ref, rim_ref, near_ref, far_ref):
    hops = own_hops(hop_ref)
    odd = lax.rem(lax.axis_index("lon"), 2) == 1
    rows = []
    for at, r in enumerate((0, ROWS - 1)):
        values = {}

        def store(c, block, value):
            values[c, block.start] = value

        zonal_row(in_ref, hops[r], r, store)
        for t in range(TILES):
            values[COMP, t * SECTORS] = fetch(in_ref, COMP + 1, t, r)
        for (c, place), value in values.items():
            rim_ref[at, c, place : place + SECTORS, :] = value
        rows.append(values)
    for c, place in rows[0]:
        first, last = rows[0][c, place], rows[1][c, place]
        near_ref[c, place : place + SECTORS, :] = jnp.where(odd, first, last)
        far_ref[c, place : place + SECTORS, :] = jnp.where(odd, last, first)


def filter_group(slabs, damping, tables):
    first, forward, backward, last, twist_cos, twist_sin = tables
    count = len(slabs)
    high, low = halves(jnp.concatenate(slabs, axis=1))
    spectrum = jnp.dot(first, jnp.concatenate([high, low, high], axis=0), preferred_element_type=jnp.float32)
    parts = []
    for k in range(count):
        real = spectrum[:HALF_PAD, k * LANES : (k + 1) * LANES]
        imag = spectrum[HALF_PAD:, k * LANES : (k + 1) * LANES]
        parts.append(
            jnp.concatenate([real * twist_cos + imag * twist_sin, imag * twist_cos - real * twist_sin], axis=1)
        )
    high, low = halves(jnp.concatenate(parts, axis=0))
    spectrum = jnp.dot(jnp.concatenate([high, low, high], axis=1), forward, preferred_element_type=jnp.float32)
    parts = []
    for k in range(count):
        rows = spectrum[k * HALF_PAD : (k + 1) * HALF_PAD]
        parts.append(rows * jnp.concatenate([damping[k], damping[k]], axis=1))
    high, low = halves(jnp.concatenate(parts, axis=0))
    spectrum = jnp.dot(jnp.concatenate([high, low, high], axis=1), backward, preferred_element_type=jnp.float32)
    parts = []
    for k in range(count):
        real = spectrum[k * HALF_PAD : (k + 1) * HALF_PAD, :LANES]
        imag = spectrum[k * HALF_PAD : (k + 1) * HALF_PAD, LANES:]
        parts.append(
            jnp.concatenate([real * twist_cos - imag * twist_sin, imag * twist_cos + real * twist_sin], axis=0)
        )
    high, low = halves(jnp.concatenate(parts, axis=1))
    rebuilt = jnp.dot(last, jnp.concatenate([high, low, high], axis=0), preferred_element_type=jnp.float32)
    return [rebuilt[:, k * LANES : (k + 1) * LANES] for k in range(count)]


def listed_mask(listed_ref, row):
    hit = jnp.where(listed_ref[...] == row, 1.0, 0.0)
    hit = jnp.max(jnp.max(hit, axis=1, keepdims=True), axis=0, keepdims=True)
    return jnp.broadcast_to(hit, (SECTORS, LANES)) > 0.5


def filter_rows_into(out_ref, rows, ratios, merid_ref, listed_ref, sine_sq, tables):
    start = first_row()
    damping = []
    for ratio_sq in ratios:
        damping.extend([ratio_sq / jnp.maximum(ratio_sq, sine_sq)] * COMP)
    slabs = [merid_ref[c, i] for i in range(len(rows)) for c in range(COMP)]
    filtered = filter_group(slabs, damping, tables)
    for i, row in enumerate(rows):
        listed = listed_mask(listed_ref, start + row)
        for c in range(COMP):
            value = filtered[i * COMP + c]
            for t in range(TILES):
                block = slice(t * SECTORS, (t + 1) * SECTORS)
                out_ref[pl.ds((c * TILES + t) * ROWS + row, SECTORS, stride=COMP * TILES * ROWS), :] = jnp.where(
                    listed, value[block], merid_ref[c, i, block, :]
                )


def through_face(courant, own, above):
    return jnp.maximum(courant, 0.0) * own + jnp.minimum(courant, 0.0) * above


def outer_rows(line):
    odd = lax.rem(lax.axis_index("lon"), 2) == 1
    first, last = spread(line, RATIO * ROWS, HALF_PAD), spread(line, RATIO * ROWS + ROWS - 1, HALF_PAD)
    near, far = jnp.where(odd, 0, ROWS - 1), jnp.where(odd, ROWS - 1, 0)
    return near, far, jnp.where(odd, first, last), jnp.where(odd, last, first)


def interior_kernel(
    hop_ref, table_ref, listed_ref, in_ref, rim_ref, swap_ref, first_ref, forward_ref, backward_ref, last_ref,
    twist_cos_ref, twist_sin_ref, sine_ref, out_ref, kept_ref, zonal_ref, merid_ref,
):
    line = latitude_line(table_ref)
    hops = own_hops(hop_ref)
    odd = lax.rem(lax.axis_index("lon"), 2) == 1
    tables = (first_ref[...], forward_ref[...], backward_ref[...], last_ref[...], twist_cos_ref[...], twist_sin_ref[...])
    for r in INNER:

        def store(c, at, value):
            zonal_ref[c, r, at, :] = value

        zonal_row(in_ref, hops[r], r, store)
    north = [spread(line, NORTH * ROWS + r) for r in range(ROWS)]
    south = [spread(line, SOUTH * ROWS + r) for r in range(ROWS)]
    outside = jnp.where(odd, south[0], -north[ROWS - 1])
    for t in range(TILES):
        at = slice(t * SECTORS, (t + 1) * SECTORS)
        first_row_of = own = [rim_ref[0, c, at, :] for c in range(COMP)]
        last_row_of = [rim_ref[1, c, at, :] for c in range(COMP)]
        before = None
        kept = []
        for r in range(ROWS - 1):
            courant = fetch(in_ref, COMP + 1, t, r)
            above = last_row_of if r == ROWS - 2 else [zonal_ref[c, r + 1, at, :] for c in range(COMP)]
            face = [through_face(courant, own[c], above[c]) for c in range(COMP)]
            for c in range(COMP):
                merid = own[c] - north[r] * face[c]
                if r == 0:
                    kept.append(merid)
                else:
                    merid_ref[c, r - 1, at, :] = merid + south[r] * before[c]
            own, before = above, face
        courant = jnp.where(odd, swap_ref[COMP, at, :], rim_ref[1, COMP, at, :])
        for c in range(COMP):
            last = last_row_of[c] + south[ROWS - 1] * before[c]
            other = swap_ref[c, at, :]
            face = through_face(
                courant, jnp.where(odd, other, last_row_of[c]), jnp.where(odd, first_row_of[c], other)
            )
            merid_ref[c, len(INNER), at, :] = jnp.where(odd, kept[c], last) + outside * face
            kept_ref[c, at, :] = jnp.where(odd, last, kept[c])
    near, _, ratio, _ = outer_rows(line)
    ratios = [spread(line, RATIO * ROWS + r, HALF_PAD) for r in INNER] + [ratio]
    filter_rows_into(out_ref, INNER + (near,), ratios, merid_ref, listed_ref, sine_ref[...], tables)


def edge_kernel(
    table_ref, listed_ref, kept_ref, rim_ref, swap_ref, first_ref, forward_ref, backward_ref, last_ref,
    twist_cos_ref, twist_sin_ref, sine_ref, partial_ref, out_ref, merid_ref,
):
    del partial_ref
    line = latitude_line(table_ref)
    odd = lax.rem(lax.axis_index("lon"), 2) == 1
    tables = (first_ref[...], forward_ref[...], backward_ref[...], last_ref[...], twist_cos_ref[...], twist_sin_ref[...])
    outside = jnp.where(odd, -spread(line, NORTH * ROWS + ROWS - 1), spread(line, SOUTH * ROWS))
    for t in range(TILES):
        at = slice(t * SECTORS, (t + 1) * SECTORS)
        courant = jnp.where(odd, rim_ref[1, COMP, at, :], swap_ref[COMP, at, :])
        for c in range(COMP):
            other = swap_ref[c, at, :]
            face = through_face(
                courant, jnp.where(odd, rim_ref[1, c, at, :], other), jnp.where(odd, other, rim_ref[0, c, at, :])
            )
            merid_ref[c, 0, at, :] = kept_ref[c, at, :] + outside * face
    _, far, _, ratio = outer_rows(line)
    filter_rows_into(out_ref, (far,), [ratio], merid_ref, listed_ref, sine_ref[...], tables)


def on_device(fields, zonal_fraction, merid_courant, hop_counts, filter_rows):
    vmem = pl.BlockSpec(memory_space=pltpu.VMEM)
    params = pltpu.CompilerParams(vmem_limit_bytes=VMEM_LIMIT)
    hops = hop_counts.reshape(1, BAND)
    stacked = jnp.concatenate([fields[:, 0], zonal_fraction, merid_courant], axis=0)
    outgoing = stacked.reshape(ARRAYS, SECTORS, ROWS, TILES, LANES).transpose(1, 0, 3, 2, 4)
    outgoing = outgoing.reshape(SECTORS, ARRAYS * TILES * ROWS, LANES)
    incoming = lax.all_to_all(outgoing, "lon", 0, 0, tiled=True, axis_index_groups=[list(ORDER)])
    incoming = incoming.reshape(SECTORS * ARRAYS * TILES * ROWS, LANES)
    f32 = jnp.float32
    edge_shape = jax.ShapeDtypeStruct((COMP + 1, OUTER, LANES), f32)
    rim, near, far = pl.pallas_call(
        rim_kernel,
        out_shape=(jax.ShapeDtypeStruct((2, COMP + 1, OUTER, LANES), f32), edge_shape, edge_shape),
        in_specs=[vmem, vmem],
        out_specs=(vmem, vmem, vmem),
        compiler_params=params,
    )(hops, incoming)
    bands = NLAT // BAND
    total = bands * SECTORS

    def device_of(block):
        return ORDER[block % SECTORS] * bands + block // SECTORS

    def swap(value, first_block):
        pairs = [(device_of(i), device_of(i + 1)) for i in range(first_block, total - 1, 2)]
        return lax.ppermute(value, ("lon", "lat"), pairs + [(j, i) for i, j in pairs])

    swapped = swap(near, 0)
    swapped_far = swap(far, 1)
    first, forward, backward, last, twist_cos, twist_sin, sine_sq = [jnp.asarray(v) for v in filter_tables()]
    latitudes = jnp.asarray(latitude_table())
    listed = filter_rows.reshape(4, LANES)
    out_shape = jax.ShapeDtypeStruct((SECTORS * COMP * TILES * ROWS, LANES), f32)
    constants = (first, forward, backward, last, twist_cos, twist_sin, sine_sq)
    partial, kept = pl.pallas_call(
        interior_kernel,
        out_shape=(out_shape, jax.ShapeDtypeStruct((COMP, OUTER, LANES), f32)),
        in_specs=[vmem] * 13,
        out_specs=(vmem, vmem),
        scratch_shapes=[
            pltpu.VMEM((COMP, ROWS, OUTER, LANES), f32),
            pltpu.VMEM((COMP, len(INNER) + 1, OUTER, LANES), f32),
        ],
        compiler_params=params,
        cost_estimate=pl.CostEstimate(flops=5_000_000_000, bytes_accessed=8_000_000, transcendentals=0),
    )(hops, latitudes, listed, incoming, rim, swapped, *constants)
    returning = pl.pallas_call(
        edge_kernel,
        out_shape=out_shape,
        in_specs=[vmem] * 13,
        out_specs=vmem,
        input_output_aliases={12: 0},
        scratch_shapes=[pltpu.VMEM((COMP, 1, OUTER, LANES), f32)],
        compiler_params=params,
        cost_estimate=pl.CostEstimate(flops=1_000_000_000, bytes_accessed=4_000_000, transcendentals=0),
    )(latitudes, listed, kept, rim, swapped_far, *constants, partial)
    arrived = lax.all_to_all(
        returning.reshape(SECTORS, COMP * TILES * ROWS, LANES), "lon", 0, 0, tiled=True, axis_index_groups=[list(ORDER)]
    )
    arrived = arrived.reshape(SECTORS, COMP, TILES, ROWS, LANES).transpose(1, 0, 3, 2, 4)
    return arrived.reshape(COMP, 1, BAND, TILES * LANES)


def solution(mesh):
    in_specs = (
        P(None, None, "lat", "lon"),
        P(None, "lat", "lon"),
        P(None, "lat", "lon"),
        P("lat"),
        P(),
    )
    out_specs = P(None, None, "lat", "lon")
    return jax.shard_map(
        on_device, mesh=mesh, in_specs=in_specs, out_specs=out_specs, check_vma=False
    )
```

```python
import functools
import math

import jax
import jax.numpy as jnp
import ml_dtypes
import numpy as np
from jax import lax
from jax.experimental import pallas as pl
from jax.experimental.pallas import tpu as pltpu
from jax.sharding import PartitionSpec as P

NLON = 12288
NLAT = 2048
SECTORS = 16
BAND = 128
ROWS = 8
TILES = 6
LANES = 128
OUTER = SECTORS * TILES
COMP = 3
ARRAYS = COMP + 2
HALF = OUTER // 2 + 1
HALF_PAD = 56
START_Y, STEP_Y, START_X = 2, 1, 1
FIRST_CORE = (1, 1)
ORDER = tuple(
    4 * ((START_Y + STEP_Y * (step if side == 0 else 3 - step)) % 4) + 2 * (START_X ^ side) + (FIRST_CORE[side] ^ core)
    for side in (0, 1)
    for step in range(4)
    for core in (0, 1)
)
INNER = (1, 2, 3, 4, 5, 6)
VMEM_LIMIT = 48 * 1024 * 1024

cos_cutoff = 0.7071067811865476


def split_bf16(table):
    high = table.astype(np.float32).astype(ml_dtypes.bfloat16)
    low = (table - high.astype(np.float64)).astype(np.float32).astype(ml_dtypes.bfloat16)
    return high, low


def filter_tables():
    at = np.arange(OUTER)
    a = TILES * np.asarray(ORDER)[at % SECTORS] + at // SECTORS
    c = np.arange(HALF_PAD)
    valid = (c < HALF)[:, None]
    angle = 2.0 * np.pi * ((c[:, None] * a[None, :]) % OUTER) / OUTER
    first = np.concatenate([np.where(valid, np.cos(angle), 0.0), np.where(valid, -np.sin(angle), 0.0)], axis=0)
    weight = np.where((c == 0) | (c == OUTER // 2), 1.0, 2.0) / NLON
    inner_only = (c > 0) & (c < OUTER // 2)
    last = np.concatenate(
        [
            np.where(valid, np.cos(angle) * weight[:, None], 0.0),
            np.where(valid & inner_only[:, None], -np.sin(angle) * weight[:, None], 0.0),
        ],
        axis=0,
    ).T
    b = np.arange(LANES)
    twist = 2.0 * np.pi * (c[:, None] * b[None, :]) / NLON
    inner = 2.0 * np.pi * ((b[:, None] * b[None, :]) % LANES) / LANES
    cos_in, sin_in = np.cos(inner), np.sin(inner)
    forward = np.block([[cos_in, -sin_in], [sin_in, cos_in]])
    backward = np.block([[cos_in, sin_in], [-sin_in, cos_in]])
    sine = np.sin(np.pi * (c[:, None] + OUTER * b[None, :]) / NLON)
    first_h, first_l = split_bf16(first)
    last_h, last_l = split_bf16(last)
    forward_h, forward_l = split_bf16(forward)
    backward_h, backward_l = split_bf16(backward)
    return (
        np.concatenate([first_h, first_h, first_l], axis=1),
        np.concatenate([forward_h, forward_h, forward_l], axis=0),
        np.concatenate([backward_h, backward_h, backward_l], axis=0),
        np.concatenate([last_h, last_h, last_l], axis=1),
        np.cos(twist).astype(np.float32),
        np.sin(twist).astype(np.float32),
        (sine * sine).astype(np.float32),
    )


NORTH, SOUTH, RATIO = range(3)


def latitude_table():
    row = np.arange(NLAT, dtype=np.float32)
    step = np.float32(math.pi / NLAT)
    center = np.sin(((row + np.float32(0.5)) * step).astype(np.float64))
    north = np.sin(((row + np.float32(1.0)) * step).astype(np.float64))
    north[-1] = 0.0
    south = np.concatenate([np.zeros(1), north[:-1]])
    ratio = center / cos_cutoff
    kinds = [v.reshape(NLAT // ROWS, ROWS) for v in (north / center, south / center, ratio * ratio)]
    return np.pad(np.concatenate(kinds, axis=1), ((0, 0), (0, LANES - 3 * ROWS))).astype(np.float32)


def latitude_line(table_ref):
    block = lax.axis_index("lat") * SECTORS + place_of(lax.axis_index("lon"))
    return table_ref[pl.ds(block, 1), :]


def spread(line, lane, rows=SECTORS):
    return jnp.broadcast_to(line[:, lane : lane + 1], (rows, LANES))


def own_hops(hop_ref):
    start = place_of(lax.axis_index("lon")) * ROWS
    line = pltpu.roll(jnp.broadcast_to(hop_ref[...], (8, LANES)), lax.rem(LANES - start, LANES), 1)[:1]
    return [spread(line, r) for r in range(ROWS)]


def halves(value):
    high = value.astype(jnp.bfloat16)
    low = (value - high.astype(jnp.float32)).astype(jnp.bfloat16)
    return high, low


def place_of(sector):
    step = 2 * lax.bitwise_and(STEP_Y * (lax.shift_right_logical(sector, 2) - START_Y), 3)
    core = lax.bitwise_and(sector, 1)
    first_side = lax.bitwise_and(sector, 2) == 2 * START_X
    return jnp.where(
        first_side, step + lax.bitwise_xor(core, FIRST_CORE[0]), 14 - step + lax.bitwise_xor(core, FIRST_CORE[1])
    )


def sector_at(place):
    at, core = lax.shift_right_logical(lax.bitwise_and(place, 7), 1), lax.bitwise_and(place, 1)
    y = lax.bitwise_and(START_Y + STEP_Y * jnp.where(place < 8, at, 3 - at), 3)
    return 4 * y + jnp.where(
        place < 8,
        2 * START_X + lax.bitwise_xor(core, FIRST_CORE[0]),
        2 - 2 * START_X + lax.bitwise_xor(core, FIRST_CORE[1]),
    )


def first_row():
    return lax.axis_index("lat") * BAND + place_of(lax.axis_index("lon")) * ROWS


def from_sector(tile, source):
    low, high = tile[:8], tile[8:]
    parts = []
    for at in (slice(0, 8), slice(8, 16)):
        index = lax.bitwise_and(source[at], 7)
        parts.append(
            jnp.where(
                source[at] < 8,
                jnp.take_along_axis(low, index, axis=0, mode="promise_in_bounds"),
                jnp.take_along_axis(high, index, axis=0, mode="promise_in_bounds"),
            )
        )
    return jnp.concatenate(parts, axis=0)


def fetch(in_ref, array, t, r):
    return in_ref[pl.ds((array * TILES + t) * ROWS + r, SECTORS, stride=ARRAYS * TILES * ROWS), :]


def zonal_row(in_ref, hop, r, store):
    lane = lax.broadcasted_iota(jnp.int32, (SECTORS, LANES), 1)
    own_sector = sector_at(lax.broadcasted_iota(jnp.int32, (SECTORS, LANES), 0))

    def source(hops):
        return place_of(lax.bitwise_and(own_sector - hops + SECTORS, SECTORS - 1))

    sources, sources_before, sources_after = source(hop), source(hop + 1), source(hop - 1)
    weights = []
    for t in range(TILES):
        offset = 1.0 - fetch(in_ref, COMP, t, r)
        w_far = -offset * (offset - 1.0) * (offset - 2.0) * (1.0 / 6.0)
        w_near = (offset + 1.0) * (offset - 1.0) * (offset - 2.0) * 0.5
        w_next = -(offset + 1.0) * offset * (offset - 2.0) * 0.5
        w_last = (offset + 1.0) * offset * (offset - 1.0) * (1.0 / 6.0)
        weights.append((w_far, w_near, w_next, w_last))
    for c in range(COMP):
        raw = [fetch(in_ref, c, t, r) for t in range(TILES)]
        here = [from_sector(v, sources) for v in raw]
        before = from_sector(raw[TILES - 1], sources_before)
        after = from_sector(raw[0], sources_after)
        back_one = [pltpu.roll(v, 1, 1) for v in [before] + here]
        back_two = [pltpu.roll(v, 2, 1) for v in [before] + here]
        ahead = [pltpu.roll(v, LANES - 1, 1) for v in here + [after]]
        for t in range(TILES):
            w_far, w_near, w_next, w_last = weights[t]
            store(
                c,
                slice(t * SECTORS, (t + 1) * SECTORS),
                w_far * jnp.where(lane < 2, back_two[t], back_two[t + 1])
                + w_near * jnp.where(lane < 1, back_one[t], back_one[t + 1])
                + w_next * here[t]
                + w_last * jnp.where(lane == LANES - 1, ahead[t + 1], ahead[t]),
            )


def rim_kernel(hop_ref, in_ref, rim_ref, near_ref, far_ref):
    hops = own_hops(hop_ref)
    odd = lax.bitwise_and(place_of(lax.axis_index("lon")), 1) == 1
    rows = []
    for at, r in enumerate((0, ROWS - 1)):
        values = {}

        def store(c, block, value):
            values[c, block.start] = value

        zonal_row(in_ref, hops[r], r, store)
        for t in range(TILES):
            values[COMP, t * SECTORS] = fetch(in_ref, COMP + 1, t, r)
        for (c, place), value in values.items():
            rim_ref[at, c, place : place + SECTORS, :] = value
        rows.append(values)
    for c, place in rows[0]:
        first, last = rows[0][c, place], rows[1][c, place]
        near_ref[c, place : place + SECTORS, :] = jnp.where(odd, first, last)
        far_ref[c, place : place + SECTORS, :] = jnp.where(odd, last, first)


def filter_group(slabs, damping, tables):
    first, forward, backward, last, twist_cos, twist_sin = tables
    count = len(slabs)
    high, low = halves(jnp.concatenate(slabs, axis=1))
    spectrum = jnp.dot(first, jnp.concatenate([high, low, high], axis=0), preferred_element_type=jnp.float32)
    parts = []
    for k in range(count):
        real = spectrum[:HALF_PAD, k * LANES : (k + 1) * LANES]
        imag = spectrum[HALF_PAD:, k * LANES : (k + 1) * LANES]
        parts.append(
            jnp.concatenate([real * twist_cos + imag * twist_sin, imag * twist_cos - real * twist_sin], axis=1)
        )
    high, low = halves(jnp.concatenate(parts, axis=0))
    spectrum = jnp.dot(jnp.concatenate([high, low, high], axis=1), forward, preferred_element_type=jnp.float32)
    parts = []
    for k in range(count):
        rows = spectrum[k * HALF_PAD : (k + 1) * HALF_PAD]
        parts.append(rows * jnp.concatenate([damping[k], damping[k]], axis=1))
    high, low = halves(jnp.concatenate(parts, axis=0))
    spectrum = jnp.dot(jnp.concatenate([high, low, high], axis=1), backward, preferred_element_type=jnp.float32)
    parts = []
    for k in range(count):
        real = spectrum[k * HALF_PAD : (k + 1) * HALF_PAD, :LANES]
        imag = spectrum[k * HALF_PAD : (k + 1) * HALF_PAD, LANES:]
        parts.append(
            jnp.concatenate([real * twist_cos - imag * twist_sin, imag * twist_cos + real * twist_sin], axis=0)
        )
    high, low = halves(jnp.concatenate(parts, axis=1))
    rebuilt = jnp.dot(last, jnp.concatenate([high, low, high], axis=0), preferred_element_type=jnp.float32)
    return [rebuilt[:, k * LANES : (k + 1) * LANES] for k in range(count)]


def listed_mask(listed_ref, row):
    hit = jnp.where(listed_ref[...] == row, 1.0, 0.0)
    hit = jnp.max(jnp.max(hit, axis=1, keepdims=True), axis=0, keepdims=True)
    return jnp.broadcast_to(hit, (SECTORS, LANES)) > 0.5


def filter_rows_into(out_ref, rows, ratios, merid_ref, listed_ref, sine_sq, tables):
    start = first_row()
    damping = []
    for ratio_sq in ratios:
        damping.extend([ratio_sq / jnp.maximum(ratio_sq, sine_sq)] * COMP)
    slabs = [merid_ref[c, i] for i in range(len(rows)) for c in range(COMP)]
    filtered = filter_group(slabs, damping, tables)
    for i, row in enumerate(rows):
        listed = listed_mask(listed_ref, start + row)
        for c in range(COMP):
            value = filtered[i * COMP + c]
            for t in range(TILES):
                block = slice(t * SECTORS, (t + 1) * SECTORS)
                out_ref[pl.ds((c * TILES + t) * ROWS + row, SECTORS, stride=COMP * TILES * ROWS), :] = jnp.where(
                    listed, value[block], merid_ref[c, i, block, :]
                )


def through_face(courant, own, above):
    return jnp.maximum(courant, 0.0) * own + jnp.minimum(courant, 0.0) * above


def outer_rows(line):
    odd = lax.bitwise_and(place_of(lax.axis_index("lon")), 1) == 1
    first, last = spread(line, RATIO * ROWS, HALF_PAD), spread(line, RATIO * ROWS + ROWS - 1, HALF_PAD)
    near, far = jnp.where(odd, 0, ROWS - 1), jnp.where(odd, ROWS - 1, 0)
    return near, far, jnp.where(odd, first, last), jnp.where(odd, last, first)


def interior_kernel(
    hop_ref, table_ref, listed_ref, in_ref, rim_ref, swap_ref, first_ref, forward_ref, backward_ref, last_ref,
    twist_cos_ref, twist_sin_ref, sine_ref, out_ref, kept_ref, zonal_ref, merid_ref,
):
    line = latitude_line(table_ref)
    hops = own_hops(hop_ref)
    odd = lax.bitwise_and(place_of(lax.axis_index("lon")), 1) == 1
    tables = (first_ref[...], forward_ref[...], backward_ref[...], last_ref[...], twist_cos_ref[...], twist_sin_ref[...])
    for r in INNER:

        def store(c, at, value):
            zonal_ref[c, r, at, :] = value

        zonal_row(in_ref, hops[r], r, store)
    north = [spread(line, NORTH * ROWS + r) for r in range(ROWS)]
    south = [spread(line, SOUTH * ROWS + r) for r in range(ROWS)]
    outside = jnp.where(odd, south[0], -north[ROWS - 1])
    for t in range(TILES):
        at = slice(t * SECTORS, (t + 1) * SECTORS)
        first_row_of = own = [rim_ref[0, c, at, :] for c in range(COMP)]
        last_row_of = [rim_ref[1, c, at, :] for c in range(COMP)]
        before = None
        kept = []
        for r in range(ROWS - 1):
            courant = fetch(in_ref, COMP + 1, t, r)
            above = last_row_of if r == ROWS - 2 else [zonal_ref[c, r + 1, at, :] for c in range(COMP)]
            face = [through_face(courant, own[c], above[c]) for c in range(COMP)]
            for c in range(COMP):
                merid = own[c] - north[r] * face[c]
                if r == 0:
                    kept.append(merid)
                else:
                    merid_ref[c, r - 1, at, :] = merid + south[r] * before[c]
            own, before = above, face
        courant = jnp.where(odd, swap_ref[COMP, at, :], rim_ref[1, COMP, at, :])
        for c in range(COMP):
            last = last_row_of[c] + south[ROWS - 1] * before[c]
            other = swap_ref[c, at, :]
            face = through_face(
                courant, jnp.where(odd, other, last_row_of[c]), jnp.where(odd, first_row_of[c], other)
            )
            merid_ref[c, len(INNER), at, :] = jnp.where(odd, kept[c], last) + outside * face
            kept_ref[c, at, :] = jnp.where(odd, last, kept[c])
    near, _, ratio, _ = outer_rows(line)
    ratios = [spread(line, RATIO * ROWS + r, HALF_PAD) for r in INNER] + [ratio]
    filter_rows_into(out_ref, INNER + (near,), ratios, merid_ref, listed_ref, sine_ref[...], tables)


def edge_kernel(
    table_ref, listed_ref, kept_ref, rim_ref, swap_ref, first_ref, forward_ref, backward_ref, last_ref,
    twist_cos_ref, twist_sin_ref, sine_ref, partial_ref, out_ref, merid_ref,
):
    del partial_ref
    line = latitude_line(table_ref)
    odd = lax.bitwise_and(place_of(lax.axis_index("lon")), 1) == 1
    tables = (first_ref[...], forward_ref[...], backward_ref[...], last_ref[...], twist_cos_ref[...], twist_sin_ref[...])
    outside = jnp.where(odd, -spread(line, NORTH * ROWS + ROWS - 1), spread(line, SOUTH * ROWS))
    for t in range(TILES):
        at = slice(t * SECTORS, (t + 1) * SECTORS)
        courant = jnp.where(odd, rim_ref[1, COMP, at, :], swap_ref[COMP, at, :])
        for c in range(COMP):
            other = swap_ref[c, at, :]
            face = through_face(
                courant, jnp.where(odd, rim_ref[1, c, at, :], other), jnp.where(odd, other, rim_ref[0, c, at, :])
            )
            merid_ref[c, 0, at, :] = kept_ref[c, at, :] + outside * face
    _, far, _, ratio = outer_rows(line)
    filter_rows_into(out_ref, (far,), [ratio], merid_ref, listed_ref, sine_ref[...], tables)


def on_device(fields, zonal_fraction, merid_courant, hop_counts, filter_rows):
    vmem = pl.BlockSpec(memory_space=pltpu.VMEM)
    params = pltpu.CompilerParams(vmem_limit_bytes=VMEM_LIMIT)
    hops = hop_counts.reshape(1, BAND)
    stacked = jnp.concatenate([fields[:, 0], zonal_fraction, merid_courant], axis=0)
    outgoing = stacked.reshape(ARRAYS, SECTORS, ROWS, TILES, LANES).transpose(1, 0, 3, 2, 4)
    outgoing = outgoing.reshape(SECTORS, ARRAYS * TILES * ROWS, LANES)
    incoming = lax.all_to_all(outgoing, "lon", 0, 0, tiled=True, axis_index_groups=[list(ORDER)])
    incoming = incoming.reshape(SECTORS * ARRAYS * TILES * ROWS, LANES)
    f32 = jnp.float32
    edge_shape = jax.ShapeDtypeStruct((COMP + 1, OUTER, LANES), f32)
    rim, near, far = pl.pallas_call(
        rim_kernel,
        out_shape=(jax.ShapeDtypeStruct((2, COMP + 1, OUTER, LANES), f32), edge_shape, edge_shape),
        in_specs=[vmem, vmem],
        out_specs=(vmem, vmem, vmem),
        compiler_params=params,
    )(hops, incoming)
    bands = NLAT // BAND
    total = bands * SECTORS

    def device_of(block):
        return ORDER[block % SECTORS] * bands + block // SECTORS

    def swap(value, first_block):
        pairs = [(device_of(i), device_of(i + 1)) for i in range(first_block, total - 1, 2)]
        return lax.ppermute(value, ("lon", "lat"), pairs + [(j, i) for i, j in pairs])

    swapped = swap(near, 0)
    swapped_far = swap(far, 1)
    first, forward, backward, last, twist_cos, twist_sin, sine_sq = [jnp.asarray(v) for v in filter_tables()]
    latitudes = jnp.asarray(latitude_table())
    listed = filter_rows.reshape(4, LANES)
    out_shape = jax.ShapeDtypeStruct((SECTORS * COMP * TILES * ROWS, LANES), f32)
    constants = (first, forward, backward, last, twist_cos, twist_sin, sine_sq)
    partial, kept = pl.pallas_call(
        interior_kernel,
        out_shape=(out_shape, jax.ShapeDtypeStruct((COMP, OUTER, LANES), f32)),
        in_specs=[vmem] * 13,
        out_specs=(vmem, vmem),
        scratch_shapes=[
            pltpu.VMEM((COMP, ROWS, OUTER, LANES), f32),
            pltpu.VMEM((COMP, len(INNER) + 1, OUTER, LANES), f32),
        ],
        compiler_params=params,
        cost_estimate=pl.CostEstimate(flops=5_000_000_000, bytes_accessed=8_000_000, transcendentals=0),
    )(hops, latitudes, listed, incoming, rim, swapped, *constants)
    returning = pl.pallas_call(
        edge_kernel,
        out_shape=out_shape,
        in_specs=[vmem] * 13,
        out_specs=vmem,
        input_output_aliases={12: 0},
        scratch_shapes=[pltpu.VMEM((COMP, 1, OUTER, LANES), f32)],
        compiler_params=params,
        cost_estimate=pl.CostEstimate(flops=1_000_000_000, bytes_accessed=4_000_000, transcendentals=0),
    )(latitudes, listed, kept, rim, swapped_far, *constants, partial)
    arrived = lax.all_to_all(
        returning.reshape(SECTORS, COMP * TILES * ROWS, LANES), "lon", 0, 0, tiled=True, axis_index_groups=[list(ORDER)]
    )
    arrived = arrived.reshape(SECTORS, COMP, TILES, ROWS, LANES).transpose(1, 0, 3, 2, 4)
    return arrived.reshape(COMP, 1, BAND, TILES * LANES)


def solution(mesh):
    in_specs = (
        P(None, None, "lat", "lon"),
        P(None, "lat", "lon"),
        P(None, "lat", "lon"),
        P("lat"),
        P(),
    )
    out_specs = P(None, None, "lat", "lon")
    return jax.shard_map(
        on_device, mesh=mesh, in_specs=in_specs, out_specs=out_specs, check_vma=False
    )
```

```python
import functools
import math

import jax
import jax.numpy as jnp
import ml_dtypes
import numpy as np
from jax import lax
from jax.experimental import pallas as pl
from jax.experimental.pallas import tpu as pltpu
from jax.sharding import PartitionSpec as P

NLON = 12288
NLAT = 2048
SECTORS = 16
BAND = 128
ROWS = 8
TILES = 6
LANES = 128
OUTER = SECTORS * TILES
COMP = 3
ARRAYS = COMP + 2
HALF = OUTER // 2 + 1
HALF_PAD = 56
START_Y, STEP_Y, START_X = 2, 1, 1
FIRST_CORE = (1, 1)
ORDER = tuple(
    4 * ((START_Y + STEP_Y * (step if side == 0 else 3 - step)) % 4) + 2 * (START_X ^ side) + (FIRST_CORE[side] ^ core)
    for side in (0, 1)
    for step in range(4)
    for core in (0, 1)
)
INNER = (1, 2, 3, 4, 5, 6)
VMEM_LIMIT = 48 * 1024 * 1024

cos_cutoff = 0.7071067811865476


def split_bf16(table):
    high = table.astype(np.float32).astype(ml_dtypes.bfloat16)
    low = (table - high.astype(np.float64)).astype(np.float32).astype(ml_dtypes.bfloat16)
    return high, low


def filter_tables():
    at = np.arange(OUTER)
    a = TILES * np.asarray(ORDER)[at % SECTORS] + at // SECTORS
    c = np.arange(HALF_PAD)
    valid = (c < HALF)[:, None]
    angle = 2.0 * np.pi * ((c[:, None] * a[None, :]) % OUTER) / OUTER
    first = np.concatenate([np.where(valid, np.cos(angle), 0.0), np.where(valid, -np.sin(angle), 0.0)], axis=0)
    weight = np.where((c == 0) | (c == OUTER // 2), 1.0, 2.0) / NLON
    inner_only = (c > 0) & (c < OUTER // 2)
    last = np.concatenate(
        [
            np.where(valid, np.cos(angle) * weight[:, None], 0.0),
            np.where(valid & inner_only[:, None], -np.sin(angle) * weight[:, None], 0.0),
        ],
        axis=0,
    ).T
    b = np.arange(LANES)
    twist = 2.0 * np.pi * (c[:, None] * b[None, :]) / NLON
    inner = 2.0 * np.pi * ((b[:, None] * b[None, :]) % LANES) / LANES
    cos_in, sin_in = np.cos(inner), np.sin(inner)
    forward = np.block([[cos_in, -sin_in], [sin_in, cos_in]])
    backward = np.block([[cos_in, sin_in], [-sin_in, cos_in]])
    sine = np.sin(np.pi * (c[:, None] + OUTER * b[None, :]) / NLON)
    first_h, first_l = split_bf16(first)
    last_h, last_l = split_bf16(last)
    forward_h, forward_l = split_bf16(forward)
    backward_h, backward_l = split_bf16(backward)
    return (
        np.concatenate([first_h, first_h, first_l], axis=1),
        np.concatenate([forward_h, forward_l], axis=0),
        np.concatenate([backward_h, backward_l], axis=0),
        np.concatenate([last_h, last_h, last_l], axis=1),
        np.cos(twist).astype(np.float32),
        np.sin(twist).astype(np.float32),
        (sine * sine).astype(np.float32),
    )


NORTH, SOUTH, RATIO = range(3)


def latitude_table():
    row = np.arange(NLAT, dtype=np.float32)
    step = np.float32(math.pi / NLAT)
    center = np.sin(((row + np.float32(0.5)) * step).astype(np.float64))
    north = np.sin(((row + np.float32(1.0)) * step).astype(np.float64))
    north[-1] = 0.0
    south = np.concatenate([np.zeros(1), north[:-1]])
    ratio = center / cos_cutoff
    kinds = [v.reshape(NLAT // ROWS, ROWS) for v in (north / center, south / center, ratio * ratio)]
    return np.pad(np.concatenate(kinds, axis=1), ((0, 0), (0, LANES - 3 * ROWS))).astype(np.float32)


def latitude_line(table_ref):
    block = lax.axis_index("lat") * SECTORS + place_of(lax.axis_index("lon"))
    return table_ref[pl.ds(block, 1), :]


def spread(line, lane, rows=SECTORS):
    return jnp.broadcast_to(line[:, lane : lane + 1], (rows, LANES))


def own_hops(hop_ref):
    start = place_of(lax.axis_index("lon")) * ROWS
    line = pltpu.roll(jnp.broadcast_to(hop_ref[...], (8, LANES)), lax.rem(LANES - start, LANES), 1)[:1]
    return [spread(line, r) for r in range(ROWS)]


def halves(value):
    high = value.astype(jnp.bfloat16)
    low = (value - high.astype(jnp.float32)).astype(jnp.bfloat16)
    return high, low


def place_of(sector):
    step = 2 * lax.bitwise_and(STEP_Y * (lax.shift_right_logical(sector, 2) - START_Y), 3)
    core = lax.bitwise_and(sector, 1)
    first_side = lax.bitwise_and(sector, 2) == 2 * START_X
    return jnp.where(
        first_side, step + lax.bitwise_xor(core, FIRST_CORE[0]), 14 - step + lax.bitwise_xor(core, FIRST_CORE[1])
    )


def sector_at(place):
    at, core = lax.shift_right_logical(lax.bitwise_and(place, 7), 1), lax.bitwise_and(place, 1)
    y = lax.bitwise_and(START_Y + STEP_Y * jnp.where(place < 8, at, 3 - at), 3)
    return 4 * y + jnp.where(
        place < 8,
        2 * START_X + lax.bitwise_xor(core, FIRST_CORE[0]),
        2 - 2 * START_X + lax.bitwise_xor(core, FIRST_CORE[1]),
    )


def first_row():
    return lax.axis_index("lat") * BAND + place_of(lax.axis_index("lon")) * ROWS


def from_sector(tile, source):
    low, high = tile[:8], tile[8:]
    parts = []
    for at in (slice(0, 8), slice(8, 16)):
        index = lax.bitwise_and(source[at], 7)
        parts.append(
            jnp.where(
                source[at] < 8,
                jnp.take_along_axis(low, index, axis=0, mode="promise_in_bounds"),
                jnp.take_along_axis(high, index, axis=0, mode="promise_in_bounds"),
            )
        )
    return jnp.concatenate(parts, axis=0)


def fetch(in_ref, array, t, r):
    return in_ref[pl.ds((array * TILES + t) * ROWS + r, SECTORS, stride=ARRAYS * TILES * ROWS), :]


def zonal_row(in_ref, hop, r, store):
    lane = lax.broadcasted_iota(jnp.int32, (SECTORS, LANES), 1)
    own_sector = sector_at(lax.broadcasted_iota(jnp.int32, (SECTORS, LANES), 0))

    def source(hops):
        return place_of(lax.bitwise_and(own_sector - hops + SECTORS, SECTORS - 1))

    sources, sources_before, sources_after = source(hop), source(hop + 1), source(hop - 1)
    weights = []
    for t in range(TILES):
        offset = 1.0 - fetch(in_ref, COMP, t, r)
        w_far = -offset * (offset - 1.0) * (offset - 2.0) * (1.0 / 6.0)
        w_near = (offset + 1.0) * (offset - 1.0) * (offset - 2.0) * 0.5
        w_next = -(offset + 1.0) * offset * (offset - 2.0) * 0.5
        w_last = (offset + 1.0) * offset * (offset - 1.0) * (1.0 / 6.0)
        weights.append((w_far, w_near, w_next, w_last))
    for c in range(COMP):
        raw = [fetch(in_ref, c, t, r) for t in range(TILES)]
        here = [from_sector(v, sources) for v in raw]
        before = from_sector(raw[TILES - 1], sources_before)
        after = from_sector(raw[0], sources_after)
        back_one = [pltpu.roll(v, 1, 1) for v in [before] + here]
        back_two = [pltpu.roll(v, 2, 1) for v in [before] + here]
        ahead = [pltpu.roll(v, LANES - 1, 1) for v in here + [after]]
        for t in range(TILES):
            w_far, w_near, w_next, w_last = weights[t]
            store(
                c,
                slice(t * SECTORS, (t + 1) * SECTORS),
                w_far * jnp.where(lane < 2, back_two[t], back_two[t + 1])
                + w_near * jnp.where(lane < 1, back_one[t], back_one[t + 1])
                + w_next * here[t]
                + w_last * jnp.where(lane == LANES - 1, ahead[t + 1], ahead[t]),
            )


def rim_kernel(hop_ref, in_ref, near_ref, far_ref):
    hops = own_hops(hop_ref)
    odd = lax.bitwise_and(place_of(lax.axis_index("lon")), 1) == 1
    rows = []
    for r in (0, ROWS - 1):
        values = {}

        def store(c, block, value):
            values[c, block.start] = value

        zonal_row(in_ref, hops[r], r, store)
        for t in range(TILES):
            values[COMP, t * SECTORS] = fetch(in_ref, COMP + 1, t, r)
        rows.append(values)
    for c, place in rows[0]:
        first, last = rows[0][c, place], rows[1][c, place]
        near_ref[c, place : place + SECTORS, :] = jnp.where(odd, first, last)
        far_ref[c, place : place + SECTORS, :] = jnp.where(odd, last, first)


def dot(left, right):
    return jnp.dot(left, right, preferred_element_type=jnp.float32)


def data_by_table(high, low, table):
    rows, depth = high.shape
    both = dot(jnp.concatenate([high, low], axis=0), table[:depth])
    return both[:rows] + both[rows:] + dot(high, table[depth:])


def table_by_data(table, high, low):
    depth = 2 * high.shape[0]
    return dot(table[:, :depth], jnp.concatenate([high, low], axis=0)) + dot(table[:, depth:], high)


def filter_group(slabs, damping, tables):
    first, forward, backward, last, twist_cos, twist_sin = tables
    count = len(slabs)
    spectrum = table_by_data(first, *halves(jnp.concatenate(slabs, axis=1)))
    parts = []
    for k in range(count):
        real = spectrum[:HALF_PAD, k * LANES : (k + 1) * LANES]
        imag = spectrum[HALF_PAD:, k * LANES : (k + 1) * LANES]
        parts.append(
            jnp.concatenate([real * twist_cos + imag * twist_sin, imag * twist_cos - real * twist_sin], axis=1)
        )
    spectrum = data_by_table(*halves(jnp.concatenate(parts, axis=0)), forward)
    parts = []
    for k in range(count):
        rows = spectrum[k * HALF_PAD : (k + 1) * HALF_PAD]
        parts.append(rows * jnp.concatenate([damping[k], damping[k]], axis=1))
    spectrum = data_by_table(*halves(jnp.concatenate(parts, axis=0)), backward)
    parts = []
    for k in range(count):
        real = spectrum[k * HALF_PAD : (k + 1) * HALF_PAD, :LANES]
        imag = spectrum[k * HALF_PAD : (k + 1) * HALF_PAD, LANES:]
        parts.append(
            jnp.concatenate([real * twist_cos - imag * twist_sin, imag * twist_cos + real * twist_sin], axis=0)
        )
    rebuilt = table_by_data(last, *halves(jnp.concatenate(parts, axis=1)))
    return [rebuilt[:, k * LANES : (k + 1) * LANES] for k in range(count)]


def listed_mask(listed_ref, row):
    hit = jnp.where(listed_ref[...] == row, 1.0, 0.0)
    hit = jnp.max(jnp.max(hit, axis=1, keepdims=True), axis=0, keepdims=True)
    return jnp.broadcast_to(hit, (SECTORS, LANES)) > 0.5


def filter_rows_into(out_ref, rows, ratios, merid_ref, listed_ref, sine_sq, tables):
    start = first_row()
    damping = []
    for ratio_sq in ratios:
        damping.extend([ratio_sq / jnp.maximum(ratio_sq, sine_sq)] * COMP)
    slabs = [merid_ref[c, i] for i in range(len(rows)) for c in range(COMP)]
    filtered = filter_group(slabs, damping, tables)
    for i, row in enumerate(rows):
        listed = listed_mask(listed_ref, start + row)
        for c in range(COMP):
            value = filtered[i * COMP + c]
            for t in range(TILES):
                block = slice(t * SECTORS, (t + 1) * SECTORS)
                out_ref[pl.ds((c * TILES + t) * ROWS + row, SECTORS, stride=COMP * TILES * ROWS), :] = jnp.where(
                    listed, value[block], merid_ref[c, i, block, :]
                )


def through_face(courant, own, above):
    return jnp.maximum(courant, 0.0) * own + jnp.minimum(courant, 0.0) * above


def outer_rows(line):
    odd = lax.bitwise_and(place_of(lax.axis_index("lon")), 1) == 1
    first, last = spread(line, RATIO * ROWS, HALF_PAD), spread(line, RATIO * ROWS + ROWS - 1, HALF_PAD)
    near, far = jnp.where(odd, 0, ROWS - 1), jnp.where(odd, ROWS - 1, 0)
    return near, far, jnp.where(odd, first, last), jnp.where(odd, last, first)


def interior_kernel(
    hop_ref, table_ref, listed_ref, in_ref, near_ref, far_ref, swap_ref, first_ref, forward_ref, backward_ref, last_ref,
    twist_cos_ref, twist_sin_ref, sine_ref, out_ref, kept_ref, zonal_ref, merid_ref,
):
    line = latitude_line(table_ref)
    hops = own_hops(hop_ref)
    odd = lax.bitwise_and(place_of(lax.axis_index("lon")), 1) == 1
    tables = (first_ref[...], forward_ref[...], backward_ref[...], last_ref[...], twist_cos_ref[...], twist_sin_ref[...])
    for r in INNER:

        def store(c, at, value):
            zonal_ref[c, r, at, :] = value

        zonal_row(in_ref, hops[r], r, store)
    north = [spread(line, NORTH * ROWS + r) for r in range(ROWS)]
    south = [spread(line, SOUTH * ROWS + r) for r in range(ROWS)]
    outside = jnp.where(odd, south[0], -north[ROWS - 1])
    for t in range(TILES):
        at = slice(t * SECTORS, (t + 1) * SECTORS)
        nearest = [near_ref[c, at, :] for c in range(COMP + 1)]
        farthest = [far_ref[c, at, :] for c in range(COMP)]
        own = [jnp.where(odd, n, f) for n, f in zip(nearest, farthest)]
        last_row_of = [jnp.where(odd, f, n) for n, f in zip(nearest, farthest)]
        before = None
        kept = []
        for r in range(ROWS - 1):
            courant = fetch(in_ref, COMP + 1, t, r)
            above = last_row_of if r == ROWS - 2 else [zonal_ref[c, r + 1, at, :] for c in range(COMP)]
            face = [through_face(courant, own[c], above[c]) for c in range(COMP)]
            for c in range(COMP):
                merid = own[c] - north[r] * face[c]
                if r == 0:
                    kept.append(merid)
                else:
                    merid_ref[c, r - 1, at, :] = merid + south[r] * before[c]
            own, before = above, face
        courant = jnp.where(odd, swap_ref[COMP, at, :], nearest[COMP])
        for c in range(COMP):
            last = last_row_of[c] + south[ROWS - 1] * before[c]
            other = swap_ref[c, at, :]
            face = through_face(courant, jnp.where(odd, other, nearest[c]), jnp.where(odd, nearest[c], other))
            merid_ref[c, len(INNER), at, :] = jnp.where(odd, kept[c], last) + outside * face
            kept_ref[c, at, :] = jnp.where(odd, last, kept[c])
    near, _, ratio, _ = outer_rows(line)
    ratios = [spread(line, RATIO * ROWS + r, HALF_PAD) for r in INNER] + [ratio]
    filter_rows_into(out_ref, INNER + (near,), ratios, merid_ref, listed_ref, sine_ref[...], tables)


def edge_kernel(
    table_ref, listed_ref, kept_ref, far_ref, swap_ref, first_ref, forward_ref, backward_ref, last_ref,
    twist_cos_ref, twist_sin_ref, sine_ref, partial_ref, out_ref, merid_ref,
):
    del partial_ref
    line = latitude_line(table_ref)
    odd = lax.bitwise_and(place_of(lax.axis_index("lon")), 1) == 1
    tables = (first_ref[...], forward_ref[...], backward_ref[...], last_ref[...], twist_cos_ref[...], twist_sin_ref[...])
    outside = jnp.where(odd, -spread(line, NORTH * ROWS + ROWS - 1), spread(line, SOUTH * ROWS))
    for t in range(TILES):
        at = slice(t * SECTORS, (t + 1) * SECTORS)
        courant = jnp.where(odd, far_ref[COMP, at, :], swap_ref[COMP, at, :])
        for c in range(COMP):
            own, other = far_ref[c, at, :], swap_ref[c, at, :]
            face = through_face(courant, jnp.where(odd, own, other), jnp.where(odd, other, own))
            merid_ref[c, 0, at, :] = kept_ref[c, at, :] + outside * face
    _, far, _, ratio = outer_rows(line)
    filter_rows_into(out_ref, (far,), [ratio], merid_ref, listed_ref, sine_ref[...], tables)


def on_device(fields, zonal_fraction, merid_courant, hop_counts, filter_rows):
    vmem = pl.BlockSpec(memory_space=pltpu.VMEM)
    params = pltpu.CompilerParams(vmem_limit_bytes=VMEM_LIMIT)
    hops = hop_counts.reshape(1, BAND)
    stacked = jnp.concatenate([fields[:, 0], zonal_fraction, merid_courant], axis=0)
    outgoing = stacked.reshape(ARRAYS, SECTORS, ROWS, TILES, LANES).transpose(1, 0, 3, 2, 4)
    outgoing = outgoing.reshape(SECTORS, ARRAYS * TILES * ROWS, LANES)
    incoming = lax.all_to_all(outgoing, "lon", 0, 0, tiled=True, axis_index_groups=[list(ORDER)])
    incoming = incoming.reshape(SECTORS * ARRAYS * TILES * ROWS, LANES)
    f32 = jnp.float32
    edge_shape = jax.ShapeDtypeStruct((COMP + 1, OUTER, LANES), f32)
    near, far = pl.pallas_call(
        rim_kernel,
        out_shape=(edge_shape, edge_shape),
        in_specs=[vmem, vmem],
        out_specs=(vmem, vmem),
        compiler_params=params,
    )(hops, incoming)
    bands = NLAT // BAND
    total = bands * SECTORS

    def device_of(block):
        return ORDER[block % SECTORS] * bands + block // SECTORS

    def swap(value, first_block):
        pairs = [(device_of(i), device_of(i + 1)) for i in range(first_block, total - 1, 2)]
        return lax.ppermute(value, ("lon", "lat"), pairs + [(j, i) for i, j in pairs])

    swapped = swap(near, 0)
    swapped_far = swap(far, 1)
    first, forward, backward, last, twist_cos, twist_sin, sine_sq = [jnp.asarray(v) for v in filter_tables()]
    latitudes = jnp.asarray(latitude_table())
    listed = filter_rows.reshape(4, LANES)
    out_shape = jax.ShapeDtypeStruct((SECTORS * COMP * TILES * ROWS, LANES), f32)
    constants = (first, forward, backward, last, twist_cos, twist_sin, sine_sq)
    partial, kept = pl.pallas_call(
        interior_kernel,
        out_shape=(out_shape, jax.ShapeDtypeStruct((COMP, OUTER, LANES), f32)),
        in_specs=[vmem] * 14,
        out_specs=(vmem, vmem),
        scratch_shapes=[
            pltpu.VMEM((COMP, ROWS, OUTER, LANES), f32),
            pltpu.VMEM((COMP, len(INNER) + 1, OUTER, LANES), f32),
        ],
        compiler_params=params,
        cost_estimate=pl.CostEstimate(flops=5_000_000_000, bytes_accessed=8_000_000, transcendentals=0),
    )(hops, latitudes, listed, incoming, near, far, swapped, *constants)
    returning = pl.pallas_call(
        edge_kernel,
        out_shape=out_shape,
        in_specs=[vmem] * 13,
        out_specs=vmem,
        input_output_aliases={12: 0},
        scratch_shapes=[pltpu.VMEM((COMP, 1, OUTER, LANES), f32)],
        compiler_params=params,
        cost_estimate=pl.CostEstimate(flops=1_000_000_000, bytes_accessed=4_000_000, transcendentals=0),
    )(latitudes, listed, kept, far, swapped_far, *constants, partial)
    arrived = lax.all_to_all(
        returning.reshape(SECTORS, COMP * TILES * ROWS, LANES), "lon", 0, 0, tiled=True, axis_index_groups=[list(ORDER)]
    )
    arrived = arrived.reshape(SECTORS, COMP, TILES, ROWS, LANES).transpose(1, 0, 3, 2, 4)
    return arrived.reshape(COMP, 1, BAND, TILES * LANES)


def solution(mesh):
    in_specs = (
        P(None, None, "lat", "lon"),
        P(None, "lat", "lon"),
        P(None, "lat", "lon"),
        P("lat"),
        P(),
    )
    out_specs = P(None, None, "lat", "lon")
    return jax.shard_map(
        on_device, mesh=mesh, in_specs=in_specs, out_specs=out_specs, check_vma=False
    )
```

```python
import functools
import math

import jax
import jax.numpy as jnp
import ml_dtypes
import numpy as np
from jax import lax
from jax.experimental import pallas as pl
from jax.experimental.pallas import tpu as pltpu
from jax.sharding import PartitionSpec as P

NLON = 12288
NLAT = 2048
SECTORS = 16
BAND = 128
ROWS = 8
TILES = 6
LANES = 128
OUTER = SECTORS * TILES
COMP = 3
ARRAYS = COMP + 2
HALF = OUTER // 2 + 1
HALF_PAD = 56
START_Y, STEP_Y, START_X = 2, 1, 1
FIRST_CORE = (1, 1)
ORDER = tuple(
    4 * ((START_Y + STEP_Y * (step if side == 0 else 3 - step)) % 4) + 2 * (START_X ^ side) + (FIRST_CORE[side] ^ core)
    for side in (0, 1)
    for step in range(4)
    for core in (0, 1)
)
INNER = (1, 2, 3, 4, 5, 6)
VMEM_LIMIT = 48 * 1024 * 1024

cos_cutoff = 0.7071067811865476


def split_bf16(table):
    high = table.astype(np.float32).astype(ml_dtypes.bfloat16)
    low = (table - high.astype(np.float64)).astype(np.float32).astype(ml_dtypes.bfloat16)
    return high, low


def filter_tables():
    at = np.arange(OUTER)
    a = TILES * np.asarray(ORDER)[at % SECTORS] + at // SECTORS
    c = np.arange(HALF_PAD)
    valid = (c < HALF)[:, None]
    angle = 2.0 * np.pi * ((c[:, None] * a[None, :]) % OUTER) / OUTER
    first = np.concatenate([np.where(valid, np.cos(angle), 0.0), np.where(valid, -np.sin(angle), 0.0)], axis=0)
    weight = np.where((c == 0) | (c == OUTER // 2), 1.0, 2.0) / NLON
    inner_only = (c > 0) & (c < OUTER // 2)
    last = np.concatenate(
        [
            np.where(valid, np.cos(angle) * weight[:, None], 0.0),
            np.where(valid & inner_only[:, None], -np.sin(angle) * weight[:, None], 0.0),
        ],
        axis=0,
    ).T
    b = np.arange(LANES)
    twist = 2.0 * np.pi * (c[:, None] * b[None, :]) / NLON
    inner = 2.0 * np.pi * ((b[:, None] * b[None, :]) % LANES) / LANES
    cos_in, sin_in = np.cos(inner), np.sin(inner)
    forward = np.block([[cos_in, -sin_in], [sin_in, cos_in]])
    backward = np.block([[cos_in, sin_in], [-sin_in, cos_in]])
    sine = np.sin(np.pi * (c[:, None] + OUTER * b[None, :]) / NLON)
    first_h, first_l = split_bf16(first)
    last_h, last_l = split_bf16(last)
    forward_h, forward_l = split_bf16(forward)
    backward_h, backward_l = split_bf16(backward)
    return (
        np.concatenate([first_h, first_h, first_l], axis=1),
        np.concatenate([forward_h, forward_l], axis=0),
        np.concatenate([backward_h, backward_l], axis=0),
        np.concatenate([last_h, last_h, last_l], axis=1),
        np.cos(twist).astype(np.float32),
        np.sin(twist).astype(np.float32),
        (sine * sine).astype(np.float32),
    )


NORTH, SOUTH, RATIO = range(3)


def latitude_table():
    row = np.arange(NLAT, dtype=np.float32)
    step = np.float32(math.pi / NLAT)
    center = np.sin(((row + np.float32(0.5)) * step).astype(np.float64))
    north = np.sin(((row + np.float32(1.0)) * step).astype(np.float64))
    north[-1] = 0.0
    south = np.concatenate([np.zeros(1), north[:-1]])
    ratio = center / cos_cutoff
    kinds = [v.reshape(NLAT // ROWS, ROWS) for v in (north / center, south / center, ratio * ratio)]
    return np.pad(np.concatenate(kinds, axis=1), ((0, 0), (0, LANES - 3 * ROWS))).astype(np.float32)


def latitude_line(table_ref):
    block = lax.axis_index("lat") * SECTORS + place_of(lax.axis_index("lon"))
    return table_ref[pl.ds(block, 1), :]


def spread(line, lane, rows=SECTORS):
    return jnp.broadcast_to(line[:, lane : lane + 1], (rows, LANES))


def own_hops(hop_ref):
    start = place_of(lax.axis_index("lon")) * ROWS
    line = pltpu.roll(jnp.broadcast_to(hop_ref[...], (8, LANES)), lax.rem(LANES - start, LANES), 1)[:1]
    return [spread(line, r) for r in range(ROWS)]


def halves(value):
    high = value.astype(jnp.bfloat16)
    low = (value - high.astype(jnp.float32)).astype(jnp.bfloat16)
    return high, low


def place_of(sector):
    step = 2 * lax.bitwise_and(STEP_Y * (lax.shift_right_logical(sector, 2) - START_Y), 3)
    core = lax.bitwise_and(sector, 1)
    first_side = lax.bitwise_and(sector, 2) == 2 * START_X
    return jnp.where(
        first_side, step + lax.bitwise_xor(core, FIRST_CORE[0]), 14 - step + lax.bitwise_xor(core, FIRST_CORE[1])
    )


def sector_at(place):
    at, core = lax.shift_right_logical(lax.bitwise_and(place, 7), 1), lax.bitwise_and(place, 1)
    y = lax.bitwise_and(START_Y + STEP_Y * jnp.where(place < 8, at, 3 - at), 3)
    return 4 * y + jnp.where(
        place < 8,
        2 * START_X + lax.bitwise_xor(core, FIRST_CORE[0]),
        2 - 2 * START_X + lax.bitwise_xor(core, FIRST_CORE[1]),
    )


def first_row():
    return lax.axis_index("lat") * BAND + place_of(lax.axis_index("lon")) * ROWS


def from_sector(tile, source):
    low, high = tile[:8], tile[8:]
    parts = []
    for at in (slice(0, 8), slice(8, 16)):
        index = lax.bitwise_and(source[at], 7)
        parts.append(
            jnp.where(
                source[at] < 8,
                jnp.take_along_axis(low, index, axis=0, mode="promise_in_bounds"),
                jnp.take_along_axis(high, index, axis=0, mode="promise_in_bounds"),
            )
        )
    return jnp.concatenate(parts, axis=0)


def fetch(in_ref, array, t, r):
    return in_ref[pl.ds((array * TILES + t) * ROWS + r, SECTORS, stride=ARRAYS * TILES * ROWS), :]


def zonal_row(in_ref, hop, r, store):
    lane = lax.broadcasted_iota(jnp.int32, (SECTORS, LANES), 1)
    own_sector = sector_at(lax.broadcasted_iota(jnp.int32, (SECTORS, LANES), 0))

    def source(hops):
        return place_of(lax.bitwise_and(own_sector - hops + SECTORS, SECTORS - 1))

    sources, sources_before, sources_after = source(hop), source(hop + 1), source(hop - 1)
    weights = []
    for t in range(TILES):
        offset = 1.0 - fetch(in_ref, COMP, t, r)
        w_far = -offset * (offset - 1.0) * (offset - 2.0) * (1.0 / 6.0)
        w_near = (offset + 1.0) * (offset - 1.0) * (offset - 2.0) * 0.5
        w_next = -(offset + 1.0) * offset * (offset - 2.0) * 0.5
        w_last = (offset + 1.0) * offset * (offset - 1.0) * (1.0 / 6.0)
        weights.append((w_far, w_near, w_next, w_last))
    for c in range(COMP):
        raw = [fetch(in_ref, c, t, r) for t in range(TILES)]
        here = [from_sector(v, sources) for v in raw]
        before = from_sector(raw[TILES - 1], sources_before)
        after = from_sector(raw[0], sources_after)
        back_one = [pltpu.roll(v, 1, 1) for v in [before] + here]
        back_two = [pltpu.roll(v, 2, 1) for v in [before] + here]
        ahead = [pltpu.roll(v, LANES - 1, 1) for v in here + [after]]
        for t in range(TILES):
            w_far, w_near, w_next, w_last = weights[t]
            store(
                c,
                slice(t * SECTORS, (t + 1) * SECTORS),
                w_far * jnp.where(lane < 2, back_two[t], back_two[t + 1])
                + w_near * jnp.where(lane < 1, back_one[t], back_one[t + 1])
                + w_next * here[t]
                + w_last * jnp.where(lane == LANES - 1, ahead[t + 1], ahead[t]),
            )


def rim_kernel(hop_ref, in_ref, near_ref, far_ref):
    hops = own_hops(hop_ref)
    odd = lax.bitwise_and(place_of(lax.axis_index("lon")), 1) == 1
    rows = []
    for r in (0, ROWS - 1):
        values = {}

        def store(c, block, value):
            values[c, block.start] = value

        zonal_row(in_ref, hops[r], r, store)
        for t in range(TILES):
            values[COMP, t * SECTORS] = fetch(in_ref, COMP + 1, t, r)
        rows.append(values)
    for c, place in rows[0]:
        first, last = rows[0][c, place], rows[1][c, place]
        near_ref[c, place : place + SECTORS, :] = jnp.where(odd, first, last)
        far_ref[c, place : place + SECTORS, :] = jnp.where(odd, last, first)


def dot(left, right):
    return jnp.dot(left, right, preferred_element_type=jnp.float32)


def data_by_table(high, low, table):
    rows, depth = high.shape
    both = dot(jnp.concatenate([high, low], axis=0), table[:depth])
    return both[:rows] + both[rows:] + dot(high, table[depth:])


def table_by_data(table, high, low):
    depth = 2 * high.shape[0]
    return dot(table[:, :depth], jnp.concatenate([high, low], axis=0)) + dot(table[:, depth:], high)


def filter_group(slabs, damping, tables):
    first, forward, backward, last, twist_cos, twist_sin = tables
    count = len(slabs)
    spectrum = table_by_data(first, *halves(jnp.concatenate(slabs, axis=1)))
    parts = []
    for k in range(count):
        real = spectrum[:HALF_PAD, k * LANES : (k + 1) * LANES]
        imag = spectrum[HALF_PAD:, k * LANES : (k + 1) * LANES]
        parts.append(
            jnp.concatenate([real * twist_cos + imag * twist_sin, imag * twist_cos - real * twist_sin], axis=1)
        )
    spectrum = data_by_table(*halves(jnp.concatenate(parts, axis=0)), forward)
    parts = []
    for k in range(count):
        rows = spectrum[k * HALF_PAD : (k + 1) * HALF_PAD]
        parts.append(rows * jnp.concatenate([damping[k], damping[k]], axis=1))
    spectrum = data_by_table(*halves(jnp.concatenate(parts, axis=0)), backward)
    parts = []
    for k in range(count):
        real = spectrum[k * HALF_PAD : (k + 1) * HALF_PAD, :LANES]
        imag = spectrum[k * HALF_PAD : (k + 1) * HALF_PAD, LANES:]
        parts.append(
            jnp.concatenate([real * twist_cos - imag * twist_sin, imag * twist_cos + real * twist_sin], axis=0)
        )
    rebuilt = table_by_data(last, *halves(jnp.concatenate(parts, axis=1)))
    return [rebuilt[:, k * LANES : (k + 1) * LANES] for k in range(count)]


def listed_mask(listed_ref, row):
    hit = jnp.where(listed_ref[...] == row, 1.0, 0.0)
    hit = jnp.max(jnp.max(hit, axis=1, keepdims=True), axis=0, keepdims=True)
    return jnp.broadcast_to(hit, (SECTORS, LANES)) > 0.5


def filter_rows_into(out_ref, rows, ratios, merid_ref, listed_ref, sine_sq, tables):
    start = first_row()
    damping = []
    for ratio_sq in ratios:
        damping.extend([ratio_sq / jnp.maximum(ratio_sq, sine_sq)] * COMP)
    slabs = [merid_ref[c, i] for i in range(len(rows)) for c in range(COMP)]
    filtered = filter_group(slabs, damping, tables)
    for i, row in enumerate(rows):
        listed = listed_mask(listed_ref, start + row)
        for c in range(COMP):
            value = filtered[i * COMP + c]
            for t in range(TILES):
                block = slice(t * SECTORS, (t + 1) * SECTORS)
                out_ref[pl.ds((c * TILES + t) * ROWS + row, SECTORS, stride=COMP * TILES * ROWS), :] = jnp.where(
                    listed, value[block], merid_ref[c, i, block, :]
                )


def through_face(courant, own, above):
    return jnp.maximum(courant, 0.0) * own + jnp.minimum(courant, 0.0) * above


def outer_rows(line):
    odd = lax.bitwise_and(place_of(lax.axis_index("lon")), 1) == 1
    first, last = spread(line, RATIO * ROWS, HALF_PAD), spread(line, RATIO * ROWS + ROWS - 1, HALF_PAD)
    near, far = jnp.where(odd, 0, ROWS - 1), jnp.where(odd, ROWS - 1, 0)
    return near, far, jnp.where(odd, first, last), jnp.where(odd, last, first)


def interior_kernel(
    hop_ref, table_ref, listed_ref, in_ref, near_ref, far_ref, swap_ref, first_ref, forward_ref, backward_ref, last_ref,
    twist_cos_ref, twist_sin_ref, sine_ref, out_ref, kept_ref, zonal_ref, merid_ref,
):
    line = latitude_line(table_ref)
    hops = own_hops(hop_ref)
    odd = lax.bitwise_and(place_of(lax.axis_index("lon")), 1) == 1
    tables = (first_ref[...], forward_ref[...], backward_ref[...], last_ref[...], twist_cos_ref[...], twist_sin_ref[...])
    for r in INNER:

        def store(c, at, value):
            zonal_ref[c, r, at, :] = value

        zonal_row(in_ref, hops[r], r, store)
    north = [spread(line, NORTH * ROWS + r) for r in range(ROWS)]
    south = [spread(line, SOUTH * ROWS + r) for r in range(ROWS)]
    outside = jnp.where(odd, south[0], -north[ROWS - 1])
    for t in range(TILES):
        at = slice(t * SECTORS, (t + 1) * SECTORS)
        nearest = [near_ref[c, at, :] for c in range(COMP + 1)]
        farthest = [far_ref[c, at, :] for c in range(COMP)]
        own = [jnp.where(odd, n, f) for n, f in zip(nearest, farthest)]
        last_row_of = [jnp.where(odd, f, n) for n, f in zip(nearest, farthest)]
        before = None
        kept = []
        for r in range(ROWS - 1):
            courant = fetch(in_ref, COMP + 1, t, r)
            above = last_row_of if r == ROWS - 2 else [zonal_ref[c, r + 1, at, :] for c in range(COMP)]
            face = [through_face(courant, own[c], above[c]) for c in range(COMP)]
            for c in range(COMP):
                merid = own[c] - north[r] * face[c]
                if r == 0:
                    kept.append(merid)
                else:
                    merid_ref[c, r - 1, at, :] = merid + south[r] * before[c]
            own, before = above, face
        courant = jnp.where(odd, swap_ref[COMP, at, :], nearest[COMP])
        for c in range(COMP):
            last = last_row_of[c] + south[ROWS - 1] * before[c]
            other = swap_ref[c, at, :]
            face = through_face(courant, jnp.where(odd, other, nearest[c]), jnp.where(odd, nearest[c], other))
            merid_ref[c, len(INNER), at, :] = jnp.where(odd, kept[c], last) + outside * face
            kept_ref[c, at, :] = jnp.where(odd, last, kept[c])
    near, _, ratio, _ = outer_rows(line)
    ratios = [spread(line, RATIO * ROWS + r, HALF_PAD) for r in INNER] + [ratio]
    filter_rows_into(out_ref, INNER + (near,), ratios, merid_ref, listed_ref, sine_ref[...], tables)


def edge_kernel(
    table_ref, listed_ref, kept_ref, far_ref, swap_ref, first_ref, forward_ref, backward_ref, last_ref,
    twist_cos_ref, twist_sin_ref, sine_ref, partial_ref, out_ref, merid_ref,
):
    del partial_ref
    line = latitude_line(table_ref)
    odd = lax.bitwise_and(place_of(lax.axis_index("lon")), 1) == 1
    tables = (first_ref[...], forward_ref[...], backward_ref[...], last_ref[...], twist_cos_ref[...], twist_sin_ref[...])
    outside = jnp.where(odd, -spread(line, NORTH * ROWS + ROWS - 1), spread(line, SOUTH * ROWS))
    for t in range(TILES):
        at = slice(t * SECTORS, (t + 1) * SECTORS)
        courant = jnp.where(odd, far_ref[COMP, at, :], swap_ref[COMP, at, :])
        for c in range(COMP):
            own, other = far_ref[c, at, :], swap_ref[c, at, :]
            face = through_face(courant, jnp.where(odd, own, other), jnp.where(odd, other, own))
            merid_ref[c, 0, at, :] = kept_ref[c, at, :] + outside * face
    _, far, _, ratio = outer_rows(line)
    filter_rows_into(out_ref, (far,), [ratio], merid_ref, listed_ref, sine_ref[...], tables)


def on_device(fields, zonal_fraction, merid_courant, hop_counts, filter_rows):
    vmem = pl.BlockSpec(memory_space=pltpu.VMEM)
    params = pltpu.CompilerParams(vmem_limit_bytes=VMEM_LIMIT)
    hops = hop_counts.reshape(1, BAND)
    parts = []
    for value in (fields, zonal_fraction, merid_courant):
        value = value.reshape(-1, SECTORS, ROWS, TILES, LANES).transpose(1, 0, 3, 2, 4)
        parts.append(value.reshape(SECTORS, -1, LANES))
    outgoing = jnp.concatenate(parts, axis=1)
    incoming = lax.all_to_all(outgoing, "lon", 0, 0, tiled=True, axis_index_groups=[list(ORDER)])
    incoming = incoming.reshape(SECTORS * ARRAYS * TILES * ROWS, LANES)
    f32 = jnp.float32
    edge_shape = jax.ShapeDtypeStruct((COMP + 1, OUTER, LANES), f32)
    near, far = pl.pallas_call(
        rim_kernel,
        out_shape=(edge_shape, edge_shape),
        in_specs=[vmem, vmem],
        out_specs=(vmem, vmem),
        compiler_params=params,
    )(hops, incoming)
    bands = NLAT // BAND
    total = bands * SECTORS

    def device_of(block):
        return ORDER[block % SECTORS] * bands + block // SECTORS

    def swap(value, first_block):
        pairs = [(device_of(i), device_of(i + 1)) for i in range(first_block, total - 1, 2)]
        return lax.ppermute(value, ("lon", "lat"), pairs + [(j, i) for i, j in pairs])

    swapped = swap(near, 0)
    swapped_far = swap(far, 1)
    first, forward, backward, last, twist_cos, twist_sin, sine_sq = [jnp.asarray(v) for v in filter_tables()]
    latitudes = jnp.asarray(latitude_table())
    listed = filter_rows.reshape(4, LANES)
    out_shape = jax.ShapeDtypeStruct((SECTORS * COMP * TILES * ROWS, LANES), f32)
    constants = (first, forward, backward, last, twist_cos, twist_sin, sine_sq)
    partial, kept = pl.pallas_call(
        interior_kernel,
        out_shape=(out_shape, jax.ShapeDtypeStruct((COMP, OUTER, LANES), f32)),
        in_specs=[vmem] * 14,
        out_specs=(vmem, vmem),
        scratch_shapes=[
            pltpu.VMEM((COMP, ROWS, OUTER, LANES), f32),
            pltpu.VMEM((COMP, len(INNER) + 1, OUTER, LANES), f32),
        ],
        compiler_params=params,
        cost_estimate=pl.CostEstimate(flops=5_000_000_000, bytes_accessed=8_000_000, transcendentals=0),
    )(hops, latitudes, listed, incoming, near, far, swapped, *constants)
    returning = pl.pallas_call(
        edge_kernel,
        out_shape=out_shape,
        in_specs=[vmem] * 13,
        out_specs=vmem,
        input_output_aliases={12: 0},
        scratch_shapes=[pltpu.VMEM((COMP, 1, OUTER, LANES), f32)],
        compiler_params=params,
        cost_estimate=pl.CostEstimate(flops=1_000_000_000, bytes_accessed=4_000_000, transcendentals=0),
    )(latitudes, listed, kept, far, swapped_far, *constants, partial)
    arrived = lax.all_to_all(
        returning.reshape(SECTORS, COMP * TILES * ROWS, LANES), "lon", 0, 0, tiled=True, axis_index_groups=[list(ORDER)]
    )
    arrived = arrived.reshape(SECTORS, COMP, TILES, ROWS, LANES).transpose(1, 0, 3, 2, 4)
    return arrived.reshape(COMP, 1, BAND, TILES * LANES)


def solution(mesh):
    in_specs = (
        P(None, None, "lat", "lon"),
        P(None, "lat", "lon"),
        P(None, "lat", "lon"),
        P("lat"),
        P(),
    )
    out_specs = P(None, None, "lat", "lon")
    return jax.shard_map(
        on_device, mesh=mesh, in_specs=in_specs, out_specs=out_specs, check_vma=False
    )
```

```python
import functools
import math

import jax
import jax.numpy as jnp
import ml_dtypes
import numpy as np
from jax import lax
from jax.experimental import pallas as pl
from jax.experimental.pallas import tpu as pltpu
from jax.sharding import PartitionSpec as P

NLON = 12288
NLAT = 2048
SECTORS = 16
BAND = 128
ROWS = 8
TILES = 6
LANES = 128
OUTER = SECTORS * TILES
COMP = 3
ARRAYS = COMP + 2
HALF = OUTER // 2 + 1
HALF_PAD = 56
START_Y, STEP_Y, START_X = 2, 1, 1
FIRST_CORE = (1, 1)
ORDER = tuple(
    4 * ((START_Y + STEP_Y * (step if side == 0 else 3 - step)) % 4) + 2 * (START_X ^ side) + (FIRST_CORE[side] ^ core)
    for side in (0, 1)
    for step in range(4)
    for core in (0, 1)
)
INNER = (1, 2, 3, 4, 5, 6)
VMEM_LIMIT = 48 * 1024 * 1024

cos_cutoff = 0.7071067811865476


def split_bf16(table):
    high = table.astype(np.float32).astype(ml_dtypes.bfloat16)
    low = (table - high.astype(np.float64)).astype(np.float32).astype(ml_dtypes.bfloat16)
    return high, low


def filter_tables():
    at = np.arange(OUTER)
    a = TILES * np.asarray(ORDER)[at % SECTORS] + at // SECTORS
    c = np.arange(HALF_PAD)
    valid = (c < HALF)[:, None]
    angle = 2.0 * np.pi * ((c[:, None] * a[None, :]) % OUTER) / OUTER
    first = np.concatenate([np.where(valid, np.cos(angle), 0.0), np.where(valid, -np.sin(angle), 0.0)], axis=0)
    weight = np.where((c == 0) | (c == OUTER // 2), 1.0, 2.0) / NLON
    inner_only = (c > 0) & (c < OUTER // 2)
    last = np.concatenate(
        [
            np.where(valid, np.cos(angle) * weight[:, None], 0.0),
            np.where(valid & inner_only[:, None], -np.sin(angle) * weight[:, None], 0.0),
        ],
        axis=0,
    ).T
    b = np.arange(LANES)
    twist = 2.0 * np.pi * (c[:, None] * b[None, :]) / NLON
    inner = 2.0 * np.pi * ((b[:, None] * b[None, :]) % LANES) / LANES
    cos_in, sin_in = np.cos(inner), np.sin(inner)
    forward = np.block([[cos_in, -sin_in], [sin_in, cos_in]])
    backward = np.block([[cos_in, sin_in], [-sin_in, cos_in]])
    sine = np.sin(np.pi * (c[:, None] + OUTER * b[None, :]) / NLON)
    first_h, first_l = split_bf16(first)
    last_h, last_l = split_bf16(last)
    forward_h, forward_l = split_bf16(forward)
    backward_h, backward_l = split_bf16(backward)
    return (
        np.concatenate([first_h, first_h, first_l], axis=1),
        np.concatenate([forward_h, forward_l], axis=0),
        np.concatenate([backward_h, backward_l], axis=0),
        np.concatenate([last_h, last_h, last_l], axis=1),
        np.cos(twist).astype(np.float32),
        np.sin(twist).astype(np.float32),
        (sine * sine).astype(np.float32),
    )


NORTH, SOUTH, RATIO = range(3)


def latitude_table():
    row = np.arange(NLAT, dtype=np.float32)
    step = np.float32(math.pi / NLAT)
    center = np.sin(((row + np.float32(0.5)) * step).astype(np.float64))
    north = np.sin(((row + np.float32(1.0)) * step).astype(np.float64))
    north[-1] = 0.0
    south = np.concatenate([np.zeros(1), north[:-1]])
    ratio = center / cos_cutoff
    kinds = [v.reshape(NLAT // ROWS, ROWS) for v in (north / center, south / center, ratio * ratio)]
    return np.pad(np.concatenate(kinds, axis=1), ((0, 0), (0, LANES - 3 * ROWS))).astype(np.float32)


def latitude_line(table_ref):
    block = lax.axis_index("lat") * SECTORS + place_of(lax.axis_index("lon"))
    return table_ref[pl.ds(block, 1), :]


def spread(line, lane, rows=SECTORS):
    return jnp.broadcast_to(line[:, lane : lane + 1], (rows, LANES))


def own_hops(hop_ref):
    start = place_of(lax.axis_index("lon")) * ROWS
    line = pltpu.roll(jnp.broadcast_to(hop_ref[...], (8, LANES)), lax.rem(LANES - start, LANES), 1)[:1]
    return [spread(line, r) for r in range(ROWS)]


def halves(value):
    high = value.astype(jnp.bfloat16)
    low = (value - high.astype(jnp.float32)).astype(jnp.bfloat16)
    return high, low


def place_of(sector):
    step = 2 * lax.bitwise_and(STEP_Y * (lax.shift_right_logical(sector, 2) - START_Y), 3)
    core = lax.bitwise_and(sector, 1)
    first_side = lax.bitwise_and(sector, 2) == 2 * START_X
    return jnp.where(
        first_side, step + lax.bitwise_xor(core, FIRST_CORE[0]), 14 - step + lax.bitwise_xor(core, FIRST_CORE[1])
    )


def sector_at(place):
    at, core = lax.shift_right_logical(lax.bitwise_and(place, 7), 1), lax.bitwise_and(place, 1)
    y = lax.bitwise_and(START_Y + STEP_Y * jnp.where(place < 8, at, 3 - at), 3)
    return 4 * y + jnp.where(
        place < 8,
        2 * START_X + lax.bitwise_xor(core, FIRST_CORE[0]),
        2 - 2 * START_X + lax.bitwise_xor(core, FIRST_CORE[1]),
    )


def first_row():
    return lax.axis_index("lat") * BAND + place_of(lax.axis_index("lon")) * ROWS


def from_sector(tile, source):
    low, high = tile[:8], tile[8:]
    parts = []
    for at in (slice(0, 8), slice(8, 16)):
        index = lax.bitwise_and(source[at], 7)
        parts.append(
            jnp.where(
                source[at] < 8,
                jnp.take_along_axis(low, index, axis=0, mode="promise_in_bounds"),
                jnp.take_along_axis(high, index, axis=0, mode="promise_in_bounds"),
            )
        )
    return jnp.concatenate(parts, axis=0)


def fetch(in_ref, array, t, r):
    return in_ref[pl.ds((array * TILES + t) * ROWS + r, SECTORS, stride=ARRAYS * TILES * ROWS), :]


def zonal_row(in_ref, hop, r, store):
    lane = lax.broadcasted_iota(jnp.int32, (SECTORS, LANES), 1)
    own_sector = sector_at(lax.broadcasted_iota(jnp.int32, (SECTORS, LANES), 0))

    def source(hops):
        return place_of(lax.bitwise_and(own_sector - hops + SECTORS, SECTORS - 1))

    sources, sources_before, sources_after = source(hop), source(hop + 1), source(hop - 1)
    weights = []
    for t in range(TILES):
        offset = 1.0 - fetch(in_ref, COMP, t, r)
        w_far = -offset * (offset - 1.0) * (offset - 2.0) * (1.0 / 6.0)
        w_near = (offset + 1.0) * (offset - 1.0) * (offset - 2.0) * 0.5
        w_next = -(offset + 1.0) * offset * (offset - 2.0) * 0.5
        w_last = (offset + 1.0) * offset * (offset - 1.0) * (1.0 / 6.0)
        weights.append((w_far, w_near, w_next, w_last))
    for c in range(COMP):
        raw = [fetch(in_ref, c, t, r) for t in range(TILES)]
        here = [from_sector(v, sources) for v in raw]
        before = from_sector(raw[TILES - 1], sources_before)
        after = from_sector(raw[0], sources_after)
        back_one = [pltpu.roll(v, 1, 1) for v in [before] + here]
        back_two = [pltpu.roll(v, 2, 1) for v in [before] + here]
        ahead = [pltpu.roll(v, LANES - 1, 1) for v in here + [after]]
        for t in range(TILES):
            w_far, w_near, w_next, w_last = weights[t]
            store(
                c,
                slice(t * SECTORS, (t + 1) * SECTORS),
                w_far * jnp.where(lane < 2, back_two[t], back_two[t + 1])
                + w_near * jnp.where(lane < 1, back_one[t], back_one[t + 1])
                + w_next * here[t]
                + w_last * jnp.where(lane == LANES - 1, ahead[t + 1], ahead[t]),
            )


def rim_kernel(hop_ref, in_ref, near_ref, far_ref):
    hops = own_hops(hop_ref)
    odd = lax.bitwise_and(place_of(lax.axis_index("lon")), 1) == 1
    rows = []
    for r in (0, ROWS - 1):
        values = {}

        def store(c, block, value):
            values[c, block.start] = value

        zonal_row(in_ref, hops[r], r, store)
        for t in range(TILES):
            values[COMP, t * SECTORS] = fetch(in_ref, COMP + 1, t, r)
        rows.append(values)
    for c, place in rows[0]:
        first, last = rows[0][c, place], rows[1][c, place]
        near_ref[c, place : place + SECTORS, :] = jnp.where(odd, first, last)
        far_ref[c, place : place + SECTORS, :] = jnp.where(odd, last, first)


def dot(left, right):
    return jnp.dot(left, right, preferred_element_type=jnp.float32)


def data_by_table(high, low, table):
    rows, depth = high.shape
    both = dot(jnp.concatenate([high, low], axis=0), table[:depth])
    return both[:rows] + both[rows:] + dot(high, table[depth:])


def table_by_data(table, high, low):
    depth = 2 * high.shape[0]
    return dot(table[:, :depth], jnp.concatenate([high, low], axis=0)) + dot(table[:, depth:], high)


def filter_group(slabs, damping, tables):
    first, forward, backward, last, twist_cos, twist_sin = tables
    count = len(slabs)
    spectrum = table_by_data(first, *halves(jnp.concatenate(slabs, axis=1)))
    parts = []
    for k in range(count):
        real = spectrum[:HALF_PAD, k * LANES : (k + 1) * LANES]
        imag = spectrum[HALF_PAD:, k * LANES : (k + 1) * LANES]
        parts.append(
            jnp.concatenate([real * twist_cos + imag * twist_sin, imag * twist_cos - real * twist_sin], axis=1)
        )
    spectrum = data_by_table(*halves(jnp.concatenate(parts, axis=0)), forward)
    parts = []
    for k in range(count):
        rows = spectrum[k * HALF_PAD : (k + 1) * HALF_PAD]
        parts.append(rows * jnp.concatenate([damping[k], damping[k]], axis=1))
    spectrum = data_by_table(*halves(jnp.concatenate(parts, axis=0)), backward)
    parts = []
    for k in range(count):
        real = spectrum[k * HALF_PAD : (k + 1) * HALF_PAD, :LANES]
        imag = spectrum[k * HALF_PAD : (k + 1) * HALF_PAD, LANES:]
        parts.append(
            jnp.concatenate([real * twist_cos - imag * twist_sin, imag * twist_cos + real * twist_sin], axis=0)
        )
    rebuilt = table_by_data(last, *halves(jnp.concatenate(parts, axis=1)))
    return [rebuilt[:, k * LANES : (k + 1) * LANES] for k in range(count)]


def listed_mask(listed_ref, row):
    hit = jnp.where(listed_ref[...] == row, 1.0, 0.0)
    hit = jnp.max(jnp.max(hit, axis=1, keepdims=True), axis=0, keepdims=True)
    return jnp.broadcast_to(hit, (SECTORS, LANES)) > 0.5


def filter_rows_into(out_ref, rows, ratios, merid_ref, listed_ref, sine_sq, tables):
    start = first_row()
    damping = []
    for ratio_sq in ratios:
        damping.extend([ratio_sq / jnp.maximum(ratio_sq, sine_sq)] * COMP)
    slabs = [merid_ref[c, i] for i in range(len(rows)) for c in range(COMP)]
    filtered = filter_group(slabs, damping, tables)
    for i, row in enumerate(rows):
        listed = listed_mask(listed_ref, start + row)
        for c in range(COMP):
            value = filtered[i * COMP + c]
            for t in range(TILES):
                block = slice(t * SECTORS, (t + 1) * SECTORS)
                out_ref[pl.ds((c * TILES + t) * ROWS + row, SECTORS, stride=COMP * TILES * ROWS), :] = jnp.where(
                    listed, value[block], merid_ref[c, i, block, :]
                )


def through_face(courant, own, above):
    return jnp.maximum(courant, 0.0) * own + jnp.minimum(courant, 0.0) * above


def outer_rows(line):
    odd = lax.bitwise_and(place_of(lax.axis_index("lon")), 1) == 1
    first, last = spread(line, RATIO * ROWS, HALF_PAD), spread(line, RATIO * ROWS + ROWS - 1, HALF_PAD)
    near, far = jnp.where(odd, 0, ROWS - 1), jnp.where(odd, ROWS - 1, 0)
    return near, far, jnp.where(odd, first, last), jnp.where(odd, last, first)


def interior_kernel(
    hop_ref, table_ref, listed_ref, in_ref, near_ref, far_ref, swap_ref, first_ref, forward_ref, backward_ref, last_ref,
    twist_cos_ref, twist_sin_ref, sine_ref, out_ref, kept_ref, zonal_ref, merid_ref,
):
    line = latitude_line(table_ref)
    hops = own_hops(hop_ref)
    odd = lax.bitwise_and(place_of(lax.axis_index("lon")), 1) == 1
    tables = (first_ref[...], forward_ref[...], backward_ref[...], last_ref[...], twist_cos_ref[...], twist_sin_ref[...])
    for r in INNER:

        def store(c, at, value):
            zonal_ref[c, r, at, :] = value

        zonal_row(in_ref, hops[r], r, store)
    north = [spread(line, NORTH * ROWS + r) for r in range(ROWS)]
    south = [spread(line, SOUTH * ROWS + r) for r in range(ROWS)]
    outside = jnp.where(odd, south[0], -north[ROWS - 1])
    for t in range(TILES):
        at = slice(t * SECTORS, (t + 1) * SECTORS)
        nearest = [near_ref[c, at, :] for c in range(COMP + 1)]
        farthest = [far_ref[c, at, :] for c in range(COMP)]
        own = [jnp.where(odd, n, f) for n, f in zip(nearest, farthest)]
        last_row_of = [jnp.where(odd, f, n) for n, f in zip(nearest, farthest)]
        before = None
        kept = []
        for r in range(ROWS - 1):
            courant = fetch(in_ref, COMP + 1, t, r)
            above = last_row_of if r == ROWS - 2 else [zonal_ref[c, r + 1, at, :] for c in range(COMP)]
            face = [through_face(courant, own[c], above[c]) for c in range(COMP)]
            for c in range(COMP):
                merid = own[c] - north[r] * face[c]
                if r == 0:
                    kept.append(merid)
                else:
                    merid_ref[c, r - 1, at, :] = merid + south[r] * before[c]
            own, before = above, face
        courant = jnp.where(odd, swap_ref[COMP, at, :], nearest[COMP])
        for c in range(COMP):
            last = last_row_of[c] + south[ROWS - 1] * before[c]
            other = swap_ref[c, at, :]
            face = through_face(courant, jnp.where(odd, other, nearest[c]), jnp.where(odd, nearest[c], other))
            merid_ref[c, len(INNER), at, :] = jnp.where(odd, kept[c], last) + outside * face
            kept_ref[c, at, :] = jnp.where(odd, last, kept[c])
    near, _, ratio, _ = outer_rows(line)
    ratios = [spread(line, RATIO * ROWS + r, HALF_PAD) for r in INNER] + [ratio]
    filter_rows_into(out_ref, INNER + (near,), ratios, merid_ref, listed_ref, sine_ref[...], tables)


def edge_kernel(
    table_ref, listed_ref, kept_ref, far_ref, swap_ref, first_ref, forward_ref, backward_ref, last_ref,
    twist_cos_ref, twist_sin_ref, sine_ref, partial_ref, out_ref, merid_ref,
):
    del partial_ref
    line = latitude_line(table_ref)
    odd = lax.bitwise_and(place_of(lax.axis_index("lon")), 1) == 1
    tables = (first_ref[...], forward_ref[...], backward_ref[...], last_ref[...], twist_cos_ref[...], twist_sin_ref[...])
    outside = jnp.where(odd, -spread(line, NORTH * ROWS + ROWS - 1), spread(line, SOUTH * ROWS))
    for t in range(TILES):
        at = slice(t * SECTORS, (t + 1) * SECTORS)
        courant = jnp.where(odd, far_ref[COMP, at, :], swap_ref[COMP, at, :])
        for c in range(COMP):
            own, other = far_ref[c, at, :], swap_ref[c, at, :]
            face = through_face(courant, jnp.where(odd, own, other), jnp.where(odd, other, own))
            merid_ref[c, 0, at, :] = kept_ref[c, at, :] + outside * face
    _, far, _, ratio = outer_rows(line)
    filter_rows_into(out_ref, (far,), [ratio], merid_ref, listed_ref, sine_ref[...], tables)


def unpack_kernel(in_ref, out_ref, sems):
    size = TILES * ROWS
    copies = [
        pltpu.make_async_copy(in_ref.at[:, pl.ds(c * size, size), :], out_ref.at[c], sems.at[c]) for c in range(COMP)
    ]
    for copy in copies:
        copy.start()
    for copy in copies:
        copy.wait()


def on_device(fields, zonal_fraction, merid_courant, hop_counts, filter_rows):
    vmem = pl.BlockSpec(memory_space=pltpu.VMEM)
    params = pltpu.CompilerParams(vmem_limit_bytes=VMEM_LIMIT)
    hops = hop_counts.reshape(1, BAND)
    parts = []
    for value in (fields, zonal_fraction, merid_courant):
        value = value.reshape(-1, SECTORS, ROWS, TILES, LANES).transpose(1, 0, 3, 2, 4)
        parts.append(value.reshape(SECTORS, -1, LANES))
    outgoing = jnp.concatenate(parts, axis=1)
    incoming = lax.all_to_all(outgoing, "lon", 0, 0, tiled=True, axis_index_groups=[list(ORDER)])
    incoming = incoming.reshape(SECTORS * ARRAYS * TILES * ROWS, LANES)
    f32 = jnp.float32
    edge_shape = jax.ShapeDtypeStruct((COMP + 1, OUTER, LANES), f32)
    near, far = pl.pallas_call(
        rim_kernel,
        out_shape=(edge_shape, edge_shape),
        in_specs=[vmem, vmem],
        out_specs=(vmem, vmem),
        compiler_params=params,
    )(hops, incoming)
    bands = NLAT // BAND
    total = bands * SECTORS

    def device_of(block):
        return ORDER[block % SECTORS] * bands + block // SECTORS

    def swap(value, first_block):
        pairs = [(device_of(i), device_of(i + 1)) for i in range(first_block, total - 1, 2)]
        return lax.ppermute(value, ("lon", "lat"), pairs + [(j, i) for i, j in pairs])

    swapped = swap(near, 0)
    swapped_far = swap(far, 1)
    first, forward, backward, last, twist_cos, twist_sin, sine_sq = [jnp.asarray(v) for v in filter_tables()]
    latitudes = jnp.asarray(latitude_table())
    listed = filter_rows.reshape(4, LANES)
    out_shape = jax.ShapeDtypeStruct((SECTORS * COMP * TILES * ROWS, LANES), f32)
    constants = (first, forward, backward, last, twist_cos, twist_sin, sine_sq)
    partial, kept = pl.pallas_call(
        interior_kernel,
        out_shape=(out_shape, jax.ShapeDtypeStruct((COMP, OUTER, LANES), f32)),
        in_specs=[vmem] * 14,
        out_specs=(vmem, vmem),
        scratch_shapes=[
            pltpu.VMEM((COMP, ROWS, OUTER, LANES), f32),
            pltpu.VMEM((COMP, len(INNER) + 1, OUTER, LANES), f32),
        ],
        compiler_params=params,
        cost_estimate=pl.CostEstimate(flops=5_000_000_000, bytes_accessed=8_000_000, transcendentals=0),
    )(hops, latitudes, listed, incoming, near, far, swapped, *constants)
    returning = pl.pallas_call(
        edge_kernel,
        out_shape=out_shape,
        in_specs=[vmem] * 13,
        out_specs=vmem,
        input_output_aliases={12: 0},
        scratch_shapes=[pltpu.VMEM((COMP, 1, OUTER, LANES), f32)],
        compiler_params=params,
        cost_estimate=pl.CostEstimate(flops=1_000_000_000, bytes_accessed=4_000_000, transcendentals=0),
    )(latitudes, listed, kept, far, swapped_far, *constants, partial)
    arrived = lax.all_to_all(
        returning.reshape(SECTORS, COMP * TILES * ROWS, LANES), "lon", 0, 0, tiled=True, axis_index_groups=[list(ORDER)]
    )
    anywhere = pl.BlockSpec(memory_space=pl.ANY)
    result = pl.pallas_call(
        unpack_kernel,
        out_shape=jax.ShapeDtypeStruct((COMP, SECTORS, TILES * ROWS, LANES), f32),
        in_specs=[anywhere],
        out_specs=anywhere,
        scratch_shapes=[pltpu.SemaphoreType.DMA((COMP,))],
        compiler_params=params,
    )(arrived)
    result = result.reshape(COMP, SECTORS, TILES, ROWS, LANES).transpose(0, 1, 3, 2, 4)
    return result.reshape(COMP, 1, BAND, TILES * LANES)


def solution(mesh):
    in_specs = (
        P(None, None, "lat", "lon"),
        P(None, "lat", "lon"),
        P(None, "lat", "lon"),
        P("lat"),
        P(),
    )
    out_specs = P(None, None, "lat", "lon")
    return jax.shard_map(
        on_device, mesh=mesh, in_specs=in_specs, out_specs=out_specs, check_vma=False
    )
```

```python
import functools
import math

import jax
import jax.numpy as jnp
import ml_dtypes
import numpy as np
from jax import lax
from jax.experimental import pallas as pl
from jax.experimental.pallas import tpu as pltpu
from jax.sharding import PartitionSpec as P

NLON = 12288
NLAT = 2048
SECTORS = 16
BAND = 128
ROWS = 8
TILES = 6
LANES = 128
OUTER = SECTORS * TILES
COMP = 3
ARRAYS = COMP + 2
HALF = OUTER // 2 + 1
HALF_PAD = 56
START_Y, STEP_Y, START_X = 2, 1, 1
FIRST_CORE = (1, 1)
ORDER = tuple(
    4 * ((START_Y + STEP_Y * (step if side == 0 else 3 - step)) % 4) + 2 * (START_X ^ side) + (FIRST_CORE[side] ^ core)
    for side in (0, 1)
    for step in range(4)
    for core in (0, 1)
)
INNER = (1, 2, 3, 4, 5, 6)
VMEM_LIMIT = 48 * 1024 * 1024

cos_cutoff = 0.7071067811865476


def split_bf16(table):
    high = table.astype(np.float32).astype(ml_dtypes.bfloat16)
    low = (table - high.astype(np.float64)).astype(np.float32).astype(ml_dtypes.bfloat16)
    return high, low


def filter_tables():
    at = np.arange(OUTER)
    a = TILES * np.asarray(ORDER)[at % SECTORS] + at // SECTORS
    c = np.arange(HALF_PAD)
    valid = (c < HALF)[:, None]
    angle = 2.0 * np.pi * ((c[:, None] * a[None, :]) % OUTER) / OUTER
    first = np.concatenate([np.where(valid, np.cos(angle), 0.0), np.where(valid, -np.sin(angle), 0.0)], axis=0)
    weight = np.where((c == 0) | (c == OUTER // 2), 1.0, 2.0) / NLON
    inner_only = (c > 0) & (c < OUTER // 2)
    last = np.concatenate(
        [
            np.where(valid, np.cos(angle) * weight[:, None], 0.0),
            np.where(valid & inner_only[:, None], -np.sin(angle) * weight[:, None], 0.0),
        ],
        axis=0,
    ).T
    b = np.arange(LANES)
    twist = 2.0 * np.pi * (c[:, None] * b[None, :]) / NLON
    inner = 2.0 * np.pi * ((b[:, None] * b[None, :]) % LANES) / LANES
    cos_in, sin_in = np.cos(inner), np.sin(inner)
    forward = np.block([[cos_in, -sin_in], [sin_in, cos_in]])
    backward = np.block([[cos_in, sin_in], [-sin_in, cos_in]])
    sine = np.sin(np.pi * (c[:, None] + OUTER * b[None, :]) / NLON)
    first_h, first_l = split_bf16(first)
    last_h, last_l = split_bf16(last)
    forward_h, forward_l = split_bf16(forward)
    backward_h, backward_l = split_bf16(backward)
    return (
        np.concatenate([first_h, first_h, first_l], axis=1),
        np.concatenate([forward_h, forward_l], axis=0),
        np.concatenate([backward_h, backward_l], axis=0),
        np.concatenate([last_h, last_h, last_l], axis=1),
        np.cos(twist).astype(np.float32),
        np.sin(twist).astype(np.float32),
        (sine * sine).astype(np.float32),
    )


NORTH, SOUTH, RATIO = range(3)


def latitude_table():
    row = np.arange(NLAT, dtype=np.float32)
    step = np.float32(math.pi / NLAT)
    center = np.sin(((row + np.float32(0.5)) * step).astype(np.float64))
    north = np.sin(((row + np.float32(1.0)) * step).astype(np.float64))
    north[-1] = 0.0
    south = np.concatenate([np.zeros(1), north[:-1]])
    ratio = center / cos_cutoff
    kinds = [v.reshape(NLAT // ROWS, ROWS) for v in (north / center, south / center, ratio * ratio)]
    return np.pad(np.concatenate(kinds, axis=1), ((0, 0), (0, LANES - 3 * ROWS))).astype(np.float32)


def latitude_line(table_ref):
    block = lax.axis_index("lat") * SECTORS + place_of(lax.axis_index("lon"))
    return table_ref[pl.ds(block, 1), :]


def spread(line, lane, rows=SECTORS):
    return jnp.broadcast_to(line[:, lane : lane + 1], (rows, LANES))


def own_hops(hop_ref):
    start = place_of(lax.axis_index("lon")) * ROWS
    line = pltpu.roll(jnp.broadcast_to(hop_ref[...], (8, LANES)), lax.rem(LANES - start, LANES), 1)[:1]
    return [spread(line, r) for r in range(ROWS)]


def halves(value):
    high = value.astype(jnp.bfloat16)
    low = (value - high.astype(jnp.float32)).astype(jnp.bfloat16)
    return high, low


def place_of(sector):
    step = 2 * lax.bitwise_and(STEP_Y * (lax.shift_right_logical(sector, 2) - START_Y), 3)
    core = lax.bitwise_and(sector, 1)
    first_side = lax.bitwise_and(sector, 2) == 2 * START_X
    return jnp.where(
        first_side, step + lax.bitwise_xor(core, FIRST_CORE[0]), 14 - step + lax.bitwise_xor(core, FIRST_CORE[1])
    )


def sector_at(place):
    at, core = lax.shift_right_logical(lax.bitwise_and(place, 7), 1), lax.bitwise_and(place, 1)
    y = lax.bitwise_and(START_Y + STEP_Y * jnp.where(place < 8, at, 3 - at), 3)
    return 4 * y + jnp.where(
        place < 8,
        2 * START_X + lax.bitwise_xor(core, FIRST_CORE[0]),
        2 - 2 * START_X + lax.bitwise_xor(core, FIRST_CORE[1]),
    )


def first_row():
    return lax.axis_index("lat") * BAND + place_of(lax.axis_index("lon")) * ROWS


def from_sector(tile, source):
    low, high = tile[:8], tile[8:]
    parts = []
    for at in (slice(0, 8), slice(8, 16)):
        index = lax.bitwise_and(source[at], 7)
        parts.append(
            jnp.where(
                source[at] < 8,
                jnp.take_along_axis(low, index, axis=0, mode="promise_in_bounds"),
                jnp.take_along_axis(high, index, axis=0, mode="promise_in_bounds"),
            )
        )
    return jnp.concatenate(parts, axis=0)


def fetch(in_ref, array, t, r):
    return in_ref[pl.ds((array * TILES + t) * ROWS + r, SECTORS, stride=ARRAYS * TILES * ROWS), :]


def zonal_row(in_ref, hop, r, store):
    lane = lax.broadcasted_iota(jnp.int32, (SECTORS, LANES), 1)
    own_sector = sector_at(lax.broadcasted_iota(jnp.int32, (SECTORS, LANES), 0))

    def source(hops):
        return place_of(lax.bitwise_and(own_sector - hops + SECTORS, SECTORS - 1))

    sources, sources_before, sources_after = source(hop), source(hop + 1), source(hop - 1)
    weights = []
    for t in range(TILES):
        offset = 1.0 - fetch(in_ref, COMP, t, r)
        w_far = -offset * (offset - 1.0) * (offset - 2.0) * (1.0 / 6.0)
        w_near = (offset + 1.0) * (offset - 1.0) * (offset - 2.0) * 0.5
        w_next = -(offset + 1.0) * offset * (offset - 2.0) * 0.5
        w_last = (offset + 1.0) * offset * (offset - 1.0) * (1.0 / 6.0)
        weights.append((w_far, w_near, w_next, w_last))
    for c in range(COMP):
        raw = [fetch(in_ref, c, t, r) for t in range(TILES)]
        here = [from_sector(v, sources) for v in raw]
        before = from_sector(raw[TILES - 1], sources_before)
        after = from_sector(raw[0], sources_after)
        back_one = [pltpu.roll(v, 1, 1) for v in [before] + here]
        back_two = [pltpu.roll(v, 2, 1) for v in [before] + here]
        ahead = [pltpu.roll(v, LANES - 1, 1) for v in here + [after]]
        for t in range(TILES):
            w_far, w_near, w_next, w_last = weights[t]
            store(
                c,
                slice(t * SECTORS, (t + 1) * SECTORS),
                w_far * jnp.where(lane < 2, back_two[t], back_two[t + 1])
                + w_near * jnp.where(lane < 1, back_one[t], back_one[t + 1])
                + w_next * here[t]
                + w_last * jnp.where(lane == LANES - 1, ahead[t + 1], ahead[t]),
            )


def rim_kernel(hop_ref, in_ref, near_ref, far_ref):
    hops = own_hops(hop_ref)
    odd = lax.bitwise_and(place_of(lax.axis_index("lon")), 1) == 1
    for at_end, out_ref in ((odd, far_ref), (jnp.logical_not(odd), near_ref)):
        r = jnp.where(at_end, ROWS - 1, 0)

        def store(c, at, value):
            out_ref[c, at, :] = value

        zonal_row(in_ref, jnp.where(at_end, hops[ROWS - 1], hops[0]), r, store)
        for t in range(TILES):
            out_ref[COMP, t * SECTORS : (t + 1) * SECTORS, :] = fetch(in_ref, COMP + 1, t, r)


def dot(left, right):
    return jnp.dot(left, right, preferred_element_type=jnp.float32)


def data_by_table(high, low, table):
    rows, depth = high.shape
    both = dot(jnp.concatenate([high, low], axis=0), table[:depth])
    return both[:rows] + both[rows:] + dot(high, table[depth:])


def table_by_data(table, high, low):
    depth = 2 * high.shape[0]
    return dot(table[:, :depth], jnp.concatenate([high, low], axis=0)) + dot(table[:, depth:], high)


def filter_group(slabs, damping, tables):
    first, forward, backward, last, twist_cos, twist_sin = tables
    count = len(slabs)
    spectrum = table_by_data(first, *halves(jnp.concatenate(slabs, axis=1)))
    parts = []
    for k in range(count):
        real = spectrum[:HALF_PAD, k * LANES : (k + 1) * LANES]
        imag = spectrum[HALF_PAD:, k * LANES : (k + 1) * LANES]
        parts.append(
            jnp.concatenate([real * twist_cos + imag * twist_sin, imag * twist_cos - real * twist_sin], axis=1)
        )
    spectrum = data_by_table(*halves(jnp.concatenate(parts, axis=0)), forward)
    parts = []
    for k in range(count):
        rows = spectrum[k * HALF_PAD : (k + 1) * HALF_PAD]
        parts.append(rows * jnp.concatenate([damping[k], damping[k]], axis=1))
    spectrum = data_by_table(*halves(jnp.concatenate(parts, axis=0)), backward)
    parts = []
    for k in range(count):
        real = spectrum[k * HALF_PAD : (k + 1) * HALF_PAD, :LANES]
        imag = spectrum[k * HALF_PAD : (k + 1) * HALF_PAD, LANES:]
        parts.append(
            jnp.concatenate([real * twist_cos - imag * twist_sin, imag * twist_cos + real * twist_sin], axis=0)
        )
    rebuilt = table_by_data(last, *halves(jnp.concatenate(parts, axis=1)))
    return [rebuilt[:, k * LANES : (k + 1) * LANES] for k in range(count)]


def listed_mask(listed_ref, row):
    hit = jnp.where(listed_ref[...] == row, 1.0, 0.0)
    hit = jnp.max(jnp.max(hit, axis=1, keepdims=True), axis=0, keepdims=True)
    return jnp.broadcast_to(hit, (SECTORS, LANES)) > 0.5


def filter_rows_into(out_ref, rows, ratios, merid_ref, listed_ref, sine_sq, tables):
    start = first_row()
    damping = []
    for ratio_sq in ratios:
        damping.extend([ratio_sq / jnp.maximum(ratio_sq, sine_sq)] * COMP)
    slabs = [merid_ref[c, i] for i in range(len(rows)) for c in range(COMP)]
    filtered = filter_group(slabs, damping, tables)
    for i, row in enumerate(rows):
        listed = listed_mask(listed_ref, start + row)
        for c in range(COMP):
            value = filtered[i * COMP + c]
            for t in range(TILES):
                block = slice(t * SECTORS, (t + 1) * SECTORS)
                out_ref[pl.ds((c * TILES + t) * ROWS + row, SECTORS, stride=COMP * TILES * ROWS), :] = jnp.where(
                    listed, value[block], merid_ref[c, i, block, :]
                )


def through_face(courant, own, above):
    return jnp.maximum(courant, 0.0) * own + jnp.minimum(courant, 0.0) * above


def outer_rows(line):
    odd = lax.bitwise_and(place_of(lax.axis_index("lon")), 1) == 1
    first, last = spread(line, RATIO * ROWS, HALF_PAD), spread(line, RATIO * ROWS + ROWS - 1, HALF_PAD)
    near, far = jnp.where(odd, 0, ROWS - 1), jnp.where(odd, ROWS - 1, 0)
    return near, far, jnp.where(odd, first, last), jnp.where(odd, last, first)


def interior_kernel(
    hop_ref, table_ref, listed_ref, in_ref, near_ref, far_ref, swap_ref, first_ref, forward_ref, backward_ref, last_ref,
    twist_cos_ref, twist_sin_ref, sine_ref, out_ref, kept_ref, zonal_ref, merid_ref,
):
    line = latitude_line(table_ref)
    hops = own_hops(hop_ref)
    odd = lax.bitwise_and(place_of(lax.axis_index("lon")), 1) == 1
    tables = (first_ref[...], forward_ref[...], backward_ref[...], last_ref[...], twist_cos_ref[...], twist_sin_ref[...])
    for r in INNER:

        def store(c, at, value):
            zonal_ref[c, r, at, :] = value

        zonal_row(in_ref, hops[r], r, store)
    north = [spread(line, NORTH * ROWS + r) for r in range(ROWS)]
    south = [spread(line, SOUTH * ROWS + r) for r in range(ROWS)]
    outside = jnp.where(odd, south[0], -north[ROWS - 1])
    for t in range(TILES):
        at = slice(t * SECTORS, (t + 1) * SECTORS)
        nearest = [near_ref[c, at, :] for c in range(COMP + 1)]
        farthest = [far_ref[c, at, :] for c in range(COMP)]
        own = [jnp.where(odd, n, f) for n, f in zip(nearest, farthest)]
        last_row_of = [jnp.where(odd, f, n) for n, f in zip(nearest, farthest)]
        before = None
        kept = []
        for r in range(ROWS - 1):
            courant = fetch(in_ref, COMP + 1, t, r)
            above = last_row_of if r == ROWS - 2 else [zonal_ref[c, r + 1, at, :] for c in range(COMP)]
            face = [through_face(courant, own[c], above[c]) for c in range(COMP)]
            for c in range(COMP):
                merid = own[c] - north[r] * face[c]
                if r == 0:
                    kept.append(merid)
                else:
                    merid_ref[c, r - 1, at, :] = merid + south[r] * before[c]
            own, before = above, face
        courant = jnp.where(odd, swap_ref[COMP, at, :], nearest[COMP])
        for c in range(COMP):
            last = last_row_of[c] + south[ROWS - 1] * before[c]
            other = swap_ref[c, at, :]
            face = through_face(courant, jnp.where(odd, other, nearest[c]), jnp.where(odd, nearest[c], other))
            merid_ref[c, len(INNER), at, :] = jnp.where(odd, kept[c], last) + outside * face
            kept_ref[c, at, :] = jnp.where(odd, last, kept[c])
    near, _, ratio, _ = outer_rows(line)
    ratios = [spread(line, RATIO * ROWS + r, HALF_PAD) for r in INNER] + [ratio]
    filter_rows_into(out_ref, INNER + (near,), ratios, merid_ref, listed_ref, sine_ref[...], tables)


def edge_kernel(
    table_ref, listed_ref, kept_ref, far_ref, swap_ref, first_ref, forward_ref, backward_ref, last_ref,
    twist_cos_ref, twist_sin_ref, sine_ref, partial_ref, out_ref, merid_ref,
):
    del partial_ref
    line = latitude_line(table_ref)
    odd = lax.bitwise_and(place_of(lax.axis_index("lon")), 1) == 1
    tables = (first_ref[...], forward_ref[...], backward_ref[...], last_ref[...], twist_cos_ref[...], twist_sin_ref[...])
    outside = jnp.where(odd, -spread(line, NORTH * ROWS + ROWS - 1), spread(line, SOUTH * ROWS))
    for t in range(TILES):
        at = slice(t * SECTORS, (t + 1) * SECTORS)
        courant = jnp.where(odd, far_ref[COMP, at, :], swap_ref[COMP, at, :])
        for c in range(COMP):
            own, other = far_ref[c, at, :], swap_ref[c, at, :]
            face = through_face(courant, jnp.where(odd, own, other), jnp.where(odd, other, own))
            merid_ref[c, 0, at, :] = kept_ref[c, at, :] + outside * face
    _, far, _, ratio = outer_rows(line)
    filter_rows_into(out_ref, (far,), [ratio], merid_ref, listed_ref, sine_ref[...], tables)


def on_device(fields, zonal_fraction, merid_courant, hop_counts, filter_rows):
    vmem = pl.BlockSpec(memory_space=pltpu.VMEM)
    params = pltpu.CompilerParams(vmem_limit_bytes=VMEM_LIMIT)
    hops = hop_counts.reshape(1, BAND)
    parts = []
    for value in (fields, zonal_fraction, merid_courant):
        value = value.reshape(-1, SECTORS, ROWS, TILES, LANES).transpose(1, 0, 3, 2, 4)
        parts.append(value.reshape(SECTORS, -1, LANES))
    outgoing = jnp.concatenate(parts, axis=1)
    incoming = lax.all_to_all(outgoing, "lon", 0, 0, tiled=True, axis_index_groups=[list(ORDER)])
    incoming = incoming.reshape(SECTORS * ARRAYS * TILES * ROWS, LANES)
    f32 = jnp.float32
    edge_shape = jax.ShapeDtypeStruct((COMP + 1, OUTER, LANES), f32)
    near, far = pl.pallas_call(
        rim_kernel,
        out_shape=(edge_shape, edge_shape),
        in_specs=[vmem, vmem],
        out_specs=(vmem, vmem),
        compiler_params=params,
    )(hops, incoming)
    bands = NLAT // BAND
    total = bands * SECTORS

    def device_of(block):
        return ORDER[block % SECTORS] * bands + block // SECTORS

    def swap(value, first_block):
        pairs = [(device_of(i), device_of(i + 1)) for i in range(first_block, total - 1, 2)]
        return lax.ppermute(value, ("lon", "lat"), pairs + [(j, i) for i, j in pairs])

    swapped = swap(near, 0)
    swapped_far = swap(far, 1)
    first, forward, backward, last, twist_cos, twist_sin, sine_sq = [jnp.asarray(v) for v in filter_tables()]
    latitudes = jnp.asarray(latitude_table())
    listed = filter_rows.reshape(4, LANES)
    out_shape = jax.ShapeDtypeStruct((SECTORS * COMP * TILES * ROWS, LANES), f32)
    constants = (first, forward, backward, last, twist_cos, twist_sin, sine_sq)
    partial, kept = pl.pallas_call(
        interior_kernel,
        out_shape=(out_shape, jax.ShapeDtypeStruct((COMP, OUTER, LANES), f32)),
        in_specs=[vmem] * 14,
        out_specs=(vmem, vmem),
        scratch_shapes=[
            pltpu.VMEM((COMP, ROWS, OUTER, LANES), f32),
            pltpu.VMEM((COMP, len(INNER) + 1, OUTER, LANES), f32),
        ],
        compiler_params=params,
        cost_estimate=pl.CostEstimate(flops=5_000_000_000, bytes_accessed=8_000_000, transcendentals=0),
    )(hops, latitudes, listed, incoming, near, far, swapped, *constants)
    returning = pl.pallas_call(
        edge_kernel,
        out_shape=out_shape,
        in_specs=[vmem] * 13,
        out_specs=vmem,
        input_output_aliases={12: 0},
        scratch_shapes=[pltpu.VMEM((COMP, 1, OUTER, LANES), f32)],
        compiler_params=params,
        cost_estimate=pl.CostEstimate(flops=1_000_000_000, bytes_accessed=4_000_000, transcendentals=0),
    )(latitudes, listed, kept, far, swapped_far, *constants, partial)
    arrived = lax.all_to_all(
        returning.reshape(SECTORS, COMP * TILES * ROWS, LANES), "lon", 0, 0, tiled=True, axis_index_groups=[list(ORDER)]
    )
    arrived = arrived.reshape(SECTORS, COMP, TILES, ROWS, LANES).transpose(1, 0, 3, 2, 4)
    return arrived.reshape(COMP, 1, BAND, TILES * LANES)


def solution(mesh):
    in_specs = (
        P(None, None, "lat", "lon"),
        P(None, "lat", "lon"),
        P(None, "lat", "lon"),
        P("lat"),
        P(),
    )
    out_specs = P(None, None, "lat", "lon")
    return jax.shard_map(
        on_device, mesh=mesh, in_specs=in_specs, out_specs=out_specs, check_vma=False
    )
```
